256 devices in a mesh: pair: 64 (over z, x, core), col: 4 (over y).
Axes of the slice: x: 4, y: 4, z: 8, core: 2. Of those that a mesh axis runs over, the one named last changes fastest.
Arguments:
- left_tiles: bfloat16 [768, 64, 4096], P('pair'), may hold values from -0.078125 to 0.078125
- left_row: int32 [768], P('pair'), may hold values from 0 to 8
- left_lam: int32 [768], P('pair'), may hold values from 0 to 7
- left_count: int32 [64], P('pair'), may hold values from 1 to 12, as said below
- density: bfloat16 [36864, 256], P('pair', 'col'), may hold values from -6 to 6
- metric: float32 [64, 64], replicated, as said below
- back_tiles: bfloat16 [36864, 16384], P('pair', 'col'), may hold values from -0.046875 to 0.046875
- back_pattern: int32 [576, 4], P('pair', 'col'), may hold values 0 or 1
Outputs:
- exchange_block: float32 [512, 36864], P('col', 'pair')
The draws below stay inside these ranges and needn't reach their ends.
Inputs may be any that keep to these rules, and one draw needn't show every extreme that they name: `left_count`: slots at or past a device's count are unused; some index of pair has all 12 slots live. `metric`: symmetric.
All inputs are finite; a program needn't handle non-finite values. No bound on the sum of `back_pattern` on one device may be relied on, other than what follows from the above.
Results may differ from the reference program's by a relative error of at most 0.0029.
Values may be sent and summed in bfloat16 or wider, within the bound.
A program may use at most 128 MiB of HBM per device.

```python
import math
import jax
import jax.numpy as jnp
from jax import lax

BLK = 64
AUX = 64
NBLK = 576
LW = 8
TL_CAP = 12
BASIS = 36864
MB_DEV = 9
TILES = 768
SIGMA = 256
N_PAIR = 64
N_COL = 4


def draw_left_count(key, part):
    first_key, second_key = jax.random.split(jax.random.fold_in(key, 7))
    lowest = max(1, TL_CAP // 4)
    counts = jax.random.randint(first_key, (N_PAIR,), lowest, TL_CAP + 1)
    filled = jax.random.randint(second_key, (), 0, N_PAIR)
    return jnp.where(jnp.arange(N_PAIR) == filled, TL_CAP, counts).astype(jnp.int32)


def draw_metric(key, part):
    first_key, second_key = jax.random.split(jax.random.fold_in(key, 11), 2)
    diagonal = jnp.exp(jax.random.uniform(first_key, (AUX,), jnp.float32, math.log(0.5), math.log(2.0)))
    random_part = jax.random.normal(second_key, (AUX, AUX), jnp.float32)
    symmetric = (random_part + random_part.T) * (0.5 / math.sqrt(AUX))
    return (jnp.diag(diagonal) + symmetric).astype(jnp.float32)


def with_ends(values, rng, smallest, top_value):
    longest = values.shape.index(max(values.shape))
    spots = []
    for shift in (0, 1):
        where = [jax.random.randint(jax.random.fold_in(rng, axis), (), 0, length) for axis, length in enumerate(values.shape)]
        where[longest] = (where[longest] + shift) % values.shape[longest]
        spots.append(tuple(where))
    return values.at[spots[0]].set(smallest).at[spots[1]].set(top_value)


def shard_levels(key, extent, shards, least, high):
    def one(dim, shards_of):
        draws = jax.random.uniform(jax.random.fold_in(jax.random.fold_in(key, 6), dim), (shards_of,), jnp.float32, least / len(shards), high / len(shards))
        return jnp.repeat(jnp.exp(draws), extent[dim] // shards_of).reshape((-1,) + (1,) * (len(extent) - dim - 1))

    level = one(*shards[0])
    for cut in shards[1:]:
        level = level * one(*cut)
    return level


def gaussian(key, extent, deviation, bound, pieces=(), held_as=jnp.bfloat16):
    drawn = deviation * jax.random.normal(key, extent, jnp.float32)
    if pieces:
        drawn = drawn * shard_levels(key, extent, pieces, -0.22, 0.18)
    return jnp.clip(drawn, -bound, bound).astype(held_as)


def setup_inputs(seed: int = 0) -> dict:
    splits = jax.random.split(jax.random.key(seed), 9)
    left_tiles = gaussian(splits[0], (TILES, BLK, BLK * AUX), (BLK * N_PAIR * TL_CAP // LW) ** -0.5, 0.078125, ((0, 64),))
    left_row = with_ends(jax.random.randint(splits[1], (TILES,), 0, MB_DEV), jax.random.fold_in(splits[1], 1), 0, MB_DEV - 1).astype(jnp.int32)
    left_lam = with_ends(jax.random.randint(splits[2], (TILES,), 0, LW), jax.random.fold_in(splits[2], 1), 0, LW - 1).astype(jnp.int32)
    left_count = draw_left_count(jax.random.fold_in(splits[8], 71), 0)
    density = gaussian(splits[4], (BASIS, SIGMA), 1.0, 6.0, ((0, 64), (1, 4)))
    metric = draw_metric(jax.random.fold_in(splits[8], 71), 0)
    back_tiles = gaussian(splits[6], (BASIS, SIGMA * AUX), (BLK * AUX * N_COL) ** -0.5, 0.046875, ((0, 64), (1, 4)))
    back_pattern = with_ends((jax.random.randint(splits[7], (NBLK, N_COL), 0, 4) < 3).astype(jnp.int32), jax.random.fold_in(splits[7], 1), 0, 1)
    return {"left_tiles": left_tiles, "left_row": left_row, "left_lam": left_lam, "left_count": left_count, "density": density, "metric": metric, "back_tiles": back_tiles, "back_pattern": back_pattern}


def reference(left_tiles, left_row, left_lam, left_count, density, metric, back_tiles, back_pattern):
    slot_ids = jnp.arange(TILES, dtype=jnp.int32)
    owners = (slot_ids // TL_CAP).astype(jnp.int32)
    alive_slots = ((slot_ids % TL_CAP) < left_count[owners]).astype(jnp.float32)
    mu_blocks = (owners * MB_DEV + left_row).astype(jnp.int32)
    initial = jnp.zeros((LW * BLK, SIGMA * AUX), jnp.float32)

    def add_tile(running, inputs):
        tile_block, mu_block, lam_block, weight = inputs
        dens_rows = lax.dynamic_slice_in_dim(density, (mu_block * BLK).astype(jnp.int32), BLK, 0)
        contrib = jnp.einsum("mlp,ms->lsp", tile_block.reshape(BLK, BLK, AUX).astype(jnp.float32), dens_rows.astype(jnp.float32))
        contrib = contrib.reshape(BLK, SIGMA * AUX) * weight
        target = (lam_block * BLK).astype(jnp.int32)
        current = lax.dynamic_slice_in_dim(running, target, BLK, 0)
        return lax.dynamic_update_slice_in_dim(running, current + contrib, target, 0), weight

    summed, unused = lax.scan(add_tile, initial, (left_tiles, mu_blocks, left_lam, alive_slots))
    applied = jnp.dot(summed.reshape(-1, AUX), metric, precision=lax.Precision.HIGHEST, preferred_element_type=jnp.float32)
    applied = applied.reshape(LW * BLK, SIGMA * AUX).astype(jnp.bfloat16)
    exchange = jnp.zeros((LW * BLK, BASIS), jnp.float32)
    for column in range(N_COL):
        first_col = column * BLK * AUX
        mixed_block = applied[:, first_col:first_col + BLK * AUX]
        back_block = back_tiles[:, first_col:first_col + BLK * AUX]
        pattern_cols = jnp.repeat(back_pattern[:, column], BLK).astype(jnp.float32)
        exchange = exchange + jnp.dot(mixed_block, back_block.T, preferred_element_type=jnp.float32) * pattern_cols[None, :]
    return exchange
```

```python
import jax
import jax.numpy as jnp
from jax import lax
from jax.experimental import pallas as pl
from jax.experimental.pallas import tpu as pltpu
from jax.sharding import PartitionSpec as P

MESH = pl.DeviceIdType.MESH
F32, BF16, I16, I32 = jnp.float32, jnp.bfloat16, jnp.int16, jnp.int32

NZ, NX, NY = 8, 4, 4
SLOTS = 12
Z_ORDER = (4, 3, 5, 2, 6, 1, 7, 0)
X_ORDER = (2, 1, 3, 0)
TOP = 32000.0
ROUND = 12582912.0
POOL = 1036
N_MSG = 4 + 4 + 8 + 8 + 4
N_GATHER = 64


def kernel(
    row_s, lam_s, count_s, pattern_s, density, metric, left_hbm, back_hbm, out_ref,
    left_v, back_v, pick, amat, stage, acc, pool_s, pool_r, applied, y_send, y_recv,
    metric2, turn, msg_send, msg_recv, ag_send, ag_recv, y_ssem, y_rsem, local_sem,
):
    pair = lax.axis_index("pair")
    y = lax.axis_index("col")
    core = lax.rem(pair, 2)
    x = lax.rem(lax.div(pair, 2), NX)
    z = lax.div(pair, 2 * NX)

    def at(zz, xx, cc):
        return {"pair": (lax.rem(zz, NZ) * NX + lax.rem(xx, NX)) * 2 + cc}

    peer = at(z, x, 1 - core)
    x_right, x_left = at(z, x + 1, core), at(z, x + NX - 1, core)
    z_right, z_left = at(z + 1, x, core), at(z + NZ - 1, x, core)
    y_peers = [{"col": lax.rem(y + dy, NY)} for dy in (1, 2, 3)]

    barrier = pltpu.get_barrier_semaphore()
    for other in [peer, x_right, x_left, z_right, z_left] + y_peers:
        pl.semaphore_signal(barrier, inc=1, device_id=other, device_id_type=MESH)

    loads = []
    for i, off in enumerate(X_ORDER):
        first = pl.multiple_of(lax.rem(x + off, NX) * 1024, 1024)
        load = pltpu.make_async_copy(left_hbm.at[:, pl.ds(first, 1024)], left_v.at[i], local_sem.at[i])
        load.start()
        loads.append(load)
    back_load = pltpu.make_async_copy(back_hbm, back_v, local_sem.at[4])
    back_load.start()

    j = lax.broadcasted_iota(I32, (64, 64), 0)
    half_core = jnp.where(j < 32, 1 - core, core)
    sigma = half_core * 32 + 2 * (j & 15) + ((j >> 4) & 1)
    perm = jnp.where(lax.broadcasted_iota(I32, (64, 64), 1) == sigma, 1.0, 0.0).astype(BF16)
    sorted_density = jnp.dot(perm, density[...], preferred_element_type=F32).astype(BF16)
    lane = lax.broadcasted_iota(I32, (16, SLOTS * 64), 1)
    slot_of = lane >> 6
    lam_of = jnp.zeros((16, SLOTS * 64), I32)
    row_of = jnp.zeros((16, SLOTS * 64), I32)
    for s in range(SLOTS):
        lam_of = jnp.where(slot_of == s, lam_s[s], lam_of)
        row_of = jnp.where(slot_of == s, row_s[s], row_of)
    live = slot_of < count_s[0]
    source = row_of * 64 + (lane & 63)
    deep = lax.broadcasted_iota(I32, (16, SLOTS * 64), 0)
    for b in range(36):
        pick[b * 16:(b + 1) * 16, :] = jnp.where(source == deep + b * 16, 1.0, 0.0).astype(BF16)
    turned = jnp.dot(sorted_density, pick[...], preferred_element_type=F32)
    for r, off in enumerate(Z_ORDER):
        here = live & (lam_of == lax.rem(z + off, NZ))
        for q in range(4):
            first = (q * 8 + r) * 16
            amat[first:first + 16, :] = jnp.where(here, turned[q * 16:(q + 1) * 16, :], 0.0).astype(BF16)

    metric2[...] = jnp.zeros((128, 128), F32)
    metric2[0:64, 0:64] = metric[...]
    metric2[64:128, 64:128] = metric[...]

    pl.semaphore_wait(barrier, 8)

    copies = []
    counter = [0, 0]

    def message(tiles, target):
        off, number = counter
        counter[0] += tiles + 1
        counter[1] += 1
        copy = pltpu.make_async_remote_copy(
            src_ref=pool_s.at[pl.ds(off, tiles + 1)], dst_ref=pool_r.at[pl.ds(off, tiles + 1)],
            send_sem=msg_send.at[number], recv_sem=msg_recv.at[number],
            device_id=target, device_id_type=MESH,
        )
        copies.append(copy)
        return copy, off, tiles

    def send(get, groups, size, msg):
        copy, off, tiles = msg
        assert tiles == groups * size

        def largest(g, m):
            return jnp.maximum(m, jnp.max(jnp.abs(get(g)[...]), axis=0))

        top = lax.fori_loop(0, groups, largest, jnp.zeros((16, 128), F32))
        power = jnp.ceil(jnp.log2(jnp.maximum(top, 1e-30)))
        scale = jnp.exp2(-power) * TOP
        pool_s[off + tiles] = power.astype(I16)

        def code(g, carry):
            value = (get(g)[...] * scale + ROUND) - ROUND
            pool_s[pl.ds(off + g * size, size)] = value.astype(I16)
            return carry

        lax.fori_loop(0, groups, code, 0)
        copy.start()

    def receive(get, groups, size, msg):
        copy, off, tiles = msg
        assert tiles == groups * size
        copy.wait_recv()
        scale = jnp.exp2(pool_r[off + tiles].astype(F32)) * (1.0 / TOP)

        def add(g, carry):
            ref = get(g)
            ref[...] = ref[...] + pool_r[pl.ds(off + g * size, size)].astype(F32) * scale
            return carry

        lax.fori_loop(0, groups, add, 0)

    core_msgs = [message(128, peer) for i in range(4)]

    def left_step(i):
        loads[i].wait()

        def columns(jc, carry):
            tile = left_v[i, :, pl.ds(pl.multiple_of(jc * 256, 256), 256)]
            part = jnp.dot(amat[...], tile, preferred_element_type=F32)
            for u in range(2):
                value = part[:, u * 128:(u + 1) * 128].reshape(32, 16, 128)
                stage[:, 2 * jc + u] = value[0:16]
                acc[i, :, 2 * jc + u] = value[16:32]
            return carry

        lax.fori_loop(0, 4, columns, 0)
        send(lambda g: stage.at[g], 16, 8, core_msgs[i])

    def core_sum(i):
        receive(lambda g: acc.at[i, g], 16, 8, core_msgs[i])

    a1 = [(message(32, x_right), message(32, x_left)), (message(64, x_right), message(64, x_left))]
    b1 = [(message(16, z_right), message(16, z_left))]
    b1 += [(message(32, z_right), message(32, z_left)) for s in range(3)]
    a2 = [(message(4, z_right), message(4, z_left))]
    a2 += [(message(8, z_right), message(8, z_left)) for s in range(3)]
    b2 = [(message(4, x_right), message(4, x_left)), (message(8, x_right), message(8, x_left))]
    assert counter == [POOL, N_MSG]

    def a1_at(slot, first=0):
        return lambda g: acc.at[slot, first + g]

    def b1_at(row, first=0):
        return lambda g: acc.at[first + g, 8 + row]

    def a2_at(row, first=0, size=8):
        return lambda g: acc.at[3, row, pl.ds(first, size)]

    def b2_at(slot, first=0, size=8):
        return lambda g: acc.at[slot, 15, pl.ds(first, size)]

    left_step(0)
    left_step(1)
    core_sum(0)
    send(a1_at(0, 0), 4, 8, a1[0][0])
    send(a1_at(0, 4), 4, 8, a1[0][1])
    left_step(2)
    core_sum(1)
    left_step(3)
    core_sum(2)
    core_sum(3)
    send(b1_at(0, 0), 2, 8, b1[0][0])
    send(b1_at(0, 2), 2, 8, b1[0][1])
    receive(a1_at(1, 0), 4, 8, a1[0][0])
    send(a1_at(1), 8, 8, a1[1][0])
    receive(a1_at(2, 4), 4, 8, a1[0][1])
    send(a1_at(2), 8, 8, a1[1][1])
    receive(b1_at(1, 0), 2, 8, b1[0][0])
    send(b1_at(1), 4, 8, b1[1][0])
    receive(b1_at(2, 2), 2, 8, b1[0][1])
    send(b1_at(2), 4, 8, b1[1][1])
    receive(b1_at(3), 4, 8, b1[1][0])
    send(b1_at(3), 4, 8, b1[2][0])
    receive(b1_at(4), 4, 8, b1[1][1])
    send(b1_at(4), 4, 8, b1[2][1])
    receive(a1_at(3), 8, 8, a1[1][0])
    receive(a1_at(3), 8, 8, a1[1][1])
    send(a2_at(0, 0, 4), 1, 4, a2[0][0])
    send(a2_at(0, 4, 4), 1, 4, a2[0][1])
    receive(b1_at(5), 4, 8, b1[2][0])
    send(b1_at(5), 4, 8, b1[3][0])
    receive(b1_at(6), 4, 8, b1[2][1])
    send(b1_at(6), 4, 8, b1[3][1])
    receive(a2_at(1, 0, 4), 1, 4, a2[0][0])
    send(a2_at(1), 1, 8, a2[1][0])
    receive(a2_at(2, 4, 4), 1, 4, a2[0][1])
    send(a2_at(2), 1, 8, a2[1][1])
    receive(b1_at(7), 4, 8, b1[3][0])
    receive(b1_at(7), 4, 8, b1[3][1])
    send(b2_at(0, 0, 4), 1, 4, b2[0][0])
    send(b2_at(0, 4, 4), 1, 4, b2[0][1])
    receive(a2_at(3), 1, 8, a2[1][0])
    send(a2_at(3), 1, 8, a2[2][0])
    receive(a2_at(4), 1, 8, a2[1][1])
    send(a2_at(4), 1, 8, a2[2][1])
    receive(b2_at(1, 0, 4), 1, 4, b2[0][0])
    send(b2_at(1), 1, 8, b2[1][0])
    receive(b2_at(2, 4, 4), 1, 4, b2[0][1])
    send(b2_at(2), 1, 8, b2[1][1])
    receive(a2_at(5), 1, 8, a2[2][0])
    send(a2_at(5), 1, 8, a2[3][0])
    receive(a2_at(6), 1, 8, a2[2][1])
    send(a2_at(6), 1, 8, a2[3][1])
    receive(b2_at(3), 1, 8, b2[1][0])
    receive(b2_at(3), 1, 8, b2[1][1])
    receive(a2_at(7), 1, 8, a2[3][0])
    receive(a2_at(7), 1, 8, a2[3][1])

    def with_metric(row):
        rows = acc[3, row].reshape(128, 128)
        return jnp.dot(rows, metric2[...], precision=lax.Precision.HIGHEST, preferred_element_type=F32)

    even, odd = with_metric(7), with_metric(15)
    low = lax.broadcasted_iota(I32, (16, 128), 1) < 64
    for t in range(8):
        e, o = even[t * 16:(t + 1) * 16], odd[t * 16:(t + 1) * 16]
        turn[2 * t] = jnp.where(low, e, pltpu.roll(o, 64, 1))
        turn[2 * t + 1] = jnp.where(low, pltpu.roll(e, 64, 1), o)
    my_rows = pl.ds(pl.multiple_of(x * 16, 16), 16)
    core_first = core * 2048
    for sp in range(16):
        cols = pl.ds(pl.multiple_of(core_first + sp * 128, 128), 128)
        applied[z, my_rows, cols] = turn[:, sp, :].astype(BF16)

    used = [0]

    def share(view, target):
        number = used[0]
        used[0] += 1
        copy = pltpu.make_async_remote_copy(
            src_ref=view, dst_ref=view, send_sem=ag_send.at[number], recv_sem=ag_recv.at[number],
            device_id=target, device_id_type=MESH,
        )
        copy.start()
        copies.append(copy)
        return copy

    def cols_of(first, size):
        return pl.ds(pl.multiple_of(core_first + first, 512), size)

    def group_rows(dx):
        return pl.ds(pl.multiple_of(lax.rem(x + dx + NX, NX) * 16, 16), 16)

    def zz(dz):
        return lax.rem(z + dz + NZ, NZ)

    def a1_view(dz, first=0, size=1024):
        return applied.at[zz(dz), my_rows, cols_of(first, size)]

    def b1_view(dx, first=0, size=1024):
        return applied.at[z, group_rows(dx), cols_of(1024 + first, size)]

    def a2_view(dx, first=0, size=1024):
        return applied.at[:, group_rows(dx), cols_of(first, size)]

    def b2_view(dz, first=0, size=1024):
        return applied.at[zz(dz), :, cols_of(1024 + first, size)]

    ga = [(share(a1_view(0), z_right), share(a1_view(0), z_left))]
    gb = [(share(b1_view(0), x_right), share(b1_view(0), x_left))]
    gb[0][0].wait_recv()
    r = share(b1_view(-1, 0, 512), x_right)
    gb[0][1].wait_recv()
    gb.append((r, share(b1_view(1, 512, 512), x_left)))
    for s in (1, 2):
        ga[s - 1][0].wait_recv()
        r = share(a1_view(-s), z_right)
        ga[s - 1][1].wait_recv()
        ga.append((r, share(a1_view(s), z_left)))
        if s == 1:
            gb[1][0].wait_recv()
            gb[1][1].wait_recv()
            hb = [(share(b2_view(0), z_right), share(b2_view(0), z_left))]
            forward = [share(b2_view(0), peer)]
    ga[2][0].wait_recv()
    r = share(a1_view(-3, 0, 512), z_right)
    ga[2][1].wait_recv()
    ga.append((r, share(a1_view(3, 512, 512), z_left)))
    ga[3][0].wait_recv()
    ga[3][1].wait_recv()
    ha = [(share(a2_view(0), x_right), share(a2_view(0), x_left))]
    forward.append(share(a2_view(0), peer))

    def b2_step(s):
        half = s == 3
        hb[s - 1][0].wait_recv()
        r = share(b2_view(-s, 0, 512) if half else b2_view(-s), z_right)
        forward.append(share(b2_view(-s), peer))
        hb[s - 1][1].wait_recv()
        hb.append((r, share(b2_view(s, 512, 512) if half else b2_view(s), z_left)))
        forward.append(share(b2_view(s), peer))

    b2_step(1)
    b2_step(2)
    ha[0][0].wait_recv()
    r = share(a2_view(-1, 0, 512), x_right)
    forward.append(share(a2_view(-1), peer))
    ha[0][1].wait_recv()
    ha.append((r, share(a2_view(1, 512, 512), x_left)))
    forward.append(share(a2_view(1), peer))
    b2_step(3)
    ha[1][0].wait_recv()
    ha[1][1].wait_recv()
    forward.append(share(a2_view(2), peer))
    hb[3][0].wait_recv()
    hb[3][1].wait_recv()
    forward.append(share(b2_view(4), peer))
    for copy in forward:
        copy.wait_recv()

    back_load.wait()
    block_of = lax.shift_right_logical(lax.broadcasted_iota(I32, (1, 576), 1), 6)
    present = jnp.zeros((1, 576), F32)
    for b in range(9):
        present = jnp.where(block_of == b, pattern_s[b].astype(F32), present)

    def product(block):
        rows = applied[pl.ds(block * 2, 2)].reshape(128, 4096)
        return lax.dot_general(rows, back_v[...], (((1,), (1,)), ((), ())), preferred_element_type=F32) * present

    y_copies = []
    for n in (1, 0, 2):
        y_send[n] = product(lax.rem(y + n + 1, NY)).astype(BF16)
        copy = pltpu.make_async_remote_copy(
            src_ref=y_send.at[n], dst_ref=y_recv.at[n], send_sem=y_ssem.at[n], recv_sem=y_rsem.at[n],
            device_id=y_peers[n], device_id_type=MESH,
        )
        copy.start()
        y_copies.append(copy)
    out_ref[...] = product(y)
    for copy in y_copies:
        copy.wait_recv()
    out_ref[...] = out_ref[...] + y_recv[0].astype(F32) + y_recv[1].astype(F32) + y_recv[2].astype(F32)
    for copy in copies + y_copies:
        copy.wait_send()


def per_device(left_tiles, left_row, left_lam, left_count, density, metric, back_tiles, back_pattern):
    vmem = pl.BlockSpec(memory_space=pltpu.VMEM)
    smem = pl.BlockSpec(memory_space=pltpu.SMEM)
    hbm = pl.BlockSpec(memory_space=pl.ANY)
    return pl.pallas_call(
        kernel,
        out_shape=jax.ShapeDtypeStruct((128, 576), F32),
        in_specs=[smem, smem, smem, smem, vmem, vmem, hbm, hbm],
        out_specs=vmem,
        scratch_shapes=[
            pltpu.VMEM((4, 768, 1024), BF16),
            pltpu.VMEM((576, 4096), BF16),
            pltpu.VMEM((576, 768), BF16),
            pltpu.VMEM((512, 768), BF16),
            pltpu.VMEM((16, 8, 16, 128), F32),
            pltpu.VMEM((4, 16, 8, 16, 128), F32),
            pltpu.VMEM((POOL, 16, 128), I16),
            pltpu.VMEM((POOL, 16, 128), I16),
            pltpu.VMEM((8, 64, 4096), BF16),
            pltpu.VMEM((3, 128, 576), BF16),
            pltpu.VMEM((3, 128, 576), BF16),
            pltpu.VMEM((128, 128), F32),
            pltpu.VMEM((16, 16, 128), F32),
            pltpu.SemaphoreType.DMA((N_MSG,)),
            pltpu.SemaphoreType.DMA((N_MSG,)),
            pltpu.SemaphoreType.DMA((N_GATHER,)),
            pltpu.SemaphoreType.DMA((N_GATHER,)),
            pltpu.SemaphoreType.DMA((3,)),
            pltpu.SemaphoreType.DMA((3,)),
            pltpu.SemaphoreType.DMA((5,)),
        ],
        compiler_params=pltpu.CompilerParams(
            collective_id=0, has_side_effects=True, vmem_limit_bytes=56 * 1024 * 1024
        ),
        cost_estimate=pl.CostEstimate(flops=6_000_000_000, bytes_accessed=12_000_000, transcendentals=0),
    )(
        left_row, left_lam, left_count, back_pattern.reshape(9), density.T, metric,
        left_tiles.reshape(768, 4096), back_tiles,
    )


def solution(mesh):
    placed = (
        P("pair", None, None),
        P("pair"),
        P("pair"),
        P("pair"),
        P("pair", "col"),
        P(),
        P("pair", "col"),
        P("pair", "col"),
    )
    return jax.shard_map(
        per_device, mesh=mesh, in_specs=placed, out_specs=P("col", "pair"), check_vma=False
    )
```

```python
import jax
import jax.numpy as jnp
from jax import lax
from jax.experimental import pallas as pl
from jax.experimental.pallas import tpu as pltpu
from jax.sharding import PartitionSpec as P

MESH = pl.DeviceIdType.MESH
F32, BF16, I16, I32 = jnp.float32, jnp.bfloat16, jnp.int16, jnp.int32

NZ, NX, NY = 8, 4, 4
SLOTS = 12
Z_ORDER = (4, 3, 5, 2, 6, 1, 7, 0)
X_ORDER = (2, 1, 3, 0)
TOP = 32000.0
ROUND = 12582912.0
PART_A = 10
COLS_A = 1280
POOL = 1063
N_MSG = 55
N_GATHER = 91


def in_order(tasks):
    now, free, arrival, done, order, left = 0.0, {}, {}, set(), [], list(tasks)
    while left:
        best = None
        for task in left:
            name, needs, after, cost, rank, sends, run = task
            if all(n in arrival for n in needs) and all(t in done for t in after):
                ready = max([arrival[n] for n in needs] + [now])
                if best is None or (ready, rank) < best[:2]:
                    best = (ready, rank, task)
        ready, rank, task = best
        now = ready + task[3]
        for key, link, hops, kib in task[5]:
            now += 0.1
            if link == "core":
                arrival[key] = now + 1.0 + kib * 0.001
                continue
            each = kib * 2 * 1.024 / 115.0
            start = max(free.get(link, 0.0), now)
            free[link] = start + each * hops
            arrival[key] = start + each + 2.0 + 0.4 * (hops - 1)
        order.append(task)
        done.add(task[0])
        left.remove(task)
    return order


def kernel(
    row_s, lam_s, count_s, pattern_s, density, metric, left_hbm, back_hbm, out_ref,
    left_v, back_v, pick, amat, stage, acc, pool_s, pool_r, applied, y_send, y_recv,
    metric2, turn, msg_send, msg_recv, ag_send, ag_recv, y_ssem, y_rsem, local_sem,
):
    pair = lax.axis_index("pair")
    y = lax.axis_index("col")
    core = lax.rem(pair, 2)
    x = lax.rem(lax.div(pair, 2), NX)
    z = lax.div(pair, 2 * NX)

    def at(zz, xx, cc):
        return {"pair": (lax.rem(zz, NZ) * NX + lax.rem(xx, NX)) * 2 + cc}

    peer = at(z, x, 1 - core)
    x_right, x_left = at(z, x + 1, core), at(z, x + NX - 1, core)
    z_right, z_left = at(z + 1, x, core), at(z + NZ - 1, x, core)
    y_peers = [{"col": lax.rem(y + dy, NY)} for dy in (1, 2, 3)]

    barrier = pltpu.get_barrier_semaphore()
    far_peers = [at(z, x + 2, core), at(z + 2, x, core), at(z + NZ - 2, x, core)]
    for other in [peer, x_right, x_left, z_right, z_left] + far_peers + y_peers:
        pl.semaphore_signal(barrier, inc=1, device_id=other, device_id_type=MESH)

    loads = []
    for i, off in enumerate(X_ORDER):
        first = pl.multiple_of(lax.rem(x + off, NX) * 1024, 1024)
        load = pltpu.make_async_copy(left_hbm.at[:, pl.ds(first, 1024)], left_v.at[i], local_sem.at[i])
        load.start()
        loads.append(load)
    back_load = pltpu.make_async_copy(back_hbm, back_v, local_sem.at[4])
    back_load.start()

    j = lax.broadcasted_iota(I32, (64, 64), 0)
    half_core = jnp.where(j < 32, 1 - core, core)
    sigma = half_core * 32 + 2 * (j & 15) + ((j >> 4) & 1)
    perm = jnp.where(lax.broadcasted_iota(I32, (64, 64), 1) == sigma, 1.0, 0.0).astype(BF16)
    sorted_density = jnp.dot(perm, density[...], preferred_element_type=F32).astype(BF16)
    lane = lax.broadcasted_iota(I32, (16, SLOTS * 64), 1)
    slot_of = lane >> 6
    lam_of = jnp.zeros((16, SLOTS * 64), I32)
    row_of = jnp.zeros((16, SLOTS * 64), I32)
    for s in range(SLOTS):
        lam_of = jnp.where(slot_of == s, lam_s[s], lam_of)
        row_of = jnp.where(slot_of == s, row_s[s], row_of)
    live = slot_of < count_s[0]
    source = row_of * 64 + (lane & 63)
    deep = lax.broadcasted_iota(I32, (16, SLOTS * 64), 0)
    for b in range(36):
        pick[b * 16:(b + 1) * 16, :] = jnp.where(source == deep + b * 16, 1.0, 0.0).astype(BF16)
    turned = jnp.dot(sorted_density, pick[...], preferred_element_type=F32)
    for r, off in enumerate(Z_ORDER):
        here = live & (lam_of == lax.rem(z + off, NZ))
        for q in range(4):
            first = (q * 8 + r) * 16
            amat[first:first + 16, :] = jnp.where(here, turned[q * 16:(q + 1) * 16, :], 0.0).astype(BF16)

    metric2[...] = jnp.zeros((128, 128), F32)
    metric2[0:64, 0:64] = metric[...]
    metric2[64:128, 64:128] = metric[...]

    pl.semaphore_wait(barrier, 11)

    links = {
        "core": peer, "x+": x_right, "x-": x_left, "x2": at(z, x + 2, core),
        "z+": z_right, "z-": z_left, "z++": at(z + 2, x, core), "z--": at(z + NZ - 2, x, core),
    }
    lanes = {"x2": ("x+", 2), "z++": ("z+", 2), "z--": ("z-", 2)}
    copies, flights, tasks = [], {}, []
    counter, gathers = [0, 0], [0]

    def task(name, needs, after, cost, rank, sends, run):
        tasks.append((name, needs, after, cost, rank, [(k,) + lanes.get(l, (l, 1)) + (n,) for k, l, n in sends], run))

    def message(key, tiles, link):
        off, number = counter
        counter[0] += tiles + 1
        counter[1] += 1
        copy = pltpu.make_async_remote_copy(
            src_ref=pool_s.at[pl.ds(off, tiles + 1)], dst_ref=pool_r.at[pl.ds(off, tiles + 1)],
            send_sem=msg_send.at[number], recv_sem=msg_recv.at[number],
            device_id=links[link], device_id_type=MESH,
        )
        flights[key] = (copy, off, tiles)
        return (key, link, 4 * (tiles + 1))

    def send(get, groups, size, key):
        copy, off, tiles = flights[key]
        assert tiles == groups * size

        def largest(g, m):
            return jnp.maximum(m, jnp.max(jnp.abs(get(g)[...]), axis=0))

        def code(g, carry):
            value = (get(g)[...] * scale + ROUND) - ROUND
            pool_s[pl.ds(off + g * size, size)] = value.astype(I16)
            return carry

        top = jnp.zeros((16, 128), F32)
        top = largest(0, top) if groups == 1 else lax.fori_loop(0, groups, largest, top)
        power = jnp.ceil(jnp.log2(jnp.maximum(top, 1e-30)))
        scale = jnp.exp2(-power) * TOP
        pool_s[off + tiles] = power.astype(I16)
        if groups == 1:
            code(0, 0)
        else:
            lax.fori_loop(0, groups, code, 0)
        copy.start()
        copies.append(copy)

    def receive(get, groups, size, key):
        copy, off, tiles = flights[key]
        assert tiles == groups * size
        copy.wait_recv()
        scale = jnp.exp2(pool_r[off + tiles].astype(F32)) * (1.0 / TOP)

        def add(g, carry):
            ref = get(g)
            ref[...] = ref[...] + pool_r[pl.ds(off + g * size, size)].astype(F32) * scale
            return carry

        if groups == 1:
            add(0, 0)
        else:
            lax.fori_loop(0, groups, add, 0)

    def rows_at(slot, row, first, size):
        return lambda g: acc.at[slot, row + g, pl.ds(first, size)]

    def left_step(i):
        loads[i].wait()

        def columns(jc, carry):
            tile = left_v[i, :, pl.ds(pl.multiple_of(jc * 512, 512), 512)]
            part = jnp.dot(amat[...], tile, preferred_element_type=F32)
            for u in range(4):
                value = part[:, u * 128:(u + 1) * 128].reshape(32, 16, 128)
                stage[:, 4 * jc + u] = value[0:8]
                stage[:, 8 + 4 * jc + u] = value[8:16]
                acc[i, :, 4 * jc + u] = value[16:24]
                acc[i, :, 8 + 4 * jc + u] = value[24:32]
            return carry

        lax.fori_loop(0, 2, columns, 0)
        send(lambda g: stage.at[g], 8, 16, ("core", i))

    for i in range(4):
        task(("left", i), [], [("left", i - 1)] if i else [], 1.4, 2,
             [message(("core", i), 128, "core")], lambda i=i: left_step(i))
        task(("sum", i), [("core", i)], [("left", i)], 0.25, 1, [],
             lambda i=i: receive(rows_at(i, 0, 0, 16), 8, 16, ("core", i)))

    na, half_a = PART_A, PART_A // 2
    for m in (0, 1):
        first = 4 * m

        def a_start(first=first, m=m):
            send(rows_at(0, first, 0, na), 2, na, ("A", m, 0, "+"))
            send(rows_at(0, first + 2, 0, na), 2, na, ("A", m, 0, "-"))

        def a_next(sign, first=first, m=m):
            slot, shift = (1, 0) if sign == "+" else (2, 2)
            receive(rows_at(slot, first + shift, 0, na), 2, na, ("A", m, 0, sign))
            send(rows_at(slot, first, 0, na), 4, na, ("A", m, 1, sign))

        def a_end(first=first, m=m):
            receive(rows_at(3, first, 0, na), 4, na, ("A", m, 1, "+"))
            receive(rows_at(3, first, 0, na), 4, na, ("A", m, 1, "-"))
            if m == 0:
                send(rows_at(3, 0, 0, half_a), 1, half_a, ("Z", 4))
                send(rows_at(3, 0, half_a, half_a), 1, half_a, ("Z", -4))
                send(rows_at(3, 1, 0, na), 1, na, ("Z", 3))
                send(rows_at(3, 2, 0, na), 1, na, ("Z", -3))
            else:
                send(rows_at(3, 5, 0, na), 1, na, ("Z", 1))
                send(rows_at(3, 6, 0, na), 1, na, ("Z", -1))

        task(("A", m, 0), [], [("sum", 0)], 0.3, 0,
             [message(("A", m, 0, "+"), 2 * na, "x+"), message(("A", m, 0, "-"), 2 * na, "x-")], a_start)
        for sign, before in (("+", 1), ("-", 2)):
            task(("A", m, 1, sign), [("A", m, 0, sign)], [("sum", before)], 0.4, 0,
                 [message(("A", m, 1, sign), 4 * na, "x" + sign)], lambda f=a_next, sign=sign: f(sign))
        if m == 0:
            sends = [message(("Z", 4), half_a, "z++"), message(("Z", -4), half_a, "z--"),
                     message(("Z", 3), na, "z+"), message(("Z", -3), na, "z-")]
        else:
            sends = [message(("Z", 1), na, "z+"), message(("Z", -1), na, "z-")]
        task(("A", m, 2), [("A", m, 1, "+"), ("A", m, 1, "-")], [("sum", 3)], 0.5, 0, sends, a_end)

    def z_relay(sign):
        row = 3 if sign > 0 else 4
        receive(rows_at(3, row, 0, na), 1, na, ("Z", 3 * sign))
        receive(rows_at(3, row, 0 if sign > 0 else half_a, half_a), 1, half_a, ("Z", 4 * sign))
        send(rows_at(3, row, 0, na), 1, na, ("Z", 2 * sign))

    def z_end(d):
        receive(rows_at(3, 7, 0, na), 1, na, ("Z", d))

    for sign in (1, -1):
        task(("Z", 2 * sign, 0), [("Z", 3 * sign), ("Z", 4 * sign)], [("A", 0, 2), ("A", 1, 2)], 0.25, 0,
             [message(("Z", 2 * sign), na, "z++" if sign > 0 else "z--")], lambda sign=sign: z_relay(sign))
    for d in (1, -1, 2, -2):
        task(("Z", d, 1), [("Z", d)], [("A", 1, 2)], 0.1, 1, [], lambda d=d: z_end(d))

    nb, half_b = 16 - na, (16 - na) // 2
    for i in range(4):
        def b_start(i=i):
            send(rows_at(i, 0, na, half_b), 1, half_b, ("B", i, 0, "+"))
            send(rows_at(i, 0, na + half_b, half_b), 1, half_b, ("B", i, 0, "-"))

        def b_next(s, sign, i=i):
            row = 2 * s - 1 if sign == "+" else 2 * s
            if s == 1:
                first = na if sign == "+" else na + half_b
                receive(rows_at(i, row, first, half_b), 1, half_b, ("B", i, 0, sign))
            else:
                receive(rows_at(i, row, na, nb), 1, nb, ("B", i, s - 1, sign))
            send(rows_at(i, row, na, nb), 1, nb, ("B", i, s, sign))

        def b_end(i=i):
            receive(rows_at(i, 7, na, nb), 1, nb, ("B", i, 3, "+"))
            receive(rows_at(i, 7, na, nb), 1, nb, ("B", i, 3, "-"))
            if i < 3:
                send(rows_at(i, 7, na, nb), 1, nb, ("X", i))

        task(("B", i, 0), [], [("sum", i)], 0.15, 0,
             [message(("B", i, 0, "+"), half_b, "z+"), message(("B", i, 0, "-"), half_b, "z-")], b_start)
        for s in (1, 2, 3):
            for sign in ("+", "-"):
                task(("B", i, s, sign), [("B", i, s - 1, sign)], [("sum", i)], 0.15, 0,
                     [message(("B", i, s, sign), nb, "z" + sign)], lambda f=b_next, s=s, sign=sign: f(s, sign))
        task(("B", i, 4), [("B", i, 3, "+"), ("B", i, 3, "-")], [("sum", i)], 0.2, 0,
             [message(("X", i), nb, ("x2", "x+", "x-")[i])] if i < 3 else [], b_end)
    for i in range(3):
        task(("X", i, 1), [("X", i)], [("B", 3, 4)], 0.1, 1, [],
             lambda i=i: receive(rows_at(3, 7, na, nb), 1, nb, ("X", i)))
    sums = [t[0] for t in tasks]

    core_first = core * 2048

    def finish():
        rows = acc[3, 7].reshape(256, 128)
        both = jnp.dot(rows, metric2[...], precision=lax.Precision.HIGHEST, preferred_element_type=F32)
        low = lax.broadcasted_iota(I32, (16, 128), 1) < 64
        for t in range(8):
            e, o = both[t * 16:(t + 1) * 16], both[128 + t * 16:144 + t * 16]
            turn[2 * t] = jnp.where(low, e, pltpu.roll(o, 64, 1))
            turn[2 * t + 1] = jnp.where(low, pltpu.roll(e, 64, 1), o)
        for sp in range(16):
            cols = pl.ds(pl.multiple_of(core_first + sp * 128, 128), 128)
            applied[z, pl.ds(pl.multiple_of(x * 16, 16), 16), cols] = turn[:, sp, :].astype(BF16)

    def piece(dz, dx, first, size):
        cols = pl.ds(pl.multiple_of(core_first + first, 128), size)
        block = lax.rem(z + dz + NZ, NZ)
        if dx is None:
            return applied.at[block, :, cols]
        return applied.at[block, pl.ds(pl.multiple_of(lax.rem(x + dx + NX, NX) * 16, 16), 16), cols]

    def share(key, link, dz, dx, first, size):
        number = gathers[0]
        gathers[0] += 1
        view = piece(dz, dx, first, size)
        flights[key] = pltpu.make_async_remote_copy(
            src_ref=view, dst_ref=view, send_sem=ag_send.at[number], recv_sem=ag_recv.at[number],
            device_id=links[link], device_id_type=MESH,
        )
        rows = 64 if dx is None else 16
        return (key, link, rows * size // 512)

    def gather(name, needs, after, shares, cost=0.05, rank=0, before=None):
        sends = [share(*a) for a in shares]

        def run():
            for key in needs:
                flights[key].wait_recv()
            if before is not None:
                before()
            for key, link, kib in sends:
                flights[key].start()
                copies.append(flights[key])

        task(name, needs, after, cost, rank, sends, run)

    ca, cb = COLS_A, 2048 - COLS_A
    ha, hb = ca // 2, cb // 2

    def along_x(dz):
        return [(("gx", dz, "+"), "x+", dz, 0, 0, ca), (("gx", dz, "-"), "x-", dz, 0, 0, ca)]

    def along_z(dx):
        return [(("gz", dx, 0, "+"), "z+", 0, dx, ca, cb), (("gz", dx, 0, "-"), "z-", 0, dx, ca, cb)]

    own = [(("ga", -1), "z+", 0, 0, 0, ca), (("ga", 1), "z-", 0, 0, 0, ca),
           (("gb", -1), "x+", 0, 0, ca, cb), (("gb", 1), "x-", 0, 0, ca, cb),
           (("ga", -2), "z++", 0, 0, 0, ca), (("ga", 2), "z--", 0, 0, 0, ca),
           (("gb", 2), "x2", 0, 0, ca, cb)]
    gather("own", [], sums, own + along_x(0) + along_z(0), cost=0.6, before=finish)
    for sign, way, first in ((-1, "+", 0), (1, "-", ha)):
        gather(("ga", 2 * sign), [("ga", 2 * sign)], ["own"],
               [(("ga", 3 * sign), "z" + way, 2 * sign, 0, 0, ca),
                (("ga", 4 * sign), "z" + way + way, 2 * sign, 0, first, ha)] + along_x(2 * sign))
        for d in (1, 3):
            gather(("ga", d * sign), [("ga", d * sign)], ["own"], along_x(d * sign))
    gather(("ga", 4), [("ga", -4), ("ga", 4)], ["own"], along_x(4))
    for dz in (0, -1, 1, -2, 2, -3, 3, 4):
        gather(("gx", dz, "+"), [("gx", dz, "+")], ["own"], [(("gy", dz, "+"), "x+", dz, -1, 0, ha)])
        gather(("gx", dz, "-"), [("gx", dz, "-")], ["own"], [(("gy", dz, "-"), "x-", dz, 1, ha, ha)])
        held = ["own", ("gx", dz, "+"), ("gx", dz, "-")] + ([("ga", dz)] if dz else [])
        gather(("gy", dz), [("gy", dz, "+"), ("gy", dz, "-")], held,
               [(("fa", dz), "core", dz, None, 0, ca)], rank=1)
    for dx in (-1, 1, 2):
        gather(("gb", dx), [("gb", dx)], ["own"], along_z(dx))
    for dx in (0, -1, 1, 2):
        for s in (1, 2, 3):
            size = cb if s < 3 else hb
            for way, dz, first in (("+", -s, ca), ("-", s, ca if s < 3 else ca + hb)):
                gather(("gz", dx, s, way), [("gz", dx, s - 1, way)], ["own"],
                       [(("gz", dx, s, way), "z" + way, dz, dx, first, size)])
        gather(("gz", dx, 4), [("gz", dx, 3, "+"), ("gz", dx, 3, "-")], ["own"], [])
    for dz in (0, -1, 1, -2, 2, -3, 3, 4):
        if dz == 0:
            held = ["own"] + [("gb", dx) for dx in (-1, 1, 2)]
        elif dz == 4:
            held = [("gz", dx, 4) for dx in (0, -1, 1, 2)]
        else:
            held = [("gz", dx, abs(dz), "+" if dz < 0 else "-") for dx in (0, -1, 1, 2)]
        gather(("fb", dz, 0), [], held, [(("fb", dz), "core", dz, None, ca, cb)], rank=1)
    assert counter == [POOL, N_MSG] and gathers == [N_GATHER]
    for one in in_order(tasks):
        one[-1]()
    for dz in (0, -1, 1, -2, 2, -3, 3, 4):
        flights[("fa", dz)].wait_recv()
        flights[("fb", dz)].wait_recv()

    back_load.wait()
    block_of = lax.shift_right_logical(lax.broadcasted_iota(I32, (1, 576), 1), 6)
    present = jnp.zeros((1, 576), F32)
    for b in range(9):
        present = jnp.where(block_of == b, pattern_s[b].astype(F32), present)

    def products(first, second):
        pieces = [applied[pl.ds(block * 2, 2)].reshape(128, 4096) for block in (first, second)]
        rows = jnp.concatenate(pieces, axis=0)
        both = lax.dot_general(rows, back_v[...], (((1,), (1,)), ((), ())), preferred_element_type=F32) * present
        return both[0:128], both[128:256]

    y_copies = []

    def y_start(n, value):
        y_send[n] = value.astype(BF16)
        copy = pltpu.make_async_remote_copy(
            src_ref=y_send.at[n], dst_ref=y_recv.at[n], send_sem=y_ssem.at[n], recv_sem=y_rsem.at[n],
            device_id=y_peers[n], device_id_type=MESH,
        )
        copy.start()
        y_copies.append(copy)

    far, near = products(lax.rem(y + 2, NY), lax.rem(y + 1, NY))
    y_start(1, far)
    y_start(0, near)
    near, mine = products(lax.rem(y + 3, NY), y)
    y_start(2, near)
    out_ref[...] = mine
    for copy in y_copies:
        copy.wait_recv()
    out_ref[...] = out_ref[...] + y_recv[0].astype(F32) + y_recv[1].astype(F32) + y_recv[2].astype(F32)
    for copy in copies + y_copies:
        copy.wait_send()


def per_device(left_tiles, left_row, left_lam, left_count, density, metric, back_tiles, back_pattern):
    vmem = pl.BlockSpec(memory_space=pltpu.VMEM)
    smem = pl.BlockSpec(memory_space=pltpu.SMEM)
    hbm = pl.BlockSpec(memory_space=pl.ANY)
    return pl.pallas_call(
        kernel,
        out_shape=jax.ShapeDtypeStruct((128, 576), F32),
        in_specs=[smem, smem, smem, smem, vmem, vmem, hbm, hbm],
        out_specs=vmem,
        scratch_shapes=[
            pltpu.VMEM((4, 768, 1024), BF16),
            pltpu.VMEM((576, 4096), BF16),
            pltpu.VMEM((576, 768), BF16),
            pltpu.VMEM((512, 768), BF16),
            pltpu.VMEM((8, 16, 16, 128), F32),
            pltpu.VMEM((4, 8, 16, 16, 128), F32),
            pltpu.VMEM((POOL, 16, 128), I16),
            pltpu.VMEM((POOL, 16, 128), I16),
            pltpu.VMEM((8, 64, 4096), BF16),
            pltpu.VMEM((3, 128, 576), BF16),
            pltpu.VMEM((3, 128, 576), BF16),
            pltpu.VMEM((128, 128), F32),
            pltpu.VMEM((16, 16, 128), F32),
            pltpu.SemaphoreType.DMA((N_MSG,)),
            pltpu.SemaphoreType.DMA((N_MSG,)),
            pltpu.SemaphoreType.DMA((N_GATHER,)),
            pltpu.SemaphoreType.DMA((N_GATHER,)),
            pltpu.SemaphoreType.DMA((3,)),
            pltpu.SemaphoreType.DMA((3,)),
            pltpu.SemaphoreType.DMA((5,)),
        ],
        compiler_params=pltpu.CompilerParams(
            collective_id=0, has_side_effects=True, vmem_limit_bytes=56 * 1024 * 1024
        ),
        cost_estimate=pl.CostEstimate(flops=6_000_000_000, bytes_accessed=12_000_000, transcendentals=0),
    )(
        left_row, left_lam, left_count, back_pattern.reshape(9), density.T, metric,
        left_tiles.reshape(768, 4096), back_tiles,
    )


def solution(mesh):
    placed = (
        P("pair", None, None),
        P("pair"),
        P("pair"),
        P("pair"),
        P("pair", "col"),
        P(),
        P("pair", "col"),
        P("pair", "col"),
    )
    return jax.shard_map(
        per_device, mesh=mesh, in_specs=placed, out_specs=P("col", "pair"), check_vma=False
    )
```

```python
import jax
import jax.numpy as jnp
from jax import lax
from jax.experimental import pallas as pl
from jax.experimental.pallas import tpu as pltpu
from jax.sharding import PartitionSpec as P

MESH = pl.DeviceIdType.MESH
F32, BF16, I16, I32 = jnp.float32, jnp.bfloat16, jnp.int16, jnp.int32

NZ, NX, NY = 8, 4, 4
SLOTS = 12
Z_ORDER = (4, 3, 5, 2, 6, 1, 7, 0)
X_ORDER = (2, 1, 3, 0)
TOP = 32000.0
ROUND = 12582912.0
COLS_A = 1536
ROWS_A = ((0, 3), (3, 5), (5, 8))
POSITION = {0: 0, 1: 1, 2: 2, -1: 3, 4: 4, -4: 4, -3: 5, -2: 6, 3: 7}
BLOCKS = ((0, 1), (1, 3), (4, 4))
POOL = 1032
N_MSG = 24
N_GATHER = 45


def in_order(tasks):
    now, free, arrival, done, order, left = 0.0, {}, {}, set(), [], list(tasks)
    while left:
        best = None
        for task in left:
            name, needs, after, cost, rank, sends, run = task
            if all(n in arrival for n in needs) and all(t in done for t in after):
                ready = max([arrival[n] for n in needs] + [now])
                if best is None or (ready, rank) < best[:2]:
                    best = (ready, rank, task)
        ready, rank, task = best
        now = ready + task[3] + 0.08 * len(task[1])
        for key, link, hops, kib in task[5]:
            now += 0.08
            if link == "core":
                arrival[key] = now + 1.0 + kib * 0.001
                continue
            each = kib * 2 * 1.024 / 115.0
            start = max(free.get(link, 0.0), now)
            free[link] = start + each * hops
            arrival[key] = start + each + 2.3 + 0.4 * (hops - 1)
        order.append(task)
        done.add(task[0])
        left.remove(task)
    return order


def kernel(
    row_s, lam_s, count_s, pattern_s, density, metric, left_hbm, back_hbm, out_ref,
    left_v, back_v, pick, amat, stage, acc, pool_s, pool_r, applied, y_send, y_recv, mine,
    metric2, turn, msg_send, msg_recv, ag_send, ag_recv, y_ssem, y_rsem, local_sem,
):
    pair = lax.axis_index("pair")
    y = lax.axis_index("col")
    core = lax.rem(pair, 2)
    x = lax.rem(lax.div(pair, 2), NX)
    z = lax.div(pair, 2 * NX)

    def at(zz, xx, cc):
        return {"pair": (lax.rem(zz, NZ) * NX + lax.rem(xx, NX)) * 2 + cc}

    peer = at(z, x, 1 - core)
    x_right, x_left = at(z, x + 1, core), at(z, x + NX - 1, core)
    z_right, z_left = at(z + 1, x, core), at(z + NZ - 1, x, core)
    y_peers = [{"col": lax.rem(y + dy, NY)} for dy in (1, 2, 3)]

    barrier = pltpu.get_barrier_semaphore()
    far_peers = [at(z, x + 2, core), at(z + 2, x, core), at(z + NZ - 2, x, core)]
    for other in [peer, x_right, x_left, z_right, z_left] + far_peers + y_peers:
        pl.semaphore_signal(barrier, inc=1, device_id=other, device_id_type=MESH)

    loads = []
    for i, off in enumerate(X_ORDER):
        first = pl.multiple_of(lax.rem(x + off, NX) * 1024, 1024)
        load = pltpu.make_async_copy(left_hbm.at[:, pl.ds(first, 1024)], left_v.at[i], local_sem.at[i])
        load.start()
        loads.append(load)
    back_load = pltpu.make_async_copy(back_hbm, back_v, local_sem.at[4])

    j = lax.broadcasted_iota(I32, (64, 64), 0)
    half_core = jnp.where(j < 32, 1 - core, core)
    sigma = half_core * 32 + 2 * (j & 15) + ((j >> 4) & 1)
    perm = jnp.where(lax.broadcasted_iota(I32, (64, 64), 1) == sigma, 1.0, 0.0).astype(BF16)
    sorted_density = jnp.dot(perm, density[...], preferred_element_type=F32).astype(BF16)
    lane = lax.broadcasted_iota(I32, (16, SLOTS * 64), 1)
    slot_of = lane >> 6
    lam_of = jnp.zeros((16, SLOTS * 64), I32)
    row_of = jnp.zeros((16, SLOTS * 64), I32)
    for s in range(SLOTS):
        lam_of = jnp.where(slot_of == s, lam_s[s], lam_of)
        row_of = jnp.where(slot_of == s, row_s[s], row_of)
    live = slot_of < count_s[0]
    source = row_of * 64 + (lane & 63)
    deep = lax.broadcasted_iota(I32, (16, SLOTS * 64), 0)
    for b in range(36):
        pick[b * 16:(b + 1) * 16, :] = jnp.where(source == deep + b * 16, 1.0, 0.0).astype(BF16)
    turned = jnp.dot(sorted_density, pick[...], preferred_element_type=F32)
    for r, off in enumerate(Z_ORDER):
        owner = lax.rem(z + off, NZ)
        here = live & (lam_of == 2 * lax.rem(owner, 4) + lax.div(owner, 4))
        for q in range(4):
            first = (q * 8 + r) * 16
            amat[first:first + 16, :] = jnp.where(here, turned[q * 16:(q + 1) * 16, :], 0.0).astype(BF16)

    metric2[...] = jnp.zeros((128, 128), F32)
    metric2[0:64, 0:64] = metric[...]
    metric2[64:128, 64:128] = metric[...]

    links = {
        "core": peer, "x+": x_right, "x-": x_left, "x2": at(z, x + 2, core),
        "z+": z_right, "z-": z_left, "z++": at(z + 2, x, core), "z--": at(z + NZ - 2, x, core),
    }
    lanes = {"x2": ("x+", 2), "z++": ("z+", 2), "z--": ("z-", 2)}
    copies, flights, tasks = [], {}, []
    counter, gathers = [0, 0], [0]

    def task(name, needs, after, cost, rank, sends, run):
        tasks.append((name, needs, after, cost, rank, [(k,) + lanes.get(l, (l, 1)) + (n,) for k, l, n in sends], run))

    def message(key, tiles, link):
        off, number = counter
        counter[0] += tiles + 1
        counter[1] += 1
        copy = pltpu.make_async_remote_copy(
            src_ref=pool_s.at[pl.ds(off, tiles + 1)], dst_ref=pool_r.at[pl.ds(off, tiles + 1)],
            send_sem=msg_send.at[number], recv_sem=msg_recv.at[number],
            device_id=links[link], device_id_type=MESH,
        )
        flights[key] = (copy, off, tiles)
        return (key, link, 4 * (tiles + 1))

    def send(get, groups, size, key):
        copy, off, tiles = flights[key]
        assert tiles == groups * size

        def largest(g, m):
            return jnp.maximum(m, jnp.max(jnp.abs(get(g)[...]), axis=0))

        def code(g, carry):
            value = (get(g)[...] * scale + ROUND) - ROUND
            pool_s[pl.ds(off + g * size, size)] = value.astype(I16)
            return carry

        top = jnp.zeros((16, 128), F32)
        top = largest(0, top) if groups == 1 else lax.fori_loop(0, groups, largest, top)
        power = jnp.ceil(jnp.log2(jnp.maximum(top, 1e-30)))
        scale = jnp.exp2(-power) * TOP
        pool_s[off + tiles] = power.astype(I16)
        if groups == 1:
            code(0, 0)
        else:
            lax.fori_loop(0, groups, code, 0)
        copy.start()
        copies.append(copy)

    def receive(get, groups, size, key):
        copy, off, tiles = flights[key]
        assert tiles == groups * size
        copy.wait_recv()
        scale = jnp.exp2(pool_r[off + tiles].astype(F32)) * (1.0 / TOP)

        def add(g, carry):
            ref = get(g)
            ref[...] = ref[...] + pool_r[pl.ds(off + g * size, size)].astype(F32) * scale
            return carry

        if groups == 1:
            add(0, 0)
        else:
            lax.fori_loop(0, groups, add, 0)

    def rows_at(slot, row, first, size):
        return lambda g: acc.at[slot, row + g, pl.ds(first, size)]

    def left_step(i):
        loads[i].wait()

        def columns(jc, carry):
            tile = left_v[i, :, pl.ds(pl.multiple_of(jc * 512, 512), 512)]
            part = jnp.dot(amat[...], tile, preferred_element_type=F32)
            for u in range(4):
                value = part[:, u * 128:(u + 1) * 128].reshape(32, 16, 128)
                stage[:, 4 * jc + u] = value[0:8]
                stage[:, 8 + 4 * jc + u] = value[8:16]
                acc[i, :, 4 * jc + u] = value[16:24]
                acc[i, :, 8 + 4 * jc + u] = value[24:32]
            return carry

        lax.fori_loop(0, 2, columns, 0)
        if i == 0:
            pl.semaphore_wait(barrier, 11)
        if i == 1:
            back_load.start()
        send(lambda g: stage.at[g], 8, 16, ("core", i))

    for i in range(4):
        task(("left", i), [], [("left", i - 1)] if i else [], 1.4, 2,
             [message(("core", i), 128, "core")], lambda i=i: left_step(i))
        task(("sum", i), [("core", i)], [("left", i)], 0.25, 1, [],
             lambda i=i: receive(rows_at(i, 0, 0, 16), 8, 16, ("core", i)))

    for m, (first, last) in enumerate(ROWS_A):
        count = last - first

        def x_start(first=first, count=count, m=m):
            send(rows_at(0, first, 0, 8), count, 8, ("A", m, 0, "+"))
            send(rows_at(0, first, 8, 8), count, 8, ("A", m, 0, "-"))

        def x_next(sign, first=first, count=count, m=m):
            slot, tile = (1, 0) if sign == "+" else (2, 8)
            receive(rows_at(slot, first, tile, 8), count, 8, ("A", m, 0, sign))
            send(rows_at(slot, first, 0, 16), count, 16, ("A", m, 1, sign))

        def x_end(first=first, count=count, m=m):
            receive(rows_at(3, first, 0, 16), count, 16, ("A", m, 1, "+"))
            receive(rows_at(3, first, 0, 16), count, 16, ("A", m, 1, "-"))
            if m == 0:
                send(rows_at(3, 0, 0, 8), 1, 8, ("Z", 4))
                send(rows_at(3, 0, 8, 8), 1, 8, ("Z", -4))
                send(rows_at(3, 1, 0, 16), 1, 16, ("Z", 3))
                send(rows_at(3, 2, 0, 16), 1, 16, ("Z", -3))
            if m == 2:
                send(rows_at(3, 5, 0, 16), 1, 16, ("Z", 1))
                send(rows_at(3, 6, 0, 16), 1, 16, ("Z", -1))

        task(("A", m, 0), [], [("sum", 0)], 0.2, 0,
             [message(("A", m, 0, "+"), 8 * count, "x+"), message(("A", m, 0, "-"), 8 * count, "x-")], x_start)
        for sign, before in (("+", 1), ("-", 2)):
            task(("A", m, 1, sign), [("A", m, 0, sign)], [("sum", before)], 0.3, 0,
                 [message(("A", m, 1, sign), 16 * count, "x" + sign)], lambda f=x_next, sign=sign: f(sign))
        sends = []
        if m == 0:
            sends = [message(("Z", 4), 8, "z++"), message(("Z", -4), 8, "z--"),
                     message(("Z", 3), 16, "z+"), message(("Z", -3), 16, "z-")]
        if m == 2:
            sends = [message(("Z", 1), 16, "z+"), message(("Z", -1), 16, "z-")]
        task(("A", m, 2), [("A", m, 1, "+"), ("A", m, 1, "-")], [("sum", 3)], 0.3, 0, sends, x_end)

    def z_relay(sign):
        row = 3 if sign > 0 else 4
        receive(rows_at(3, row, 0, 16), 1, 16, ("Z", 3 * sign))
        receive(rows_at(3, row, 0 if sign > 0 else 8, 8), 1, 8, ("Z", 4 * sign))
        send(rows_at(3, row, 0, 16), 1, 16, ("Z", 2 * sign))

    for sign in (1, -1):
        task(("Z", 2 * sign, 0), [("Z", 3 * sign), ("Z", 4 * sign)], [("A", 1, 2)], 0.2, 0,
             [message(("Z", 2 * sign), 16, "z++" if sign > 0 else "z--")], lambda sign=sign: z_relay(sign))
    for d in (1, -1, 2, -2):
        task(("Z", d, 1), [("Z", d)], [("A", 2, 2)], 0.1, 1, [],
             lambda d=d: receive(rows_at(3, 7, 0, 16), 1, 16, ("Z", d)))
    sums = [t[0] for t in tasks]

    core_first = core * 2048

    def finish():
        rows = acc[3, 7].reshape(256, 128)
        both = jnp.dot(rows, metric2[...], precision=lax.Precision.HIGHEST, preferred_element_type=F32)
        low = lax.broadcasted_iota(I32, (16, 128), 1) < 64
        for t in range(8):
            e, o = both[t * 16:(t + 1) * 16], both[128 + t * 16:144 + t * 16]
            turn[2 * t] = jnp.where(low, e, pltpu.roll(o, 64, 1))
            turn[2 * t + 1] = jnp.where(low, pltpu.roll(e, 64, 1), o)
        for sp in range(16):
            cols = pl.ds(pl.multiple_of(core_first + sp * 128, 128), 128)
            applied[0, 0:16, cols] = turn[:, sp, :].astype(BF16)

    def share(key, link, source, target, first, size):
        number = gathers[0]
        gathers[0] += 1
        cols = pl.ds(pl.multiple_of(core_first + first, 128), size)

        def view(block, blocks, row, rows):
            return applied.at[pl.ds(block, blocks), pl.ds(16 * row, 16 * rows), cols]

        flights[key] = pltpu.make_async_remote_copy(
            src_ref=view(*source), dst_ref=view(*target), send_sem=ag_send.at[number], recv_sem=ag_recv.at[number],
            device_id=links[link], device_id_type=MESH,
        )
        return (key, link, source[1] * source[3] * size / 32)

    def gather(name, needs, after, shares, cost=0.02, rank=0, before=None):
        sends = [share(*a) for a in shares]

        def run():
            for key in needs:
                flights[key].wait_recv()
            if before is not None:
                before()
            for key, link, kib in sends:
                flights[key].start()
                copies.append(flights[key])

        task(name, needs, after, cost, rank, sends, run)

    ca, cb = COLS_A, 2048 - COLS_A
    ha, hb = ca // 2, cb // 2

    def z_move(key, link, dz, to, row, rows, first, size):
        return (key, link, (POSITION[dz], 1, row, rows), (POSITION[to], 1, row, rows), first, size)

    def x_move(key, link, b, row, to, first, size):
        return (key, link, BLOCKS[b] + (row, 1), BLOCKS[b] + (to, 1), first, size)

    def along_x(b):
        return [x_move(("gx", b, "+"), "x+", b, 0, 3, 0, ca), x_move(("gx", b, "-"), "x-", b, 0, 1, 0, ca)]

    def along_z(g):
        row, rows = ((0, 1), (1, 3))[g]
        return [z_move(("gz", g, 0, "+"), "z+", 0, -1, row, rows, ca, cb),
                z_move(("gz", g, 0, "-"), "z-", 0, 1, row, rows, ca, cb)]

    own = [z_move(("ga", -1), "z+", 0, -1, 0, 1, 0, ca), z_move(("ga", 1), "z-", 0, 1, 0, 1, 0, ca),
           x_move(("gb", 3), "x+", 0, 0, 3, ca, cb), x_move(("gb", 1), "x-", 0, 0, 1, ca, cb),
           z_move(("ga", -2), "z++", 0, -2, 0, 1, 0, ca), z_move(("ga", 2), "z--", 0, 2, 0, 1, 0, ca),
           x_move(("gb", 2), "x2", 0, 0, 2, ca, cb)]
    gather("own", [], sums, own + along_x(0) + along_z(0), cost=0.6, before=finish)
    for sign, way, first in ((-1, "+", 0), (1, "-", ha)):
        gather(("ga", 2 * sign), [("ga", 2 * sign)], ["own"],
               [z_move(("ga", 3 * sign), "z" + way, 2 * sign, 3 * sign, 0, 1, 0, ca),
                z_move(("ga", 4 * sign), "z" + way + way, 2 * sign, 4, 0, 1, first, ha)])
        for d in (1, 3, 4):
            gather(("ga", d * sign), [("ga", d * sign)], ["own"], [])
    gather(("gx", 1), [], [("ga", 1), ("ga", 2), ("ga", -1)], along_x(1), cost=0.0)
    gather(("gx", 2), [], [("ga", 4), ("ga", -4), ("ga", -3), ("ga", -2), ("ga", 3)], along_x(2), cost=0.0)
    for b in (0, 1, 2):
        held = [("gx", b) if b else "own"]
        gather(("gx", b, "+"), [("gx", b, "+")], held, [x_move(("gy", b, "+"), "x+", b, 3, 2, 0, ha)])
        gather(("gx", b, "-"), [("gx", b, "-")], held, [x_move(("gy", b, "-"), "x-", b, 1, 2, ha, ha)])
        gather(("gy", b), [("gy", b, "+"), ("gy", b, "-")], [("gx", b, "+"), ("gx", b, "-")],
               [(("fa", b), "core", BLOCKS[b] + (0, 4), BLOCKS[b] + (0, 4), 0, ca)], rank=1)
    for g in (1, 2, 3):
        gather(("gb", g), [("gb", g)], ["own"], [])
    gather(("gz", 1), [], [("gb", 1), ("gb", 2), ("gb", 3)], along_z(1), cost=0.0)
    for g, (row, rows) in enumerate(((0, 1), (1, 3))):
        held = [("gz", 1) if g else "own"]
        for d in (1, 2, 3):
            size = cb if d < 3 else hb
            for way, sign, first in (("+", -1, ca), ("-", 1, ca if d < 3 else ca + hb)):
                gather(("gz", g, d, way), [("gz", g, d - 1, way)], held,
                       [z_move(("gz", g, d, way), "z" + way, d * sign, (d + 1) * sign, row, rows, first, size)])
        gather(("gz", g, 4), [("gz", g, 3, "+"), ("gz", g, 3, "-")], held, [])
    near = [("gz", g, d, way) for g in (0, 1) for d, way in ((1, "+"), (1, "-"), (2, "-"))]
    far = [("gz", g, d, way) for g in (0, 1) for d, way in ((2, "+"), (3, "+"), (3, "-"))]
    far += [("gz", 0, 4), ("gz", 1, 4)]
    for b, held in enumerate((["own", ("gz", 1)], near, far)):
        gather(("fb", b, 0), [], held, [(("fb", b), "core", BLOCKS[b] + (0, 4), BLOCKS[b] + (0, 4), ca, cb)], rank=1)

    block_of = lax.shift_right_logical(lax.broadcasted_iota(I32, (1, 576), 1), 6)

    def product(half, part):
        lo, hi = ((0, 256), (256, 512), (512, 576))[part]
        present = jnp.zeros((1, 576), F32)
        for b in range(9):
            present = jnp.where(block_of == b, pattern_s[b].astype(F32), present)
        if half == 0 and part == 0:
            back_load.wait()
        blocks = [4 * half + lax.rem(y + n + 1 + NZ - z, 4) for n in (0, 1, 2, 3)]
        rows = jnp.concatenate([applied[b] for b in blocks], axis=0)
        out = lax.dot_general(rows, back_v[lo:hi, :], (((1,), (1,)), ((), ())), preferred_element_type=F32)
        out = out * present[:, lo:hi]
        for n in range(3):
            y_send[half, n, :, lo:hi] = out[64 * n:64 * n + 64].astype(BF16)
        mine[half, :, lo:hi] = out[192:256]

    def y_copy(half, n):
        number = 3 * half + n
        return pltpu.make_async_remote_copy(
            src_ref=y_send.at[half, n], dst_ref=y_recv.at[half, n],
            send_sem=y_ssem.at[number], recv_sem=y_rsem.at[number],
            device_id=y_peers[n], device_id_type=MESH,
        )

    def y_start(half):
        for n in (1, 0, 2):
            flights[("y", half, n)] = y_copy(half, n)
            flights[("y", half, n)].start()
            copies.append(flights[("y", half, n)])

    for half, arrived, before in ((0, (0, 1), [("gy", 0), ("gy", 1), ("fb", 0, 0), ("fb", 1, 0)]),
                                  (1, (2,), [("gy", 2), ("fb", 2, 0)])):
        for b in arrived:
            for kind in ("fa", "fb"):
                gather((kind, b, 1), [(kind, b)], before, [], rank=3)
                before = before + [(kind, b, 1)]
        for part in (0, 1, 2):
            task(("product", half, part), [], before, 0.65, 3, [], lambda half=half, part=part: product(half, part))
            before = before + [("product", half, part)]
        task(("y", half), [], before, 0.3, 3, [], lambda half=half: y_start(half))
    assert counter == [POOL, N_MSG] and gathers == [N_GATHER]
    for one in in_order(tasks):
        one[-1]()

    k = lax.rem(y + NZ - z, 4)
    parity = lax.div(lax.rem(z + k + NZ - 4 * lax.div(k, 3), NZ), 4)
    for half in (0, 1):
        for n in range(3):
            flights[("y", half, n)].wait_recv()
        total = mine[half]
        for n in range(3):
            total = total + y_recv[half, n].astype(F32)
        base = (parity if half == 0 else 1 - parity) * 64
        for j in range(4):
            row = pl.multiple_of(base + lax.rem(x + j, NX) * 16, 16)
            out_ref[pl.ds(row, 16), :] = total[16 * j:16 * j + 16]
    for copy in copies:
        copy.wait_send()


def per_device(left_tiles, left_row, left_lam, left_count, density, metric, back_tiles, back_pattern):
    vmem = pl.BlockSpec(memory_space=pltpu.VMEM)
    smem = pl.BlockSpec(memory_space=pltpu.SMEM)
    hbm = pl.BlockSpec(memory_space=pl.ANY)
    return pl.pallas_call(
        kernel,
        out_shape=jax.ShapeDtypeStruct((128, 576), F32),
        in_specs=[smem, smem, smem, smem, vmem, vmem, hbm, hbm],
        out_specs=vmem,
        scratch_shapes=[
            pltpu.VMEM((4, 768, 1024), BF16),
            pltpu.VMEM((576, 4096), BF16),
            pltpu.VMEM((576, 768), BF16),
            pltpu.VMEM((512, 768), BF16),
            pltpu.VMEM((8, 16, 16, 128), F32),
            pltpu.VMEM((4, 8, 16, 16, 128), F32),
            pltpu.VMEM((POOL, 16, 128), I16),
            pltpu.VMEM((POOL, 16, 128), I16),
            pltpu.VMEM((8, 64, 4096), BF16),
            pltpu.VMEM((2, 3, 64, 576), BF16),
            pltpu.VMEM((2, 3, 64, 576), BF16),
            pltpu.VMEM((2, 64, 576), F32),
            pltpu.VMEM((128, 128), F32),
            pltpu.VMEM((16, 16, 128), F32),
            pltpu.SemaphoreType.DMA((N_MSG,)),
            pltpu.SemaphoreType.DMA((N_MSG,)),
            pltpu.SemaphoreType.DMA((N_GATHER,)),
            pltpu.SemaphoreType.DMA((N_GATHER,)),
            pltpu.SemaphoreType.DMA((6,)),
            pltpu.SemaphoreType.DMA((6,)),
            pltpu.SemaphoreType.DMA((5,)),
        ],
        compiler_params=pltpu.CompilerParams(
            collective_id=0, has_side_effects=True, vmem_limit_bytes=56 * 1024 * 1024
        ),
        cost_estimate=pl.CostEstimate(flops=6_000_000_000, bytes_accessed=12_000_000, transcendentals=0),
    )(
        left_row, left_lam, left_count, back_pattern.reshape(9), density.T, metric,
        left_tiles.reshape(768, 4096), back_tiles,
    )


def solution(mesh):
    placed = (
        P("pair", None, None),
        P("pair"),
        P("pair"),
        P("pair"),
        P("pair", "col"),
        P(),
        P("pair", "col"),
        P("pair", "col"),
    )
    return jax.shard_map(
        per_device, mesh=mesh, in_specs=placed, out_specs=P("col", "pair"), check_vma=False
    )
```

```python
import jax
import jax.numpy as jnp
from jax import lax
from jax.experimental import pallas as pl
from jax.experimental.pallas import tpu as pltpu
from jax.sharding import PartitionSpec as P

MESH = pl.DeviceIdType.MESH
F32, BF16, I16, I32 = jnp.float32, jnp.bfloat16, jnp.int16, jnp.int32

NZ, NX, NY = 8, 4, 4
SLOTS = 12
Z_ORDER = (4, 3, 5, 2, 6, 1, 7, 0)
X_ORDER = (2, 1, 3, 0)
TOP = 32000.0
ROUND = 12582912.0
COLS_A = 1536
ROWS_A = ((0, 3), (3, 7), (7, 8))
POSITION = {0: 0, 1: 1, 2: 2, -1: 3, 4: 4, -4: 4, -3: 5, -2: 6, 3: 7}
BLOCKS = ((0, 1), (1, 3), (6, 1), (4, 2), (7, 1))
DISTANCE = (0, 1, 2, -1, 4, -3, -2, 3)
POOL = 1032
N_MSG = 24
N_GATHER = 55


def in_order(tasks):
    now, free, arrival, done, order, left = 0.0, {}, {}, set(), [], list(tasks)
    while left:
        best = None
        for task in left:
            name, needs, after, cost, rank, sends, run = task
            if all(n in arrival for n in needs) and all(t in done for t in after):
                ready = max([arrival[n] for n in needs] + [now])
                if best is None or (ready, rank) < best[:2]:
                    best = (ready, rank, task)
        ready, rank, task = best
        now = ready + task[3] + 0.08 * len(task[1])
        for key, link, hops, kib in task[5]:
            now += 0.08
            if link == "core":
                arrival[key] = now + 1.0 + kib * 0.001
                continue
            each = kib * 2 * 1.024 / 115.0
            start = max(free.get(link, 0.0), now)
            free[link] = start + each * hops
            arrival[key] = start + each + 2.3 + 0.4 * (hops - 1)
        order.append(task)
        done.add(task[0])
        left.remove(task)
    return order


def kernel(
    row_s, lam_s, count_s, pattern_s, density, metric, left_hbm, back_hbm, out_ref,
    left_v, back_v, pick, amat, stage, acc, pool_s, pool_r, applied, y_send, y_recv, mine,
    metric2, turn, msg_send, msg_recv, ag_send, ag_recv, y_ssem, y_rsem, local_sem,
):
    pair = lax.axis_index("pair")
    y = lax.axis_index("col")
    core = lax.rem(pair, 2)
    x = lax.rem(lax.div(pair, 2), NX)
    z = lax.div(pair, 2 * NX)

    def at(zz, xx, cc):
        return {"pair": (lax.rem(zz, NZ) * NX + lax.rem(xx, NX)) * 2 + cc}

    peer = at(z, x, 1 - core)
    x_right, x_left = at(z, x + 1, core), at(z, x + NX - 1, core)
    z_right, z_left = at(z + 1, x, core), at(z + NZ - 1, x, core)
    y_peers = [{"col": lax.rem(y + dy, NY)} for dy in (1, 2, 3)]

    barrier = pltpu.get_barrier_semaphore()
    far_peers = [at(z, x + 2, core), at(z + 2, x, core), at(z + NZ - 2, x, core)]
    for other in [peer, x_right, x_left, z_right, z_left] + far_peers + y_peers:
        pl.semaphore_signal(barrier, inc=1, device_id=other, device_id_type=MESH)

    loads = []
    for i, off in enumerate(X_ORDER):
        first = pl.multiple_of(lax.rem(x + off, NX) * 1024, 1024)
        load = pltpu.make_async_copy(left_hbm.at[:, pl.ds(first, 1024)], left_v.at[i], local_sem.at[i])
        load.start()
        loads.append(load)
    back_load = pltpu.make_async_copy(back_hbm, back_v, local_sem.at[4])

    j = lax.broadcasted_iota(I32, (64, 64), 0)
    half_core = jnp.where(j < 32, 1 - core, core)
    sigma = half_core * 32 + 2 * (j & 15) + ((j >> 4) & 1)
    perm = jnp.where(lax.broadcasted_iota(I32, (64, 64), 1) == sigma, 1.0, 0.0).astype(BF16)
    sorted_density = jnp.dot(perm, density[...], preferred_element_type=F32).astype(BF16)
    lane = lax.broadcasted_iota(I32, (16, SLOTS * 64), 1)
    slot_of = lane >> 6
    lam_of = jnp.zeros((16, SLOTS * 64), I32)
    row_of = jnp.zeros((16, SLOTS * 64), I32)
    for s in range(SLOTS):
        lam_of = jnp.where(slot_of == s, lam_s[s], lam_of)
        row_of = jnp.where(slot_of == s, row_s[s], row_of)
    live = slot_of < count_s[0]
    source = row_of * 64 + (lane & 63)
    deep = lax.broadcasted_iota(I32, (16, SLOTS * 64), 0)
    for b in range(36):
        pick[b * 16:(b + 1) * 16, :] = jnp.where(source == deep + b * 16, 1.0, 0.0).astype(BF16)
    turned = jnp.dot(sorted_density, pick[...], preferred_element_type=F32)
    for r, off in enumerate(Z_ORDER):
        owner = lax.rem(z + off, NZ)
        here = live & (lam_of == 2 * lax.rem(owner, 4) + lax.div(owner, 4))
        for q in range(4):
            first = (q * 8 + r) * 16
            amat[first:first + 16, :] = jnp.where(here, turned[q * 16:(q + 1) * 16, :], 0.0).astype(BF16)

    metric2[...] = jnp.zeros((128, 128), F32)
    metric2[0:64, 0:64] = metric[...]
    metric2[64:128, 64:128] = metric[...]

    links = {
        "core": peer, "x+": x_right, "x-": x_left, "x2": at(z, x + 2, core),
        "z+": z_right, "z-": z_left, "z++": at(z + 2, x, core), "z--": at(z + NZ - 2, x, core),
    }
    lanes = {"x2": ("x+", 2), "z++": ("z+", 2), "z--": ("z-", 2)}
    copies, flights, tasks = [], {}, []
    counter, gathers = [0, 0], [0]

    def task(name, needs, after, cost, rank, sends, run):
        tasks.append((name, needs, after, cost, rank, [(k,) + lanes.get(l, (l, 1)) + (n,) for k, l, n in sends], run))

    def message(key, tiles, link):
        off, number = counter
        counter[0] += tiles + 1
        counter[1] += 1
        copy = pltpu.make_async_remote_copy(
            src_ref=pool_s.at[pl.ds(off, tiles + 1)], dst_ref=pool_r.at[pl.ds(off, tiles + 1)],
            send_sem=msg_send.at[number], recv_sem=msg_recv.at[number],
            device_id=links[link], device_id_type=MESH,
        )
        flights[key] = (copy, off, tiles)
        return (key, link, 4 * (tiles + 1))

    def send(get, groups, size, key):
        copy, off, tiles = flights[key]
        assert tiles == groups * size

        def largest(g, m):
            return jnp.maximum(m, jnp.max(jnp.abs(get(g)[...]), axis=0))

        def code(g, carry):
            value = (get(g)[...] * scale + ROUND) - ROUND
            pool_s[pl.ds(off + g * size, size)] = value.astype(I16)
            return carry

        top = jnp.zeros((16, 128), F32)
        top = largest(0, top) if groups == 1 else lax.fori_loop(0, groups, largest, top)
        power = jnp.ceil(jnp.log2(jnp.maximum(top, 1e-30)))
        scale = jnp.exp2(-power) * TOP
        pool_s[off + tiles] = power.astype(I16)
        if groups == 1:
            code(0, 0)
        else:
            lax.fori_loop(0, groups, code, 0)
        copy.start()
        copies.append(copy)

    def receive(get, groups, size, key):
        copy, off, tiles = flights[key]
        assert tiles == groups * size
        copy.wait_recv()
        scale = jnp.exp2(pool_r[off + tiles].astype(F32)) * (1.0 / TOP)

        def add(g, carry):
            ref = get(g)
            ref[...] = ref[...] + pool_r[pl.ds(off + g * size, size)].astype(F32) * scale
            return carry

        if groups == 1:
            add(0, 0)
        else:
            lax.fori_loop(0, groups, add, 0)

    def rows_at(slot, row, first, size):
        return lambda g: acc.at[slot, row + g, pl.ds(first, size)]

    def left_step(i):
        loads[i].wait()

        def columns(jc, carry):
            tile = left_v[i, :, pl.ds(pl.multiple_of(jc * 512, 512), 512)]
            part = jnp.dot(amat[...], tile, preferred_element_type=F32)
            for u in range(4):
                value = part[:, u * 128:(u + 1) * 128].reshape(32, 16, 128)
                stage[:, 4 * jc + u] = value[0:8]
                stage[:, 8 + 4 * jc + u] = value[8:16]
                acc[i, :, 4 * jc + u] = value[16:24]
                acc[i, :, 8 + 4 * jc + u] = value[24:32]
            return carry

        lax.fori_loop(0, 2, columns, 0)
        if i == 0:
            pl.semaphore_wait(barrier, 11)
        if i == 1:
            back_load.start()
        send(lambda g: stage.at[g], 8, 16, ("core", i))

    for i in range(4):
        task(("left", i), [], [("left", i - 1)] if i else [], 1.4, 2,
             [message(("core", i), 128, "core")], lambda i=i: left_step(i))
        task(("sum", i), [("core", i)], [("left", i)], 0.25, 1, [],
             lambda i=i: receive(rows_at(i, 0, 0, 16), 8, 16, ("core", i)))

    for m, (first, last) in enumerate(ROWS_A):
        count = last - first

        def x_start(first=first, count=count, m=m):
            send(rows_at(0, first, 0, 8), count, 8, ("A", m, 0, "+"))
            send(rows_at(0, first, 8, 8), count, 8, ("A", m, 0, "-"))

        def x_next(sign, first=first, count=count, m=m):
            slot, tile = (1, 0) if sign == "+" else (2, 8)
            receive(rows_at(slot, first, tile, 8), count, 8, ("A", m, 0, sign))
            send(rows_at(slot, first, 0, 16), count, 16, ("A", m, 1, sign))

        def x_end(first=first, last=last, count=count, m=m):
            receive(rows_at(3, first, 0, 16), count, 16, ("A", m, 1, "+"))
            receive(rows_at(3, first, 0, 16), count, 16, ("A", m, 1, "-"))
            if first <= 2 < last:
                send(rows_at(3, 0, 0, 8), 1, 8, ("Z", 4))
                send(rows_at(3, 0, 8, 8), 1, 8, ("Z", -4))
                send(rows_at(3, 1, 0, 16), 1, 16, ("Z", 3))
                send(rows_at(3, 2, 0, 16), 1, 16, ("Z", -3))
            if first <= 6 < last:
                send(rows_at(3, 5, 0, 16), 1, 16, ("Z", 1))
                send(rows_at(3, 6, 0, 16), 1, 16, ("Z", -1))

        task(("A", m, 0), [], [("sum", 0)], 0.2, 0,
             [message(("A", m, 0, "+"), 8 * count, "x+"), message(("A", m, 0, "-"), 8 * count, "x-")], x_start)
        for sign, before in (("+", 1), ("-", 2)):
            task(("A", m, 1, sign), [("A", m, 0, sign)], [("sum", before)], 0.3, 0,
                 [message(("A", m, 1, sign), 16 * count, "x" + sign)], lambda f=x_next, sign=sign: f(sign))
        sends = []
        if first <= 2 < last:
            sends = [message(("Z", 4), 8, "z++"), message(("Z", -4), 8, "z--"),
                     message(("Z", 3), 16, "z+"), message(("Z", -3), 16, "z-")]
        if first <= 6 < last:
            sends = sends + [message(("Z", 1), 16, "z+"), message(("Z", -1), 16, "z-")]
        task(("A", m, 2), [("A", m, 1, "+"), ("A", m, 1, "-")], [("sum", 3)], 0.3, 0, sends, x_end)

    relay_run = [m for m, (first, last) in enumerate(ROWS_A) if first <= 4 < last][0]
    end = len(ROWS_A) - 1

    def z_relay(sign):
        row = 3 if sign > 0 else 4
        receive(rows_at(3, row, 0, 16), 1, 16, ("Z", 3 * sign))
        receive(rows_at(3, row, 0 if sign > 0 else 8, 8), 1, 8, ("Z", 4 * sign))
        send(rows_at(3, row, 0, 16), 1, 16, ("Z", 2 * sign))

    for sign in (1, -1):
        task(("Z", 2 * sign, 0), [("Z", 3 * sign), ("Z", 4 * sign)], [("A", relay_run, 2)], 0.2, 0,
             [message(("Z", 2 * sign), 16, "z++" if sign > 0 else "z--")], lambda sign=sign: z_relay(sign))
    for d in (1, -1, 2, -2):
        task(("Z", d, 1), [("Z", d)], [("A", end, 2)], 0.1, 1, [],
             lambda d=d: receive(rows_at(3, 7, 0, 16), 1, 16, ("Z", d)))
    sums = [t[0] for t in tasks]

    core_first = core * 2048

    def finish():
        rows = acc[3, 7].reshape(256, 128)
        both = jnp.dot(rows, metric2[...], precision=lax.Precision.HIGHEST, preferred_element_type=F32)
        low = lax.broadcasted_iota(I32, (16, 128), 1) < 64
        for t in range(8):
            e, o = both[t * 16:(t + 1) * 16], both[128 + t * 16:144 + t * 16]
            turn[2 * t] = jnp.where(low, e, pltpu.roll(o, 64, 1))
            turn[2 * t + 1] = jnp.where(low, pltpu.roll(e, 64, 1), o)
        for sp in range(16):
            cols = pl.ds(pl.multiple_of(core_first + sp * 128, 128), 128)
            applied[0, 0:16, cols] = turn[:, sp, :].astype(BF16)

    def share(key, link, source, target, first, size):
        number = gathers[0]
        gathers[0] += 1
        cols = pl.ds(pl.multiple_of(core_first + first, 128), size)

        def view(block, blocks, row, rows):
            return applied.at[pl.ds(block, blocks), pl.ds(16 * row, 16 * rows), cols]

        flights[key] = pltpu.make_async_remote_copy(
            src_ref=view(*source), dst_ref=view(*target), send_sem=ag_send.at[number], recv_sem=ag_recv.at[number],
            device_id=links[link], device_id_type=MESH,
        )
        return (key, link, source[1] * source[3] * size / 32)

    def gather(name, needs, after, shares, cost=0.02, rank=0, before=None):
        sends = [share(*a) for a in shares]

        def run():
            for key in needs:
                flights[key].wait_recv()
            if before is not None:
                before()
            for key, link, kib in sends:
                flights[key].start()
                copies.append(flights[key])

        task(name, needs, after, cost, rank, sends, run)

    ca, cb = COLS_A, 2048 - COLS_A
    ha, hb = ca // 2, cb // 2

    def z_move(key, link, dz, to, row, rows, first, size):
        return (key, link, (POSITION[dz], 1, row, rows), (POSITION[to], 1, row, rows), first, size)

    def x_move(key, link, b, row, to, first, size):
        return (key, link, BLOCKS[b] + (row, 1), BLOCKS[b] + (to, 1), first, size)

    def along_x(b):
        return [x_move(("gx", b, "+"), "x+", b, 0, 3, 0, ca), x_move(("gx", b, "-"), "x-", b, 0, 1, 0, ca)]

    def along_z(g):
        row, rows = ((0, 1), (1, 3))[g]
        return [z_move(("gz", g, 0, "+"), "z+", 0, -1, row, rows, ca, cb),
                z_move(("gz", g, 0, "-"), "z-", 0, 1, row, rows, ca, cb)]

    own = [z_move(("ga", -1), "z+", 0, -1, 0, 1, 0, ca), z_move(("ga", 1), "z-", 0, 1, 0, 1, 0, ca),
           x_move(("gb", 3), "x+", 0, 0, 3, ca, cb), x_move(("gb", 1), "x-", 0, 0, 1, ca, cb),
           z_move(("ga", -2), "z++", 0, -2, 0, 1, 0, ca), z_move(("ga", 2), "z--", 0, 2, 0, 1, 0, ca),
           x_move(("gb", 2), "x2", 0, 0, 2, ca, cb)]
    gather("own", [], sums, own + along_x(0) + along_z(0), cost=0.6, before=finish)
    for sign, way, first in ((-1, "+", 0), (1, "-", ha)):
        gather(("ga", 2 * sign), [("ga", 2 * sign)], ["own"],
               [z_move(("ga", 3 * sign), "z" + way, 2 * sign, 3 * sign, 0, 1, 0, ca),
                z_move(("ga", 4 * sign), "z" + way + way, 2 * sign, 4, 0, 1, first, ha)])
        for d in (1, 3, 4):
            gather(("ga", d * sign), [("ga", d * sign)], ["own"], [])
    for b, (block, blocks) in enumerate(BLOCKS[1:], 1):
        held = [("ga", d) for d in DISTANCE[block:block + blocks]]
        gather(("gx", b), [], held + ([("ga", -4)] if ("ga", 4) in held else []), along_x(b), cost=0.0)
    for b in range(len(BLOCKS)):
        held = [("gx", b) if b else "own"]
        gather(("gx", b, "+"), [("gx", b, "+")], held, [x_move(("gy", b, "+"), "x+", b, 3, 2, 0, ha)])
        gather(("gx", b, "-"), [("gx", b, "-")], held, [x_move(("gy", b, "-"), "x-", b, 1, 2, ha, ha)])
        gather(("gy", b), [("gy", b, "+"), ("gy", b, "-")], [("gx", b, "+"), ("gx", b, "-")],
               [(("fa", b), "core", BLOCKS[b] + (0, 4), BLOCKS[b] + (0, 4), 0, ca)], rank=1)
    for g in (1, 2, 3):
        gather(("gb", g), [("gb", g)], ["own"], [])
    gather(("gz", 1), [], [("gb", 1), ("gb", 2), ("gb", 3)], along_z(1), cost=0.0)
    for g, (row, rows) in enumerate(((0, 1), (1, 3))):
        held = [("gz", 1) if g else "own"]
        for d in (1, 2, 3):
            size = cb if d < 3 else hb
            for way, sign, first in (("+", -1, ca), ("-", 1, ca if d < 3 else ca + hb)):
                gather(("gz", g, d, way), [("gz", g, d - 1, way)], held,
                       [z_move(("gz", g, d, way), "z" + way, d * sign, (d + 1) * sign, row, rows, first, size)])
        gather(("gz", g, 4), [("gz", g, 3, "+"), ("gz", g, 3, "-")], held, [])
    near = [("gz", g, d, way) for g in (0, 1) for d, way in ((1, "+"), (1, "-"), (2, "-"))]
    far = [("gz", g, d, way) for g in (0, 1) for d, way in ((2, "+"), (3, "+"), (3, "-"))]
    far += [("gz", 0, 4), ("gz", 1, 4)]
    for b, held in enumerate((["own", ("gz", 1)], near, far)):
        whole = ((0, 1, 0, 4), (1, 3, 0, 4), (4, 4, 0, 4))[b]
        gather(("fb", b, 0), [], held, [(("fb", b), "core", whole, whole, ca, cb)], rank=1)

    block_of = lax.shift_right_logical(lax.broadcasted_iota(I32, (1, 576), 1), 6)

    def product(half, part):
        lo, hi = ((0, 256), (256, 512), (512, 576))[part]
        present = jnp.zeros((1, 576), F32)
        for b in range(9):
            present = jnp.where(block_of == b, pattern_s[b].astype(F32), present)
        if half == 0 and part == 0:
            back_load.wait()
        blocks = [4 * half + lax.rem(y + n + 1 + NZ - z, 4) for n in (0, 1, 2, 3)]
        rows = jnp.concatenate([applied[b] for b in blocks], axis=0)
        out = lax.dot_general(rows, back_v[lo:hi, :], (((1,), (1,)), ((), ())), preferred_element_type=F32)
        out = out * present[:, lo:hi]
        for n in range(3):
            y_send[half, n, :, lo:hi] = out[64 * n:64 * n + 64].astype(BF16)
        mine[half, :, lo:hi] = out[192:256]

    def y_start(half, part):
        lo, hi = ((0, 512), (512, 576), (0, 256), (256, 576))[part]
        for n in (1, 0, 2):
            number = 3 * part + n
            copy = pltpu.make_async_remote_copy(
                src_ref=y_send.at[half, n, :, pl.ds(lo, hi - lo)], dst_ref=y_recv.at[half, n, :, pl.ds(lo, hi - lo)],
                send_sem=y_ssem.at[number], recv_sem=y_rsem.at[number],
                device_id=y_peers[n], device_id_type=MESH,
            )
            flights[("y", part, n)] = copy
            copy.start()
            copies.append(copy)

    before = []
    for half in (0, 1):
        for b in range(len(BLOCKS)):
            if BLOCKS[b][0] // 4 == half:
                gather(("fa", b, 1), [("fa", b)], before + [("gy", b)], [], rank=3)
                before = [("fa", b, 1)]
        for b in ((0, 1), (2,))[half]:
            gather(("fb", b, 1), [("fb", b)], before + [("fb", b, 0)], [], rank=3)
            before = [("fb", b, 1)]
        for part in (0, 1, 2):
            task(("product", half, part), [], before, 0.65, 3, [], lambda half=half, part=part: product(half, part))
            before = [("product", half, part)]
            if (half, part) in ((0, 1), (0, 2), (1, 0), (1, 2)):
                number = ((0, 1), (0, 2), (1, 0), (1, 2)).index((half, part))
                task(("y", number), [], before, 0.3, 2, [], lambda half=half, number=number: y_start(half, number))
    assert counter == [POOL, N_MSG] and gathers == [N_GATHER]
    for one in in_order(tasks):
        one[-1]()

    k = lax.rem(y + NZ - z, 4)
    parity = lax.div(lax.rem(z + k + NZ - 4 * lax.div(k, 3), NZ), 4)
    for half in (0, 1):
        for n in range(3):
            flights[("y", 2 * half, n)].wait_recv()
            flights[("y", 2 * half + 1, n)].wait_recv()
        total = mine[half]
        for n in range(3):
            total = total + y_recv[half, n].astype(F32)
        base = (parity if half == 0 else 1 - parity) * 64
        for j in range(4):
            row = pl.multiple_of(base + lax.rem(x + j, NX) * 16, 16)
            out_ref[pl.ds(row, 16), :] = total[16 * j:16 * j + 16]
    for copy in copies:
        copy.wait_send()


def per_device(left_tiles, left_row, left_lam, left_count, density, metric, back_tiles, back_pattern):
    vmem = pl.BlockSpec(memory_space=pltpu.VMEM)
    smem = pl.BlockSpec(memory_space=pltpu.SMEM)
    hbm = pl.BlockSpec(memory_space=pl.ANY)
    return pl.pallas_call(
        kernel,
        out_shape=jax.ShapeDtypeStruct((128, 576), F32),
        in_specs=[smem, smem, smem, smem, vmem, vmem, hbm, hbm],
        out_specs=vmem,
        scratch_shapes=[
            pltpu.VMEM((4, 768, 1024), BF16),
            pltpu.VMEM((576, 4096), BF16),
            pltpu.VMEM((576, 768), BF16),
            pltpu.VMEM((512, 768), BF16),
            pltpu.VMEM((8, 16, 16, 128), F32),
            pltpu.VMEM((4, 8, 16, 16, 128), F32),
            pltpu.VMEM((POOL, 16, 128), I16),
            pltpu.VMEM((POOL, 16, 128), I16),
            pltpu.VMEM((8, 64, 4096), BF16),
            pltpu.VMEM((2, 3, 64, 576), BF16),
            pltpu.VMEM((2, 3, 64, 576), BF16),
            pltpu.VMEM((2, 64, 576), F32),
            pltpu.VMEM((128, 128), F32),
            pltpu.VMEM((16, 16, 128), F32),
            pltpu.SemaphoreType.DMA((N_MSG,)),
            pltpu.SemaphoreType.DMA((N_MSG,)),
            pltpu.SemaphoreType.DMA((N_GATHER,)),
            pltpu.SemaphoreType.DMA((N_GATHER,)),
            pltpu.SemaphoreType.DMA((12,)),
            pltpu.SemaphoreType.DMA((12,)),
            pltpu.SemaphoreType.DMA((5,)),
        ],
        compiler_params=pltpu.CompilerParams(
            collective_id=0, has_side_effects=True, vmem_limit_bytes=56 * 1024 * 1024
        ),
        cost_estimate=pl.CostEstimate(flops=6_000_000_000, bytes_accessed=12_000_000, transcendentals=0),
    )(
        left_row, left_lam, left_count, back_pattern.reshape(9), density.T, metric,
        left_tiles.reshape(768, 4096), back_tiles,
    )


def solution(mesh):
    placed = (
        P("pair", None, None),
        P("pair"),
        P("pair"),
        P("pair"),
        P("pair", "col"),
        P(),
        P("pair", "col"),
        P("pair", "col"),
    )
    return jax.shard_map(
        per_device, mesh=mesh, in_specs=placed, out_specs=P("col", "pair"), check_vma=False
    )
```

```python
import jax
import jax.numpy as jnp
from jax import lax
from jax.experimental import pallas as pl
from jax.experimental.pallas import tpu as pltpu
from jax.sharding import PartitionSpec as P

MESH = pl.DeviceIdType.MESH
F32, BF16, I16, I32 = jnp.float32, jnp.bfloat16, jnp.int16, jnp.int32

NZ, NX, NY = 8, 4, 4
SLOTS = 12
Z_ORDER = (4, 3, 5, 2, 6, 1, 7, 0)
X_ORDER = (2, 1, 3, 0)
TOP = 32000.0
ROUND = 12582912.0
PART_A = 12
COLS_A = 1280
ROWS_A = ((0, 3), (3, 7), (7, 8))
POSITION = {0: 0, 1: 1, 2: 2, -1: 3, 4: 4, -4: 4, -3: 5, -2: 6, 3: 7}
BLOCKS = ((0, 1), (1, 3), (6, 1), (4, 2), (7, 1))
DISTANCE = (0, 1, 2, -1, 4, -3, -2, 3)
POOL = 1043
N_MSG = 35
N_GATHER = 47


def in_order(tasks):
    now, free, arrival, done, order, left = 0.0, {}, {}, set(), [], list(tasks)
    while left:
        best = None
        for task in left:
            name, needs, after, cost, rank, sends, run = task
            if all(n in arrival for n in needs) and all(t in done for t in after):
                ready = max([arrival[n] for n in needs] + [now])
                if best is None or (ready, rank) < best[:2]:
                    best = (ready, rank, task)
        ready, rank, task = best
        now = ready + task[3] + 0.08 * len(task[1])
        for key, link, hops, kib in task[5]:
            now += 0.08
            if link == "core":
                arrival[key] = now + 1.0 + kib * 0.001
                continue
            each = kib * 2 * 1.024 / 115.0
            start = max(free.get(link, 0.0), now)
            free[link] = start + each * hops
            arrival[key] = start + each + 2.3 + 0.4 * (hops - 1)
        order.append(task)
        done.add(task[0])
        left.remove(task)
    return order


def kernel(
    row_s, lam_s, count_s, pattern_s, density, metric, left_hbm, back_hbm, out_ref,
    left_v, back_v, pick, amat, stage, acc, pool_s, pool_r, applied, y_send, y_recv, mine,
    metric2, turn, msg_send, msg_recv, ag_send, ag_recv, y_ssem, y_rsem, local_sem,
):
    pair = lax.axis_index("pair")
    y = lax.axis_index("col")
    core = lax.rem(pair, 2)
    x = lax.rem(lax.div(pair, 2), NX)
    z = lax.div(pair, 2 * NX)

    def at(zz, xx, cc):
        return {"pair": (lax.rem(zz, NZ) * NX + lax.rem(xx, NX)) * 2 + cc}

    peer = at(z, x, 1 - core)
    x_right, x_left = at(z, x + 1, core), at(z, x + NX - 1, core)
    z_right, z_left = at(z + 1, x, core), at(z + NZ - 1, x, core)
    y_peers = [{"col": lax.rem(y + dy, NY)} for dy in (1, 2, 3)]

    barrier = pltpu.get_barrier_semaphore()
    far_peers = [at(z, x + 2, core), at(z + 2, x, core), at(z + NZ - 2, x, core)]
    for other in [peer, x_right, x_left, z_right, z_left] + far_peers + y_peers:
        pl.semaphore_signal(barrier, inc=1, device_id=other, device_id_type=MESH)

    loads = []
    for i, off in enumerate(X_ORDER):
        first = pl.multiple_of(lax.rem(x + off, NX) * 1024, 1024)
        load = pltpu.make_async_copy(left_hbm.at[:, pl.ds(first, 1024)], left_v.at[i], local_sem.at[i])
        load.start()
        loads.append(load)
    back_load = pltpu.make_async_copy(back_hbm, back_v, local_sem.at[4])

    j = lax.broadcasted_iota(I32, (64, 64), 0)
    half_core = jnp.where(j < 32, 1 - core, core)
    sigma = half_core * 32 + 2 * (j & 15) + ((j >> 4) & 1)
    perm = jnp.where(lax.broadcasted_iota(I32, (64, 64), 1) == sigma, 1.0, 0.0).astype(BF16)
    sorted_density = jnp.dot(perm, density[...], preferred_element_type=F32).astype(BF16)
    lane = lax.broadcasted_iota(I32, (16, SLOTS * 64), 1)
    slot_of = lane >> 6
    lam_of = jnp.zeros((16, SLOTS * 64), I32)
    row_of = jnp.zeros((16, SLOTS * 64), I32)
    for s in range(SLOTS):
        lam_of = jnp.where(slot_of == s, lam_s[s], lam_of)
        row_of = jnp.where(slot_of == s, row_s[s], row_of)
    live = slot_of < count_s[0]
    source = row_of * 64 + (lane & 63)
    deep = lax.broadcasted_iota(I32, (16, SLOTS * 64), 0)
    for b in range(36):
        pick[b * 16:(b + 1) * 16, :] = jnp.where(source == deep + b * 16, 1.0, 0.0).astype(BF16)
    turned = jnp.dot(sorted_density, pick[...], preferred_element_type=F32)
    for r, off in enumerate(Z_ORDER):
        owner = lax.rem(z + off, NZ)
        here = live & (lam_of == 2 * lax.rem(owner, 4) + lax.div(owner, 4))
        for q in range(4):
            first = (q * 8 + r) * 16
            amat[first:first + 16, :] = jnp.where(here, turned[q * 16:(q + 1) * 16, :], 0.0).astype(BF16)

    metric2[...] = jnp.zeros((128, 128), F32)
    metric2[0:64, 0:64] = metric[...]
    metric2[64:128, 64:128] = metric[...]

    links = {
        "core": peer, "x+": x_right, "x-": x_left, "x2": at(z, x + 2, core),
        "z+": z_right, "z-": z_left, "z++": at(z + 2, x, core), "z--": at(z + NZ - 2, x, core),
    }
    lanes = {"x2": ("x+", 2), "z++": ("z+", 2), "z--": ("z-", 2)}
    copies, flights, tasks = [], {}, []
    counter, gathers = [0, 0], [0]

    def task(name, needs, after, cost, rank, sends, run):
        tasks.append((name, needs, after, cost, rank, [(k,) + lanes.get(l, (l, 1)) + (n,) for k, l, n in sends], run))

    def message(key, tiles, link):
        off, number = counter
        counter[0] += tiles + 1
        counter[1] += 1
        copy = pltpu.make_async_remote_copy(
            src_ref=pool_s.at[pl.ds(off, tiles + 1)], dst_ref=pool_r.at[pl.ds(off, tiles + 1)],
            send_sem=msg_send.at[number], recv_sem=msg_recv.at[number],
            device_id=links[link], device_id_type=MESH,
        )
        flights[key] = (copy, off, tiles)
        return (key, link, 4 * (tiles + 1))

    def send(get, groups, size, key):
        copy, off, tiles = flights[key]
        assert tiles == groups * size

        def largest(g, m):
            return jnp.maximum(m, jnp.max(jnp.abs(get(g)[...]), axis=0))

        def code(g, carry):
            value = (get(g)[...] * scale + ROUND) - ROUND
            pool_s[pl.ds(off + g * size, size)] = value.astype(I16)
            return carry

        top = jnp.zeros((16, 128), F32)
        top = largest(0, top) if groups == 1 else lax.fori_loop(0, groups, largest, top)
        power = jnp.ceil(jnp.log2(jnp.maximum(top, 1e-30)))
        scale = jnp.exp2(-power) * TOP
        pool_s[off + tiles] = power.astype(I16)
        if groups == 1:
            code(0, 0)
        else:
            lax.fori_loop(0, groups, code, 0)
        copy.start()
        copies.append(copy)

    def receive(get, groups, size, key):
        copy, off, tiles = flights[key]
        assert tiles == groups * size
        copy.wait_recv()
        scale = jnp.exp2(pool_r[off + tiles].astype(F32)) * (1.0 / TOP)

        def add(g, carry):
            ref = get(g)
            ref[...] = ref[...] + pool_r[pl.ds(off + g * size, size)].astype(F32) * scale
            return carry

        if groups == 1:
            add(0, 0)
        else:
            lax.fori_loop(0, groups, add, 0)

    def rows_at(slot, row, first, size):
        return lambda g: acc.at[slot, row + g, pl.ds(first, size)]

    def left_step(i):
        loads[i].wait()

        def columns(jc, carry):
            tile = left_v[i, :, pl.ds(pl.multiple_of(jc * 512, 512), 512)]
            part = jnp.dot(amat[...], tile, preferred_element_type=F32)
            for u in range(4):
                value = part[:, u * 128:(u + 1) * 128].reshape(32, 16, 128)
                stage[:, 4 * jc + u] = value[0:8]
                stage[:, 8 + 4 * jc + u] = value[8:16]
                acc[i, :, 4 * jc + u] = value[16:24]
                acc[i, :, 8 + 4 * jc + u] = value[24:32]
            return carry

        lax.fori_loop(0, 2, columns, 0)
        if i == 0:
            pl.semaphore_wait(barrier, 11)
        if i == 1:
            back_load.start()
        send(lambda g: stage.at[g], 8, 16, ("core", i))

    for i in range(4):
        task(("left", i), [], [("left", i - 1)] if i else [], 1.4, 2,
             [message(("core", i), 128, "core")], lambda i=i: left_step(i))
        task(("sum", i), [("core", i)], [("left", i)], 0.25, 1, [],
             lambda i=i: receive(rows_at(i, 0, 0, 16), 8, 16, ("core", i)))

    na, half_a = PART_A, PART_A // 2
    for m, (first, last) in enumerate(ROWS_A):
        count = last - first

        def x_start(first=first, count=count, m=m):
            send(rows_at(0, first, 0, half_a), count, half_a, ("A", m, 0, "+"))
            send(rows_at(0, first, half_a, half_a), count, half_a, ("A", m, 0, "-"))

        def x_next(sign, first=first, count=count, m=m):
            slot, tile = (1, 0) if sign == "+" else (2, half_a)
            receive(rows_at(slot, first, tile, half_a), count, half_a, ("A", m, 0, sign))
            send(rows_at(slot, first, 0, na), count, na, ("A", m, 1, sign))

        def x_end(first=first, last=last, count=count, m=m):
            receive(rows_at(3, first, 0, na), count, na, ("A", m, 1, "+"))
            receive(rows_at(3, first, 0, na), count, na, ("A", m, 1, "-"))
            if first <= 2 < last:
                send(rows_at(3, 0, 0, half_a), 1, half_a, ("Z", 4))
                send(rows_at(3, 0, half_a, half_a), 1, half_a, ("Z", -4))
                send(rows_at(3, 1, 0, na), 1, na, ("Z", 3))
                send(rows_at(3, 2, 0, na), 1, na, ("Z", -3))
            if first <= 6 < last:
                send(rows_at(3, 5, 0, na), 1, na, ("Z", 1))
                send(rows_at(3, 6, 0, na), 1, na, ("Z", -1))

        task(("A", m, 0), [], [("sum", 0)], 0.2, 0,
             [message(("A", m, 0, "+"), half_a * count, "x+"), message(("A", m, 0, "-"), half_a * count, "x-")], x_start)
        for sign, before in (("+", 1), ("-", 2)):
            task(("A", m, 1, sign), [("A", m, 0, sign)], [("sum", before)], 0.3, 0,
                 [message(("A", m, 1, sign), na * count, "x" + sign)], lambda f=x_next, sign=sign: f(sign))
        sends = []
        if first <= 2 < last:
            sends = [message(("Z", 4), half_a, "z++"), message(("Z", -4), half_a, "z--"),
                     message(("Z", 3), na, "z+"), message(("Z", -3), na, "z-")]
        if first <= 6 < last:
            sends = sends + [message(("Z", 1), na, "z+"), message(("Z", -1), na, "z-")]
        task(("A", m, 2), [("A", m, 1, "+"), ("A", m, 1, "-")], [("sum", 3)], 0.3, 0, sends, x_end)

    relay_run = [m for m, (first, last) in enumerate(ROWS_A) if first <= 4 < last][0]
    end = len(ROWS_A) - 1

    def z_relay(sign):
        row = 3 if sign > 0 else 4
        receive(rows_at(3, row, 0, na), 1, na, ("Z", 3 * sign))
        receive(rows_at(3, row, 0 if sign > 0 else half_a, half_a), 1, half_a, ("Z", 4 * sign))
        send(rows_at(3, row, 0, na), 1, na, ("Z", 2 * sign))

    for sign in (1, -1):
        task(("Z", 2 * sign, 0), [("Z", 3 * sign), ("Z", 4 * sign)], [("A", relay_run, 2)], 0.2, 0,
             [message(("Z", 2 * sign), na, "z++" if sign > 0 else "z--")], lambda sign=sign: z_relay(sign))
    for d in (1, -1, 2, -2):
        task(("Z", d, 1), [("Z", d)], [("A", end, 2)], 0.1, 1, [],
             lambda d=d: receive(rows_at(3, 7, 0, na), 1, na, ("Z", d)))

    nb, half_b = 16 - na, (16 - na) // 2

    def parts(row, first, size):
        return lambda g: acc.at[g, row, pl.ds(na + first, size)]

    def b_start():
        for row, d in ((1, 3), (2, -3)):
            send(parts(row, 0, nb), 4, nb, ("B", d))
        send(parts(0, 0, half_b), 4, half_b, ("B", 4))
        send(parts(0, half_b, half_b), 4, half_b, ("B", -4))
        for row, d in ((5, 1), (6, -1)):
            send(parts(row, 0, nb), 4, nb, ("B", d))

    def b_relay(sign):
        row = 3 if sign > 0 else 4
        receive(parts(row, 0, nb), 4, nb, ("B", 3 * sign))
        receive(parts(row, 0 if sign > 0 else half_b, half_b), 4, half_b, ("B", 4 * sign))
        send(parts(row, 0, nb), 4, nb, ("B", 2 * sign))

    def b_cross():
        for i in range(3):
            send(rows_at(i, 7, na, nb), 1, nb, ("X", i))

    sends = [message(("B", d), 4 * n, link) for d, n, link in (
        (3, nb, "z+"), (-3, nb, "z-"), (4, half_b, "z++"), (-4, half_b, "z--"), (1, nb, "z+"), (-1, nb, "z-"))]
    task(("B", 0), [], [("sum", i) for i in range(4)], 0.6, 0, sends, b_start)
    for sign in (1, -1):
        task(("B", 2 * sign, 0), [("B", 3 * sign), ("B", 4 * sign)], [("B", 0)], 0.2, 0,
             [message(("B", 2 * sign), 4 * nb, "z++" if sign > 0 else "z--")], lambda sign=sign: b_relay(sign))
    for d in (1, -1, 2, -2):
        task(("B", d, 1), [("B", d)], [("B", 0)], 0.1, 1, [],
             lambda d=d: receive(parts(7, 0, nb), 4, nb, ("B", d)))
    ends = [("B", d, 1) for d in (1, -1, 2, -2)]
    task(("X", 0), [], ends, 0.2, 0,
         [message(("X", i), nb, link) for i, link in enumerate(("x2", "x+", "x-"))], b_cross)
    for i in range(3):
        task(("X", i, 1), [("X", i)], ends, 0.1, 1, [],
             lambda i=i: receive(rows_at(3, 7, na, nb), 1, nb, ("X", i)))
    sums = [t[0] for t in tasks]

    core_first = core * 2048

    def finish():
        rows = acc[3, 7].reshape(256, 128)
        both = jnp.dot(rows, metric2[...], precision=lax.Precision.HIGHEST, preferred_element_type=F32)
        low = lax.broadcasted_iota(I32, (16, 128), 1) < 64
        for t in range(8):
            e, o = both[t * 16:(t + 1) * 16], both[128 + t * 16:144 + t * 16]
            turn[2 * t] = jnp.where(low, e, pltpu.roll(o, 64, 1))
            turn[2 * t + 1] = jnp.where(low, pltpu.roll(e, 64, 1), o)
        for sp in range(16):
            cols = pl.ds(pl.multiple_of(core_first + sp * 128, 128), 128)
            applied[0, 0:16, cols] = turn[:, sp, :].astype(BF16)

    def share(key, link, source, target, first, size):
        number = gathers[0]
        gathers[0] += 1
        cols = pl.ds(pl.multiple_of(core_first + first, 128), size)

        def view(block, blocks, row, rows):
            return applied.at[pl.ds(block, blocks), pl.ds(16 * row, 16 * rows), cols]

        flights[key] = pltpu.make_async_remote_copy(
            src_ref=view(*source), dst_ref=view(*target), send_sem=ag_send.at[number], recv_sem=ag_recv.at[number],
            device_id=links[link], device_id_type=MESH,
        )
        return (key, link, source[1] * source[3] * size / 32)

    def gather(name, needs, after, shares, cost=0.02, rank=0, before=None):
        sends = [share(*a) for a in shares]

        def run():
            for key in needs:
                flights[key].wait_recv()
            if before is not None:
                before()
            for key, link, kib in sends:
                flights[key].start()
                copies.append(flights[key])

        task(name, needs, after, cost, rank, sends, run)

    ca, cb = COLS_A, 2048 - COLS_A
    ha, hb = ca // 2, cb // 2

    def z_move(key, link, dz, to, row, rows, first, size):
        return (key, link, (POSITION[dz], 1, row, rows), (POSITION[to], 1, row, rows), first, size)

    def x_move(key, link, b, row, to, first, size):
        return (key, link, BLOCKS[b] + (row, 1), BLOCKS[b] + (to, 1), first, size)

    def along_x(b):
        return [x_move(("gx", b, "+"), "x+", b, 0, 3, 0, ca), x_move(("gx", b, "-"), "x-", b, 0, 1, 0, ca)]

    groups = ((0, 4),)

    def along_z(g):
        row, rows = groups[g]
        return [z_move(("gz", g, -1), "z+", 0, -1, row, rows, ca, cb),
                z_move(("gz", g, 1), "z-", 0, 1, row, rows, ca, cb),
                z_move(("gz", g, -2), "z++", 0, -2, row, rows, ca, cb),
                z_move(("gz", g, 2), "z--", 0, 2, row, rows, ca, cb)]

    own = [z_move(("ga", -1), "z+", 0, -1, 0, 1, 0, ca), z_move(("ga", 1), "z-", 0, 1, 0, 1, 0, ca),
           x_move(("gb", 3), "x+", 0, 0, 3, ca, cb), x_move(("gb", 1), "x-", 0, 0, 1, ca, cb),
           z_move(("ga", -2), "z++", 0, -2, 0, 1, 0, ca), z_move(("ga", 2), "z--", 0, 2, 0, 1, 0, ca),
           x_move(("gb", 2), "x2", 0, 0, 2, ca, cb)]
    gather("own", [], sums, own + along_x(0), cost=0.6, before=finish)
    for sign, way, first in ((-1, "+", 0), (1, "-", ha)):
        gather(("ga", 2 * sign), [("ga", 2 * sign)], ["own"],
               [z_move(("ga", 3 * sign), "z" + way, 2 * sign, 3 * sign, 0, 1, 0, ca),
                z_move(("ga", 4 * sign), "z" + way + way, 2 * sign, 4, 0, 1, first, ha)])
        for d in (1, 3, 4):
            gather(("ga", d * sign), [("ga", d * sign)], ["own"], [])
    for b, (block, blocks) in enumerate(BLOCKS[1:], 1):
        held = [("ga", d) for d in DISTANCE[block:block + blocks]]
        gather(("gx", b), [], held + ([("ga", -4)] if ("ga", 4) in held else []), along_x(b), cost=0.0)
    for b in range(len(BLOCKS)):
        held = [("gx", b) if b else "own"]
        gather(("gx", b, "+"), [("gx", b, "+")], held, [x_move(("gy", b, "+"), "x+", b, 3, 2, 0, ha)])
        gather(("gx", b, "-"), [("gx", b, "-")], held, [x_move(("gy", b, "-"), "x-", b, 1, 2, ha, ha)])
        gather(("gy", b), [("gy", b, "+"), ("gy", b, "-")], [("gx", b, "+"), ("gx", b, "-")],
               [(("fa", b), "core", BLOCKS[b] + (0, 4), BLOCKS[b] + (0, 4), 0, ca)], rank=1)
    for g in (1, 2, 3):
        gather(("gb", g), [("gb", g)], ["own"], [])
    gather(("gz", 0), [], [("gb", 1), ("gb", 2), ("gb", 3), ("ga", -2), ("ga", 2)], along_z(0), cost=0.0)
    for g, (row, rows) in enumerate(groups):
        held = [("gz", 0)]
        for sign, way, first in ((-1, "+", ca), (1, "-", ca + hb)):
            gather(("gz", g, 2 * sign), [("gz", g, 2 * sign)], held,
                   [z_move(("gz", g, 3 * sign), "z" + way, 2 * sign, 3 * sign, row, rows, ca, cb),
                    z_move(("gz", g, 4 * sign), "z" + way + way, 2 * sign, 4, row, rows, first, hb)])
            for d in (1, 3, 4):
                gather(("gz", g, d * sign), [("gz", g, d * sign)], held, [])
    near = [("gz", g, d) for g in range(len(groups)) for d in (1, 2, -1)]
    far = [("gz", g, d) for g in range(len(groups)) for d in (4, -4, -3, -2, 3)]
    for b, held in enumerate((["own", ("gz", 0)], near, far)):
        whole = ((0, 1, 0, 4), (1, 3, 0, 4), (4, 4, 0, 4))[b]
        gather(("fb", b, 0), [], held, [(("fb", b), "core", whole, whole, ca, cb)], rank=1)

    block_of = lax.shift_right_logical(lax.broadcasted_iota(I32, (1, 576), 1), 6)

    def product(half, part):
        lo, hi = ((0, 256), (256, 512), (512, 576))[part]
        present = jnp.zeros((1, 576), F32)
        for b in range(9):
            present = jnp.where(block_of == b, pattern_s[b].astype(F32), present)
        if half == 0 and part == 0:
            back_load.wait()
        blocks = [4 * half + lax.rem(y + n + 1 + NZ - z, 4) for n in (0, 1, 2, 3)]
        rows = jnp.concatenate([applied[b] for b in blocks], axis=0)
        out = lax.dot_general(rows, back_v[lo:hi, :], (((1,), (1,)), ((), ())), preferred_element_type=F32)
        out = out * present[:, lo:hi]
        for n in range(3):
            y_send[half, n, :, lo:hi] = out[64 * n:64 * n + 64].astype(BF16)
        mine[half, :, lo:hi] = out[192:256]

    def y_start(half, part):
        lo, hi = ((0, 512), (512, 576), (0, 256), (256, 576))[part]
        for n in (1, 0, 2):
            number = 3 * part + n
            copy = pltpu.make_async_remote_copy(
                src_ref=y_send.at[half, n, :, pl.ds(lo, hi - lo)], dst_ref=y_recv.at[half, n, :, pl.ds(lo, hi - lo)],
                send_sem=y_ssem.at[number], recv_sem=y_rsem.at[number],
                device_id=y_peers[n], device_id_type=MESH,
            )
            flights[("y", part, n)] = copy
            copy.start()
            copies.append(copy)

    before = []
    for half in (0, 1):
        for b in range(len(BLOCKS)):
            if BLOCKS[b][0] // 4 == half:
                gather(("fa", b, 1), [("fa", b)], before + [("gy", b)], [], rank=3)
                before = [("fa", b, 1)]
        for b in ((0, 1), (2,))[half]:
            gather(("fb", b, 1), [("fb", b)], before + [("fb", b, 0)], [], rank=3)
            before = [("fb", b, 1)]
        for part in (0, 1, 2):
            task(("product", half, part), [], before, 0.65, 3, [], lambda half=half, part=part: product(half, part))
            before = [("product", half, part)]
            if (half, part) in ((0, 1), (0, 2), (1, 0), (1, 2)):
                number = ((0, 1), (0, 2), (1, 0), (1, 2)).index((half, part))
                task(("y", number), [], before, 0.3, 2, [], lambda half=half, number=number: y_start(half, number))
    assert counter == [POOL, N_MSG] and gathers == [N_GATHER]
    for one in in_order(tasks):
        one[-1]()

    k = lax.rem(y + NZ - z, 4)
    parity = lax.div(lax.rem(z + k + NZ - 4 * lax.div(k, 3), NZ), 4)
    for half in (0, 1):
        for n in range(3):
            flights[("y", 2 * half, n)].wait_recv()
            flights[("y", 2 * half + 1, n)].wait_recv()
        total = mine[half]
        for n in range(3):
            total = total + y_recv[half, n].astype(F32)
        base = (parity if half == 0 else 1 - parity) * 64
        for j in range(4):
            row = pl.multiple_of(base + lax.rem(x + j, NX) * 16, 16)
            out_ref[pl.ds(row, 16), :] = total[16 * j:16 * j + 16]
    for copy in copies:
        copy.wait_send()


def per_device(left_tiles, left_row, left_lam, left_count, density, metric, back_tiles, back_pattern):
    vmem = pl.BlockSpec(memory_space=pltpu.VMEM)
    smem = pl.BlockSpec(memory_space=pltpu.SMEM)
    hbm = pl.BlockSpec(memory_space=pl.ANY)
    return pl.pallas_call(
        kernel,
        out_shape=jax.ShapeDtypeStruct((128, 576), F32),
        in_specs=[smem, smem, smem, smem, vmem, vmem, hbm, hbm],
        out_specs=vmem,
        scratch_shapes=[
            pltpu.VMEM((4, 768, 1024), BF16),
            pltpu.VMEM((576, 4096), BF16),
            pltpu.VMEM((576, 768), BF16),
            pltpu.VMEM((512, 768), BF16),
            pltpu.VMEM((8, 16, 16, 128), F32),
            pltpu.VMEM((4, 8, 16, 16, 128), F32),
            pltpu.VMEM((POOL, 16, 128), I16),
            pltpu.VMEM((POOL, 16, 128), I16),
            pltpu.VMEM((8, 64, 4096), BF16),
            pltpu.VMEM((2, 3, 64, 576), BF16),
            pltpu.VMEM((2, 3, 64, 576), BF16),
            pltpu.VMEM((2, 64, 576), F32),
            pltpu.VMEM((128, 128), F32),
            pltpu.VMEM((16, 16, 128), F32),
            pltpu.SemaphoreType.DMA((N_MSG,)),
            pltpu.SemaphoreType.DMA((N_MSG,)),
            pltpu.SemaphoreType.DMA((N_GATHER,)),
            pltpu.SemaphoreType.DMA((N_GATHER,)),
            pltpu.SemaphoreType.DMA((12,)),
            pltpu.SemaphoreType.DMA((12,)),
            pltpu.SemaphoreType.DMA((5,)),
        ],
        compiler_params=pltpu.CompilerParams(
            collective_id=0, has_side_effects=True, vmem_limit_bytes=56 * 1024 * 1024
        ),
        cost_estimate=pl.CostEstimate(flops=6_000_000_000, bytes_accessed=12_000_000, transcendentals=0),
    )(
        left_row, left_lam, left_count, back_pattern.reshape(9), density.T, metric,
        left_tiles.reshape(768, 4096), back_tiles,
    )


def solution(mesh):
    placed = (
        P("pair", None, None),
        P("pair"),
        P("pair"),
        P("pair"),
        P("pair", "col"),
        P(),
        P("pair", "col"),
        P("pair", "col"),
    )
    return jax.shard_map(
        per_device, mesh=mesh, in_specs=placed, out_specs=P("col", "pair"), check_vma=False
    )
```

```python
import jax
import jax.numpy as jnp
from jax import lax
from jax.experimental import pallas as pl
from jax.experimental.pallas import tpu as pltpu
from jax.sharding import PartitionSpec as P

MESH = pl.DeviceIdType.MESH
F32, BF16, I16, I32 = jnp.float32, jnp.bfloat16, jnp.int16, jnp.int32

NZ, NX, NY = 8, 4, 4
SLOTS = 12
Z_ORDER = (4, 3, 5, 2, 6, 1, 7, 0)
X_ORDER = (2, 1, 3, 0)
TOP = 32000.0
ROUND = 12582912.0
PART_A = 14
COLS_A = 1280
ROWS_A = ((0, 3), (3, 7), (7, 8))
POSITION = {0: 0, 1: 1, 2: 2, -1: 3, 4: 4, -4: 4, -3: 5, -2: 6, 3: 7}
BLOCKS = ((0, 1), (1, 3), (6, 1), (4, 2), (7, 1))
DISTANCE = (0, 1, 2, -1, 4, -3, -2, 3)
POOL = 1043
N_MSG = 35
N_GATHER = 55


def in_order(tasks):
    now, free, arrival, done, order, left = 0.0, {}, {}, set(), [], list(tasks)
    while left:
        best = None
        for task in left:
            name, needs, after, cost, rank, sends, run = task
            if all(n in arrival for n in needs) and all(t in done for t in after):
                ready = max([arrival[n] for n in needs] + [now])
                if best is None or (ready, rank) < best[:2]:
                    best = (ready, rank, task)
        ready, rank, task = best
        now = ready + task[3] + 0.08 * len(task[1])
        for key, link, hops, kib in task[5]:
            now += 0.08
            if link == "core":
                arrival[key] = now + 1.0 + kib * 0.001
                continue
            each = kib * 2 * 1.024 / 115.0
            start = max(free.get(link, 0.0), now)
            free[link] = start + each * hops
            arrival[key] = start + each + 2.3 + 0.4 * (hops - 1)
        order.append(task)
        done.add(task[0])
        left.remove(task)
    return order


def kernel(
    row_s, lam_s, count_s, pattern_s, density, metric, left_hbm, back_hbm, out_ref,
    left_v, back_v, pick, amat, stage, acc, pool_s, pool_r, applied, y_send, y_recv, mine, whole,
    metric2, turn, msg_send, msg_recv, ag_send, ag_recv, y_ssem, y_rsem, local_sem,
):
    pair = lax.axis_index("pair")
    y = lax.axis_index("col")
    core = lax.rem(pair, 2)
    x = lax.rem(lax.div(pair, 2), NX)
    z = lax.div(pair, 2 * NX)

    def at(zz, xx, cc):
        return {"pair": (lax.rem(zz, NZ) * NX + lax.rem(xx, NX)) * 2 + cc}

    peer = at(z, x, 1 - core)
    x_right, x_left = at(z, x + 1, core), at(z, x + NX - 1, core)
    z_right, z_left = at(z + 1, x, core), at(z + NZ - 1, x, core)
    y_peers = [{"col": lax.rem(y + dy, NY)} for dy in (1, 2, 3)]

    barrier = pltpu.get_barrier_semaphore()
    far_peers = [at(z, x + 2, core), at(z + 2, x, core), at(z + NZ - 2, x, core)]
    for other in [peer, x_right, x_left, z_right, z_left] + far_peers + y_peers:
        pl.semaphore_signal(barrier, inc=1, device_id=other, device_id_type=MESH)

    loads = []
    for i, off in enumerate(X_ORDER):
        first = pl.multiple_of(lax.rem(x + off, NX) * 1024, 1024)
        load = pltpu.make_async_copy(left_hbm.at[:, pl.ds(first, 1024)], left_v.at[i], local_sem.at[i])
        load.start()
        loads.append(load)
    back_load = pltpu.make_async_copy(back_hbm, back_v, local_sem.at[4])

    j = lax.broadcasted_iota(I32, (64, 64), 0)
    half_core = jnp.where(j < 32, 1 - core, core)
    sigma = half_core * 32 + 2 * (j & 15) + ((j >> 4) & 1)
    perm = jnp.where(lax.broadcasted_iota(I32, (64, 64), 1) == sigma, 1.0, 0.0).astype(BF16)
    sorted_density = jnp.dot(perm, density[...], preferred_element_type=F32).astype(BF16)
    lane = lax.broadcasted_iota(I32, (16, SLOTS * 64), 1)
    slot_of = lane >> 6
    lam_of = jnp.zeros((16, SLOTS * 64), I32)
    row_of = jnp.zeros((16, SLOTS * 64), I32)
    for s in range(SLOTS):
        lam_of = jnp.where(slot_of == s, lam_s[s], lam_of)
        row_of = jnp.where(slot_of == s, row_s[s], row_of)
    live = slot_of < count_s[0]
    source = row_of * 64 + (lane & 63)
    deep = lax.broadcasted_iota(I32, (16, SLOTS * 64), 0)
    for b in range(36):
        pick[b * 16:(b + 1) * 16, :] = jnp.where(source == deep + b * 16, 1.0, 0.0).astype(BF16)
    turned = jnp.dot(sorted_density, pick[...], preferred_element_type=F32)
    for r, off in enumerate(Z_ORDER):
        owner = lax.rem(z + off, NZ)
        here = live & (lam_of == 2 * lax.rem(owner, 4) + lax.div(owner, 4))
        for q in range(4):
            first = (q * 8 + r) * 16
            amat[first:first + 16, :] = jnp.where(here, turned[q * 16:(q + 1) * 16, :], 0.0).astype(BF16)

    metric2[...] = jnp.zeros((128, 128), F32)
    metric2[0:64, 0:64] = metric[...]
    metric2[64:128, 64:128] = metric[...]

    links = {
        "core": peer, "x+": x_right, "x-": x_left, "x2": at(z, x + 2, core),
        "z+": z_right, "z-": z_left, "z++": at(z + 2, x, core), "z--": at(z + NZ - 2, x, core),
    }
    lanes = {"x2": ("x+", 2), "z++": ("z+", 2), "z--": ("z-", 2)}
    copies, flights, tasks = [], {}, []
    counter, gathers = [0, 0], [0]

    def task(name, needs, after, cost, rank, sends, run):
        tasks.append((name, needs, after, cost, rank, [(k,) + lanes.get(l, (l, 1)) + (n,) for k, l, n in sends], run))

    def message(key, tiles, link):
        off, number = counter
        counter[0] += tiles + 1
        counter[1] += 1
        copy = pltpu.make_async_remote_copy(
            src_ref=pool_s.at[pl.ds(off, tiles + 1)], dst_ref=pool_r.at[pl.ds(off, tiles + 1)],
            send_sem=msg_send.at[number], recv_sem=msg_recv.at[number],
            device_id=links[link], device_id_type=MESH,
        )
        flights[key] = (copy, off, tiles)
        return (key, link, 4 * (tiles + 1))

    def send(get, groups, size, key):
        copy, off, tiles = flights[key]
        assert tiles == groups * size

        def largest(g, m):
            return jnp.maximum(m, jnp.max(jnp.abs(get(g)[...]), axis=0))

        def code(g, carry):
            value = (get(g)[...] * scale + ROUND) - ROUND
            pool_s[pl.ds(off + g * size, size)] = value.astype(I16)
            return carry

        top = jnp.zeros((16, 128), F32)
        top = largest(0, top) if groups == 1 else lax.fori_loop(0, groups, largest, top)
        power = jnp.ceil(jnp.log2(jnp.maximum(top, 1e-30)))
        scale = jnp.exp2(-power) * TOP
        pool_s[off + tiles] = power.astype(I16)
        if groups == 1:
            code(0, 0)
        else:
            lax.fori_loop(0, groups, code, 0)
        copy.start()
        copies.append(copy)

    def receive(get, groups, size, key):
        copy, off, tiles = flights[key]
        assert tiles == groups * size
        copy.wait_recv()
        scale = jnp.exp2(pool_r[off + tiles].astype(F32)) * (1.0 / TOP)

        def add(g, carry):
            ref = get(g)
            ref[...] = ref[...] + pool_r[pl.ds(off + g * size, size)].astype(F32) * scale
            return carry

        if groups == 1:
            add(0, 0)
        else:
            lax.fori_loop(0, groups, add, 0)

    def rows_at(slot, row, first, size):
        return lambda g: acc.at[slot, row + g, pl.ds(first, size)]

    def left_step(i):
        loads[i].wait()

        def columns(jc, carry):
            tile = left_v[i, :, pl.ds(pl.multiple_of(jc * 512, 512), 512)]
            part = jnp.dot(amat[...], tile, preferred_element_type=F32)
            for u in range(4):
                value = part[:, u * 128:(u + 1) * 128].reshape(32, 16, 128)
                stage[:, 4 * jc + u] = value[0:8]
                stage[:, 8 + 4 * jc + u] = value[8:16]
                acc[i, :, 4 * jc + u] = value[16:24]
                acc[i, :, 8 + 4 * jc + u] = value[24:32]
            return carry

        lax.fori_loop(0, 2, columns, 0)
        if i == 0:
            pl.semaphore_wait(barrier, 11)
        if i == 1:
            back_load.start()
        send(lambda g: stage.at[g], 8, 16, ("core", i))

    for i in range(4):
        task(("left", i), [], [("left", i - 1)] if i else [], 1.4, 2,
             [message(("core", i), 128, "core")], lambda i=i: left_step(i))
        task(("sum", i), [("core", i)], [("left", i)], 0.25, 1, [],
             lambda i=i: receive(rows_at(i, 0, 0, 16), 8, 16, ("core", i)))

    na, half_a = PART_A, PART_A // 2
    for m, (first, last) in enumerate(ROWS_A):
        count = last - first

        def x_start(first=first, count=count, m=m):
            send(rows_at(0, first, 0, half_a), count, half_a, ("A", m, 0, "+"))
            send(rows_at(0, first, half_a, half_a), count, half_a, ("A", m, 0, "-"))

        def x_next(sign, first=first, count=count, m=m):
            slot, tile = (1, 0) if sign == "+" else (2, half_a)
            receive(rows_at(slot, first, tile, half_a), count, half_a, ("A", m, 0, sign))
            send(rows_at(slot, first, 0, na), count, na, ("A", m, 1, sign))

        def x_end(first=first, last=last, count=count, m=m):
            receive(rows_at(3, first, 0, na), count, na, ("A", m, 1, "+"))
            receive(rows_at(3, first, 0, na), count, na, ("A", m, 1, "-"))
            if first <= 2 < last:
                send(rows_at(3, 0, 0, half_a), 1, half_a, ("Z", 4))
                send(rows_at(3, 0, half_a, half_a), 1, half_a, ("Z", -4))
                send(rows_at(3, 1, 0, na), 1, na, ("Z", 3))
                send(rows_at(3, 2, 0, na), 1, na, ("Z", -3))
            if first <= 6 < last:
                send(rows_at(3, 5, 0, na), 1, na, ("Z", 1))
                send(rows_at(3, 6, 0, na), 1, na, ("Z", -1))

        task(("A", m, 0), [], [("sum", 0)], 0.2, 0,
             [message(("A", m, 0, "+"), half_a * count, "x+"), message(("A", m, 0, "-"), half_a * count, "x-")], x_start)
        for sign, before in (("+", 1), ("-", 2)):
            task(("A", m, 1, sign), [("A", m, 0, sign)], [("sum", before)], 0.3, 0,
                 [message(("A", m, 1, sign), na * count, "x" + sign)], lambda f=x_next, sign=sign: f(sign))
        sends = []
        if first <= 2 < last:
            sends = [message(("Z", 4), half_a, "z++"), message(("Z", -4), half_a, "z--"),
                     message(("Z", 3), na, "z+"), message(("Z", -3), na, "z-")]
        if first <= 6 < last:
            sends = sends + [message(("Z", 1), na, "z+"), message(("Z", -1), na, "z-")]
        task(("A", m, 2), [("A", m, 1, "+"), ("A", m, 1, "-")], [("sum", 3)], 0.3, 0, sends, x_end)

    relay_run = [m for m, (first, last) in enumerate(ROWS_A) if first <= 4 < last][0]
    end = len(ROWS_A) - 1

    def z_relay(sign):
        row = 3 if sign > 0 else 4
        receive(rows_at(3, row, 0, na), 1, na, ("Z", 3 * sign))
        receive(rows_at(3, row, 0 if sign > 0 else half_a, half_a), 1, half_a, ("Z", 4 * sign))
        send(rows_at(3, row, 0, na), 1, na, ("Z", 2 * sign))

    for sign in (1, -1):
        task(("Z", 2 * sign, 0), [("Z", 3 * sign), ("Z", 4 * sign)], [("A", relay_run, 2)], 0.2, 0,
             [message(("Z", 2 * sign), na, "z++" if sign > 0 else "z--")], lambda sign=sign: z_relay(sign))
    for d in (1, -1, 2, -2):
        task(("Z", d, 1), [("Z", d)], [("A", end, 2)], 0.1, 1, [],
             lambda d=d: receive(rows_at(3, 7, 0, na), 1, na, ("Z", d)))

    nb, half_b = 16 - na, (16 - na) // 2

    def parts(row, first, size):
        return lambda g: acc.at[g, row, pl.ds(na + first, size)]

    def b_start():
        for row, d in ((1, 3), (2, -3)):
            send(parts(row, 0, nb), 4, nb, ("B", d))
        send(parts(0, 0, half_b), 4, half_b, ("B", 4))
        send(parts(0, half_b, half_b), 4, half_b, ("B", -4))
        for row, d in ((5, 1), (6, -1)):
            send(parts(row, 0, nb), 4, nb, ("B", d))

    def b_relay(sign):
        row = 3 if sign > 0 else 4
        receive(parts(row, 0, nb), 4, nb, ("B", 3 * sign))
        receive(parts(row, 0 if sign > 0 else half_b, half_b), 4, half_b, ("B", 4 * sign))
        send(parts(row, 0, nb), 4, nb, ("B", 2 * sign))

    def b_cross():
        for i in range(3):
            send(rows_at(i, 7, na, nb), 1, nb, ("X", i))

    sends = [message(("B", d), 4 * n, link) for d, n, link in (
        (3, nb, "z+"), (-3, nb, "z-"), (4, half_b, "z++"), (-4, half_b, "z--"), (1, nb, "z+"), (-1, nb, "z-"))]
    task(("B", 0), [], [("sum", i) for i in range(4)], 0.6, 0, sends, b_start)
    for sign in (1, -1):
        task(("B", 2 * sign, 0), [("B", 3 * sign), ("B", 4 * sign)], [("B", 0)], 0.2, 0,
             [message(("B", 2 * sign), 4 * nb, "z++" if sign > 0 else "z--")], lambda sign=sign: b_relay(sign))
    for d in (1, -1, 2, -2):
        task(("B", d, 1), [("B", d)], [("B", 0)], 0.1, 1, [],
             lambda d=d: receive(parts(7, 0, nb), 4, nb, ("B", d)))
    ends = [("B", d, 1) for d in (1, -1, 2, -2)]
    task(("X", 0), [], ends, 0.2, 0,
         [message(("X", i), nb, link) for i, link in enumerate(("x2", "x+", "x-"))], b_cross)
    for i in range(3):
        task(("X", i, 1), [("X", i)], ends, 0.1, 1, [],
             lambda i=i: receive(rows_at(3, 7, na, nb), 1, nb, ("X", i)))
    sums = [t[0] for t in tasks]

    core_first = core * 2048

    def finish():
        rows = acc[3, 7].reshape(256, 128)
        both = jnp.dot(rows, metric2[...], precision=lax.Precision.HIGHEST, preferred_element_type=F32)
        low = lax.broadcasted_iota(I32, (16, 128), 1) < 64
        for t in range(8):
            e, o = both[t * 16:(t + 1) * 16], both[128 + t * 16:144 + t * 16]
            turn[2 * t] = jnp.where(low, e, pltpu.roll(o, 64, 1))
            turn[2 * t + 1] = jnp.where(low, pltpu.roll(e, 64, 1), o)
        for sp in range(16):
            cols = pl.ds(pl.multiple_of(core_first + sp * 128, 128), 128)
            applied[0, 0:16, cols] = turn[:, sp, :].astype(BF16)

    def share(key, link, source, target, first, size):
        number = gathers[0]
        gathers[0] += 1
        cols = pl.ds(pl.multiple_of(core_first + first, 128), size)

        def view(block, blocks, row, rows):
            return applied.at[pl.ds(block, blocks), pl.ds(16 * row, 16 * rows), cols]

        flights[key] = pltpu.make_async_remote_copy(
            src_ref=view(*source), dst_ref=view(*target), send_sem=ag_send.at[number], recv_sem=ag_recv.at[number],
            device_id=links[link], device_id_type=MESH,
        )
        return (key, link, source[1] * source[3] * size / 32)

    def gather(name, needs, after, shares, cost=0.02, rank=0, before=None):
        sends = [share(*a) for a in shares]

        def run():
            for key in needs:
                flights[key].wait_recv()
            if before is not None:
                before()
            for key, link, kib in sends:
                flights[key].start()
                copies.append(flights[key])

        task(name, needs, after, cost, rank, sends, run)

    ca, cb = COLS_A, 2048 - COLS_A
    ha, hb = ca // 2, cb // 2

    def z_move(key, link, dz, to, row, rows, first, size):
        return (key, link, (POSITION[dz], 1, row, rows), (POSITION[to], 1, row, rows), first, size)

    def x_move(key, link, b, row, to, first, size):
        return (key, link, BLOCKS[b] + (row, 1), BLOCKS[b] + (to, 1), first, size)

    def along_x(b):
        return [x_move(("gx", b, "+"), "x+", b, 0, 3, 0, ca), x_move(("gx", b, "-"), "x-", b, 0, 1, 0, ca)]

    groups = ((0, 1), (1, 3))

    def along_z(g):
        row, rows = groups[g]
        return [z_move(("gz", g, -1), "z+", 0, -1, row, rows, ca, cb),
                z_move(("gz", g, 1), "z-", 0, 1, row, rows, ca, cb),
                z_move(("gz", g, -2), "z++", 0, -2, row, rows, ca, cb),
                z_move(("gz", g, 2), "z--", 0, 2, row, rows, ca, cb)]

    own = [z_move(("ga", -1), "z+", 0, -1, 0, 1, 0, ca), z_move(("ga", 1), "z-", 0, 1, 0, 1, 0, ca),
           x_move(("gb", 3), "x+", 0, 0, 3, ca, cb), x_move(("gb", 1), "x-", 0, 0, 1, ca, cb),
           z_move(("ga", -2), "z++", 0, -2, 0, 1, 0, ca), z_move(("ga", 2), "z--", 0, 2, 0, 1, 0, ca),
           x_move(("gb", 2), "x2", 0, 0, 2, ca, cb)]
    gather("own", [], sums, own + along_x(0) + along_z(0), cost=0.6, before=finish)
    for sign, way, first in ((-1, "+", 0), (1, "-", ha)):
        gather(("ga", 2 * sign), [("ga", 2 * sign)], ["own"],
               [z_move(("ga", 3 * sign), "z" + way, 2 * sign, 3 * sign, 0, 1, 0, ca),
                z_move(("ga", 4 * sign), "z" + way + way, 2 * sign, 4, 0, 1, first, ha)])
        for d in (1, 3, 4):
            gather(("ga", d * sign), [("ga", d * sign)], ["own"], [])
    for b, (block, blocks) in enumerate(BLOCKS[1:], 1):
        held = [("ga", d) for d in DISTANCE[block:block + blocks]]
        gather(("gx", b), [], held + ([("ga", -4)] if ("ga", 4) in held else []), along_x(b), cost=0.0)
    for b in range(len(BLOCKS)):
        held = [("gx", b) if b else "own"]
        gather(("gx", b, "+"), [("gx", b, "+")], held, [x_move(("gy", b, "+"), "x+", b, 3, 2, 0, ha)])
        gather(("gx", b, "-"), [("gx", b, "-")], held, [x_move(("gy", b, "-"), "x-", b, 1, 2, ha, ha)])
        gather(("gy", b), [("gy", b, "+"), ("gy", b, "-")], [("gx", b, "+"), ("gx", b, "-")],
               [(("fa", b), "core", BLOCKS[b] + (0, 4), BLOCKS[b] + (0, 4), 0, ca)], rank=1)
    for g in (1, 2, 3):
        gather(("gb", g), [("gb", g)], ["own"], [])
    gather(("gz", 1), [], [("gb", 1), ("gb", 2), ("gb", 3), ("ga", -2), ("ga", 2)], along_z(1), cost=0.0)
    for g, (row, rows) in enumerate(groups):
        held = [("gz", 1) if g else "own"]
        for sign, way, first in ((-1, "+", ca), (1, "-", ca + hb)):
            gather(("gz", g, 2 * sign), [("gz", g, 2 * sign)], held,
                   [z_move(("gz", g, 3 * sign), "z" + way, 2 * sign, 3 * sign, row, rows, ca, cb),
                    z_move(("gz", g, 4 * sign), "z" + way + way, 2 * sign, 4, row, rows, first, hb)])
            for d in (1, 3, 4):
                gather(("gz", g, d * sign), [("gz", g, d * sign)], held, [])
    near = [("gz", g, d) for g in (0, 1) for d in (1, 2, -1)]
    far = [("gz", g, d) for g in (0, 1) for d in (4, -4, -3, -2, 3)]
    for b, held in enumerate((["own", ("gz", 1)], near, far)):
        region = ((0, 1, 0, 4), (1, 3, 0, 4), (4, 4, 0, 4))[b]
        gather(("fb", b, 0), [], held, [(("fb", b), "core", region, region, ca, cb)], rank=1)

    block_of = lax.shift_right_logical(lax.broadcasted_iota(I32, (1, 576), 1), 6)

    def product(half, part):
        lo, hi = ((0, 256), (256, 512), (512, 576))[part]
        present = jnp.zeros((1, 576), F32)
        for b in range(9):
            present = jnp.where(block_of == b, pattern_s[b].astype(F32), present)
        if half == 0 and part == 0:
            back_load.wait()
        blocks = [4 * half + lax.rem(y + n + 1 + NZ - z, 4) for n in (0, 1, 2, 3)]
        rows = jnp.concatenate([applied[b] for b in blocks], axis=0)
        out = lax.dot_general(rows, back_v[lo:hi, :], (((1,), (1,)), ((), ())), preferred_element_type=F32)
        out = out * present[:, lo:hi]
        for n in range(3):
            y_send[half, n, :, lo:hi] = out[64 * n:64 * n + 64].astype(BF16)
        mine[half, :, lo:hi] = out[192:256]

    def y_start(half, part):
        lo, hi = ((0, 512), (512, 576), (0, 256), (256, 576))[part]
        for n in (1, 0, 2):
            number = 3 * part + n
            copy = pltpu.make_async_remote_copy(
                src_ref=y_send.at[half, n, :, pl.ds(lo, hi - lo)], dst_ref=y_recv.at[half, n, :, pl.ds(lo, hi - lo)],
                send_sem=y_ssem.at[number], recv_sem=y_rsem.at[number],
                device_id=y_peers[n], device_id_type=MESH,
            )
            flights[("y", part, n)] = copy
            copy.start()
            copies.append(copy)

    before = []
    for half in (0, 1):
        for b in range(len(BLOCKS)):
            if BLOCKS[b][0] // 4 == half:
                gather(("fa", b, 1), [("fa", b)], before + [("gy", b)], [], rank=3)
                before = [("fa", b, 1)]
        for b in ((0, 1), (2,))[half]:
            gather(("fb", b, 1), [("fb", b)], before + [("fb", b, 0)], [], rank=3)
            before = [("fb", b, 1)]
        for part in (0, 1, 2):
            task(("product", half, part), [], before, 0.65, 3, [], lambda half=half, part=part: product(half, part))
            before = [("product", half, part)]
            if (half, part) in ((0, 1), (0, 2), (1, 0), (1, 2)):
                number = ((0, 1), (0, 2), (1, 0), (1, 2)).index((half, part))
                task(("y", number), [], before, 0.3, 2, [], lambda half=half, number=number: y_start(half, number))
    assert counter == [POOL, N_MSG] and gathers == [N_GATHER]
    for one in in_order(tasks):
        one[-1]()

    last = [flights[("y", part, n)] for part in (2, 3) for n in range(3)]
    for copy in copies:
        if not any(copy is other for other in last):
            copy.wait_send()
    k = lax.rem(y + NZ - z, 4)
    parity = lax.div(lax.rem(z + k + NZ - 4 * lax.div(k, 3), NZ), 4)
    for half in (0, 1):
        for n in range(3):
            flights[("y", 2 * half, n)].wait_recv()
            flights[("y", 2 * half + 1, n)].wait_recv()
        total = mine[half]
        for n in range(3):
            total = total + y_recv[half, n].astype(F32)
        base = (parity if half == 0 else 1 - parity) * 64
        for j in range(4):
            row = pl.multiple_of(base + lax.rem(x + j, NX) * 16, 16)
            whole[pl.ds(row, 16), :] = total[16 * j:16 * j + 16]
    out_ref[...] = whole[...].T
    for copy in last:
        copy.wait_send()


def per_device(left_tiles, left_row, left_lam, left_count, density, metric, back_tiles, back_pattern):
    vmem = pl.BlockSpec(memory_space=pltpu.VMEM)
    smem = pl.BlockSpec(memory_space=pltpu.SMEM)
    hbm = pl.BlockSpec(memory_space=pl.ANY)
    return pl.pallas_call(
        kernel,
        out_shape=jax.ShapeDtypeStruct((576, 128), F32),
        in_specs=[smem, smem, smem, smem, vmem, vmem, hbm, hbm],
        out_specs=vmem,
        scratch_shapes=[
            pltpu.VMEM((4, 768, 1024), BF16),
            pltpu.VMEM((576, 4096), BF16),
            pltpu.VMEM((576, 768), BF16),
            pltpu.VMEM((512, 768), BF16),
            pltpu.VMEM((8, 16, 16, 128), F32),
            pltpu.VMEM((4, 8, 16, 16, 128), F32),
            pltpu.VMEM((POOL, 16, 128), I16),
            pltpu.VMEM((POOL, 16, 128), I16),
            pltpu.VMEM((8, 64, 4096), BF16),
            pltpu.VMEM((2, 3, 64, 576), BF16),
            pltpu.VMEM((2, 3, 64, 576), BF16),
            pltpu.VMEM((2, 64, 576), F32),
            pltpu.VMEM((128, 576), F32),
            pltpu.VMEM((128, 128), F32),
            pltpu.VMEM((16, 16, 128), F32),
            pltpu.SemaphoreType.DMA((N_MSG,)),
            pltpu.SemaphoreType.DMA((N_MSG,)),
            pltpu.SemaphoreType.DMA((N_GATHER,)),
            pltpu.SemaphoreType.DMA((N_GATHER,)),
            pltpu.SemaphoreType.DMA((12,)),
            pltpu.SemaphoreType.DMA((12,)),
            pltpu.SemaphoreType.DMA((5,)),
        ],
        compiler_params=pltpu.CompilerParams(
            collective_id=0, has_side_effects=True, vmem_limit_bytes=56 * 1024 * 1024
        ),
        cost_estimate=pl.CostEstimate(flops=6_000_000_000, bytes_accessed=12_000_000, transcendentals=0),
    )(
        left_row, left_lam, left_count, back_pattern.reshape(9), density.T, metric,
        left_tiles.reshape(768, 4096), back_tiles,
    ).T


def solution(mesh):
    placed = (
        P("pair", None, None),
        P("pair"),
        P("pair"),
        P("pair"),
        P("pair", "col"),
        P(),
        P("pair", "col"),
        P("pair", "col"),
    )
    return jax.shard_map(
        per_device, mesh=mesh, in_specs=placed, out_specs=P("col", "pair"), check_vma=False
    )
```

```python
import jax
import jax.numpy as jnp
from jax import lax
from jax.experimental import pallas as pl
from jax.experimental.pallas import tpu as pltpu
from jax.sharding import PartitionSpec as P

MESH = pl.DeviceIdType.MESH
F32, BF16, I16, I32 = jnp.float32, jnp.bfloat16, jnp.int16, jnp.int32

NZ, NX, NY = 8, 4, 4
SLOTS = 12
Z_ORDER = (4, 3, 5, 2, 6, 1, 7, 0)
X_ORDER = (2, 1, 3, 0)
TOP = 32000.0
ROUND = 12582912.0
PART_A = 14
COLS_A = 1280
ROWS_A = ((0, 3), (3, 7), (7, 8))
POSITION = {0: 0, 1: 1, 2: 2, -1: 3, 4: 4, -4: 4, -3: 5, -2: 6, 3: 7}
BLOCKS = ((0, 1), (1, 3), (6, 1), (4, 2), (7, 1))
DISTANCE = (0, 1, 2, -1, 4, -3, -2, 3)
POOL = 1043
N_MSG = 35
N_GATHER = 55


def in_order(tasks):
    now, free, arrival, done, order, left = 0.0, {}, {}, set(), [], list(tasks)
    while left:
        best = None
        for task in left:
            name, needs, after, cost, rank, sends, run = task
            if all(n in arrival for n in needs) and all(t in done for t in after):
                ready = max([arrival[n] for n in needs] + [now])
                if best is None or (ready, rank) < best[:2]:
                    best = (ready, rank, task)
        ready, rank, task = best
        now = ready + task[3] + 0.08 * len(task[1])
        for key, link, hops, kib in task[5]:
            now += 0.08
            if link == "core":
                arrival[key] = now + 1.0 + kib * 0.001
                continue
            each = kib * 2 * 1.024 / 115.0
            start = max(free.get(link, 0.0), now)
            free[link] = start + each * hops
            arrival[key] = start + each + 2.3 + 0.4 * (hops - 1)
        order.append(task)
        done.add(task[0])
        left.remove(task)
    return order


def kernel(
    row_s, lam_s, count_s, pattern_s, density, metric, left_hbm, back_hbm, out_ref,
    left_v, back_v, pick, amat, stage, acc, pool_s, pool_r, applied, y_send, y_recv, mine, whole, early,
    metric2, turn, msg_send, msg_recv, ag_send, ag_recv, y_ssem, y_rsem, local_sem,
):
    pair = lax.axis_index("pair")
    y = lax.axis_index("col")
    core = lax.rem(pair, 2)
    x = lax.rem(lax.div(pair, 2), NX)
    z = lax.div(pair, 2 * NX)

    def at(zz, xx, cc):
        return {"pair": (lax.rem(zz, NZ) * NX + lax.rem(xx, NX)) * 2 + cc}

    peer = at(z, x, 1 - core)
    x_right, x_left = at(z, x + 1, core), at(z, x + NX - 1, core)
    z_right, z_left = at(z + 1, x, core), at(z + NZ - 1, x, core)
    y_peers = [{"col": lax.rem(y + dy, NY)} for dy in (1, 2, 3)]

    barrier = pltpu.get_barrier_semaphore()
    far_peers = [at(z, x + 2, core), at(z + 2, x, core), at(z + NZ - 2, x, core)]
    for other in [peer, x_right, x_left, z_right, z_left] + far_peers + y_peers:
        pl.semaphore_signal(barrier, inc=1, device_id=other, device_id_type=MESH)

    loads = []
    for i, off in enumerate(X_ORDER):
        first = pl.multiple_of(lax.rem(x + off, NX) * 1024, 1024)
        load = pltpu.make_async_copy(left_hbm.at[:, pl.ds(first, 1024)], left_v.at[i], local_sem.at[i])
        load.start()
        loads.append(load)
    back_load = pltpu.make_async_copy(back_hbm, back_v, local_sem.at[4])

    j = lax.broadcasted_iota(I32, (64, 64), 0)
    half_core = jnp.where(j < 32, 1 - core, core)
    sigma = half_core * 32 + 2 * (j & 15) + ((j >> 4) & 1)
    perm = jnp.where(lax.broadcasted_iota(I32, (64, 64), 1) == sigma, 1.0, 0.0).astype(BF16)
    sorted_density = jnp.dot(perm, density[...], preferred_element_type=F32).astype(BF16)
    lane = lax.broadcasted_iota(I32, (16, SLOTS * 64), 1)
    slot_of = lane >> 6
    lam_of = jnp.zeros((16, SLOTS * 64), I32)
    row_of = jnp.zeros((16, SLOTS * 64), I32)
    for s in range(SLOTS):
        lam_of = jnp.where(slot_of == s, lam_s[s], lam_of)
        row_of = jnp.where(slot_of == s, row_s[s], row_of)
    live = slot_of < count_s[0]
    source = row_of * 64 + (lane & 63)
    deep = lax.broadcasted_iota(I32, (16, SLOTS * 64), 0)
    for b in range(36):
        pick[b * 16:(b + 1) * 16, :] = jnp.where(source == deep + b * 16, 1.0, 0.0).astype(BF16)
    turned = jnp.dot(sorted_density, pick[...], preferred_element_type=F32)
    for r, off in enumerate(Z_ORDER):
        owner = lax.rem(z + off, NZ)
        here = live & (lam_of == 2 * lax.rem(owner, 4) + lax.div(owner, 4))
        for q in range(4):
            first = (q * 8 + r) * 16
            amat[first:first + 16, :] = jnp.where(here, turned[q * 16:(q + 1) * 16, :], 0.0).astype(BF16)

    metric2[...] = jnp.zeros((128, 128), F32)
    metric2[0:64, 0:64] = metric[...]
    metric2[64:128, 64:128] = metric[...]

    links = {
        "core": peer, "x+": x_right, "x-": x_left, "x2": at(z, x + 2, core),
        "z+": z_right, "z-": z_left, "z++": at(z + 2, x, core), "z--": at(z + NZ - 2, x, core),
    }
    lanes = {"x2": ("x+", 2), "z++": ("z+", 2), "z--": ("z-", 2)}
    copies, flights, tasks = [], {}, []
    counter, gathers = [0, 0], [0]

    def task(name, needs, after, cost, rank, sends, run):
        tasks.append((name, needs, after, cost, rank, [(k,) + lanes.get(l, (l, 1)) + (n,) for k, l, n in sends], run))

    def message(key, tiles, link):
        off, number = counter
        counter[0] += tiles + 1
        counter[1] += 1
        copy = pltpu.make_async_remote_copy(
            src_ref=pool_s.at[pl.ds(off, tiles + 1)], dst_ref=pool_r.at[pl.ds(off, tiles + 1)],
            send_sem=msg_send.at[number], recv_sem=msg_recv.at[number],
            device_id=links[link], device_id_type=MESH,
        )
        flights[key] = (copy, off, tiles)
        return (key, link, 4 * (tiles + 1))

    def send(get, groups, size, key):
        copy, off, tiles = flights[key]
        assert tiles == groups * size

        def largest(g, m):
            return jnp.maximum(m, jnp.max(jnp.abs(get(g)[...]), axis=0))

        def code(g, carry):
            value = (get(g)[...] * scale + ROUND) - ROUND
            pool_s[pl.ds(off + g * size, size)] = value.astype(I16)
            return carry

        top = jnp.zeros((16, 128), F32)
        top = largest(0, top) if groups == 1 else lax.fori_loop(0, groups, largest, top)
        power = jnp.ceil(jnp.log2(jnp.maximum(top, 1e-30)))
        scale = jnp.exp2(-power) * TOP
        pool_s[off + tiles] = power.astype(I16)
        if groups == 1:
            code(0, 0)
        else:
            lax.fori_loop(0, groups, code, 0)
        copy.start()
        copies.append(copy)

    def receive(get, groups, size, key):
        copy, off, tiles = flights[key]
        assert tiles == groups * size
        copy.wait_recv()
        scale = jnp.exp2(pool_r[off + tiles].astype(F32)) * (1.0 / TOP)

        def add(g, carry):
            ref = get(g)
            ref[...] = ref[...] + pool_r[pl.ds(off + g * size, size)].astype(F32) * scale
            return carry

        if groups == 1:
            add(0, 0)
        else:
            lax.fori_loop(0, groups, add, 0)

    def rows_at(slot, row, first, size):
        return lambda g: acc.at[slot, row + g, pl.ds(first, size)]

    def left_step(i):
        loads[i].wait()

        def columns(jc, carry):
            tile = left_v[i, :, pl.ds(pl.multiple_of(jc * 512, 512), 512)]
            part = jnp.dot(amat[...], tile, preferred_element_type=F32)
            for u in range(4):
                value = part[:, u * 128:(u + 1) * 128].reshape(32, 16, 128)
                stage[:, 4 * jc + u] = value[0:8]
                stage[:, 8 + 4 * jc + u] = value[8:16]
                acc[i, :, 4 * jc + u] = value[16:24]
                acc[i, :, 8 + 4 * jc + u] = value[24:32]
            return carry

        lax.fori_loop(0, 2, columns, 0)
        if i == 0:
            pl.semaphore_wait(barrier, 11)
        if i == 1:
            back_load.start()
        send(lambda g: stage.at[g], 8, 16, ("core", i))

    for i in range(4):
        task(("left", i), [], [("left", i - 1)] if i else [], 1.4, 2,
             [message(("core", i), 128, "core")], lambda i=i: left_step(i))
        task(("sum", i), [("core", i)], [("left", i)], 0.25, 1, [],
             lambda i=i: receive(rows_at(i, 0, 0, 16), 8, 16, ("core", i)))

    na, half_a = PART_A, PART_A // 2
    for m, (first, last) in enumerate(ROWS_A):
        count = last - first

        def x_start(first=first, count=count, m=m):
            send(rows_at(0, first, 0, half_a), count, half_a, ("A", m, 0, "+"))
            send(rows_at(0, first, half_a, half_a), count, half_a, ("A", m, 0, "-"))

        def x_next(sign, first=first, count=count, m=m):
            slot, tile = (1, 0) if sign == "+" else (2, half_a)
            receive(rows_at(slot, first, tile, half_a), count, half_a, ("A", m, 0, sign))
            send(rows_at(slot, first, 0, na), count, na, ("A", m, 1, sign))

        def x_end(first=first, last=last, count=count, m=m):
            receive(rows_at(3, first, 0, na), count, na, ("A", m, 1, "+"))
            receive(rows_at(3, first, 0, na), count, na, ("A", m, 1, "-"))
            if first <= 2 < last:
                send(rows_at(3, 0, 0, half_a), 1, half_a, ("Z", 4))
                send(rows_at(3, 0, half_a, half_a), 1, half_a, ("Z", -4))
                send(rows_at(3, 1, 0, na), 1, na, ("Z", 3))
                send(rows_at(3, 2, 0, na), 1, na, ("Z", -3))
            if first <= 6 < last:
                send(rows_at(3, 5, 0, na), 1, na, ("Z", 1))
                send(rows_at(3, 6, 0, na), 1, na, ("Z", -1))

        task(("A", m, 0), [], [("sum", 0)], 0.2, 0,
             [message(("A", m, 0, "+"), half_a * count, "x+"), message(("A", m, 0, "-"), half_a * count, "x-")], x_start)
        for sign, before in (("+", 1), ("-", 2)):
            task(("A", m, 1, sign), [("A", m, 0, sign)], [("sum", before)], 0.3, 0,
                 [message(("A", m, 1, sign), na * count, "x" + sign)], lambda f=x_next, sign=sign: f(sign))
        sends = []
        if first <= 2 < last:
            sends = [message(("Z", 4), half_a, "z++"), message(("Z", -4), half_a, "z--"),
                     message(("Z", 3), na, "z+"), message(("Z", -3), na, "z-")]
        if first <= 6 < last:
            sends = sends + [message(("Z", 1), na, "z+"), message(("Z", -1), na, "z-")]
        task(("A", m, 2), [("A", m, 1, "+"), ("A", m, 1, "-")], [("sum", 3)], 0.3, 0, sends, x_end)

    relay_run = [m for m, (first, last) in enumerate(ROWS_A) if first <= 4 < last][0]
    end = len(ROWS_A) - 1

    def z_relay(sign):
        row = 3 if sign > 0 else 4
        receive(rows_at(3, row, 0, na), 1, na, ("Z", 3 * sign))
        receive(rows_at(3, row, 0 if sign > 0 else half_a, half_a), 1, half_a, ("Z", 4 * sign))
        send(rows_at(3, row, 0, na), 1, na, ("Z", 2 * sign))

    for sign in (1, -1):
        task(("Z", 2 * sign, 0), [("Z", 3 * sign), ("Z", 4 * sign)], [("A", relay_run, 2)], 0.2, 0,
             [message(("Z", 2 * sign), na, "z++" if sign > 0 else "z--")], lambda sign=sign: z_relay(sign))
    for d in (1, -1, 2, -2):
        task(("Z", d, 1), [("Z", d)], [("A", end, 2)], 0.1, 1, [],
             lambda d=d: receive(rows_at(3, 7, 0, na), 1, na, ("Z", d)))

    nb, half_b = 16 - na, (16 - na) // 2

    def parts(row, first, size):
        return lambda g: acc.at[g, row, pl.ds(na + first, size)]

    def b_start():
        for row, d in ((1, 3), (2, -3)):
            send(parts(row, 0, nb), 4, nb, ("B", d))
        send(parts(0, 0, half_b), 4, half_b, ("B", 4))
        send(parts(0, half_b, half_b), 4, half_b, ("B", -4))
        for row, d in ((5, 1), (6, -1)):
            send(parts(row, 0, nb), 4, nb, ("B", d))

    def b_relay(sign):
        row = 3 if sign > 0 else 4
        receive(parts(row, 0, nb), 4, nb, ("B", 3 * sign))
        receive(parts(row, 0 if sign > 0 else half_b, half_b), 4, half_b, ("B", 4 * sign))
        send(parts(row, 0, nb), 4, nb, ("B", 2 * sign))

    def b_cross():
        for i in range(3):
            send(rows_at(i, 7, na, nb), 1, nb, ("X", i))

    sends = [message(("B", d), 4 * n, link) for d, n, link in (
        (3, nb, "z+"), (-3, nb, "z-"), (4, half_b, "z++"), (-4, half_b, "z--"), (1, nb, "z+"), (-1, nb, "z-"))]
    task(("B", 0), [], [("sum", i) for i in range(4)], 0.6, 0, sends, b_start)
    for sign in (1, -1):
        task(("B", 2 * sign, 0), [("B", 3 * sign), ("B", 4 * sign)], [("B", 0)], 0.2, 0,
             [message(("B", 2 * sign), 4 * nb, "z++" if sign > 0 else "z--")], lambda sign=sign: b_relay(sign))
    for d in (1, -1, 2, -2):
        task(("B", d, 1), [("B", d)], [("B", 0)], 0.1, 1, [],
             lambda d=d: receive(parts(7, 0, nb), 4, nb, ("B", d)))
    ends = [("B", d, 1) for d in (1, -1, 2, -2)]
    task(("X", 0), [], ends, 0.2, 0,
         [message(("X", i), nb, link) for i, link in enumerate(("x2", "x+", "x-"))], b_cross)
    for i in range(3):
        task(("X", i, 1), [("X", i)], ends, 0.1, 1, [],
             lambda i=i: receive(rows_at(3, 7, na, nb), 1, nb, ("X", i)))
    sums = [t[0] for t in tasks]

    core_first = core * 2048

    def finish():
        rows = acc[3, 7].reshape(256, 128)
        both = jnp.dot(rows, metric2[...], precision=lax.Precision.HIGHEST, preferred_element_type=F32)
        low = lax.broadcasted_iota(I32, (16, 128), 1) < 64
        for t in range(8):
            e, o = both[t * 16:(t + 1) * 16], both[128 + t * 16:144 + t * 16]
            turn[2 * t] = jnp.where(low, e, pltpu.roll(o, 64, 1))
            turn[2 * t + 1] = jnp.where(low, pltpu.roll(e, 64, 1), o)
        for sp in range(16):
            cols = pl.ds(pl.multiple_of(core_first + sp * 128, 128), 128)
            applied[0, 0:16, cols] = turn[:, sp, :].astype(BF16)

    def share(key, link, source, target, first, size):
        number = gathers[0]
        gathers[0] += 1
        cols = pl.ds(pl.multiple_of(core_first + first, 128), size)

        def view(block, blocks, row, rows):
            return applied.at[pl.ds(block, blocks), pl.ds(16 * row, 16 * rows), cols]

        flights[key] = pltpu.make_async_remote_copy(
            src_ref=view(*source), dst_ref=view(*target), send_sem=ag_send.at[number], recv_sem=ag_recv.at[number],
            device_id=links[link], device_id_type=MESH,
        )
        return (key, link, source[1] * source[3] * size / 32)

    def gather(name, needs, after, shares, cost=0.02, rank=0, before=None):
        sends = [share(*a) for a in shares]

        def run():
            for key in needs:
                flights[key].wait_recv()
            if before is not None:
                before()
            for key, link, kib in sends:
                flights[key].start()
                copies.append(flights[key])

        task(name, needs, after, cost, rank, sends, run)

    ca, cb = COLS_A, 2048 - COLS_A
    ha, hb = ca // 2, cb // 2

    def z_move(key, link, dz, to, row, rows, first, size):
        return (key, link, (POSITION[dz], 1, row, rows), (POSITION[to], 1, row, rows), first, size)

    def x_move(key, link, b, row, to, first, size):
        return (key, link, BLOCKS[b] + (row, 1), BLOCKS[b] + (to, 1), first, size)

    def along_x(b):
        return [x_move(("gx", b, "+"), "x+", b, 0, 3, 0, ca), x_move(("gx", b, "-"), "x-", b, 0, 1, 0, ca)]

    groups = ((0, 1), (1, 3))

    def along_z(g):
        row, rows = groups[g]
        return [z_move(("gz", g, -1), "z+", 0, -1, row, rows, ca, cb),
                z_move(("gz", g, 1), "z-", 0, 1, row, rows, ca, cb),
                z_move(("gz", g, -2), "z++", 0, -2, row, rows, ca, cb),
                z_move(("gz", g, 2), "z--", 0, 2, row, rows, ca, cb)]

    own = [z_move(("ga", -1), "z+", 0, -1, 0, 1, 0, ca), z_move(("ga", 1), "z-", 0, 1, 0, 1, 0, ca),
           x_move(("gb", 3), "x+", 0, 0, 3, ca, cb), x_move(("gb", 1), "x-", 0, 0, 1, ca, cb),
           z_move(("ga", -2), "z++", 0, -2, 0, 1, 0, ca), z_move(("ga", 2), "z--", 0, 2, 0, 1, 0, ca),
           x_move(("gb", 2), "x2", 0, 0, 2, ca, cb)]
    gather("own", [], sums, own + along_x(0) + along_z(0), cost=0.6, before=finish)
    for sign, way, first in ((-1, "+", 0), (1, "-", ha)):
        gather(("ga", 2 * sign), [("ga", 2 * sign)], ["own"],
               [z_move(("ga", 3 * sign), "z" + way, 2 * sign, 3 * sign, 0, 1, 0, ca),
                z_move(("ga", 4 * sign), "z" + way + way, 2 * sign, 4, 0, 1, first, ha)])
        for d in (1, 3, 4):
            gather(("ga", d * sign), [("ga", d * sign)], ["own"], [])
    for b, (block, blocks) in enumerate(BLOCKS[1:], 1):
        held = [("ga", d) for d in DISTANCE[block:block + blocks]]
        gather(("gx", b), [], held + ([("ga", -4)] if ("ga", 4) in held else []), along_x(b), cost=0.0)
    for b in range(len(BLOCKS)):
        held = [("gx", b) if b else "own"]
        gather(("gx", b, "+"), [("gx", b, "+")], held, [x_move(("gy", b, "+"), "x+", b, 3, 2, 0, ha)])
        gather(("gx", b, "-"), [("gx", b, "-")], held, [x_move(("gy", b, "-"), "x-", b, 1, 2, ha, ha)])
        gather(("gy", b), [("gy", b, "+"), ("gy", b, "-")], [("gx", b, "+"), ("gx", b, "-")],
               [(("fa", b), "core", BLOCKS[b] + (0, 4), BLOCKS[b] + (0, 4), 0, ca)], rank=1)
    for g in (1, 2, 3):
        gather(("gb", g), [("gb", g)], ["own"], [])
    gather(("gz", 1), [], [("gb", 1), ("gb", 2), ("gb", 3), ("ga", -2), ("ga", 2)], along_z(1), cost=0.0)
    for g, (row, rows) in enumerate(groups):
        held = [("gz", 1) if g else "own"]
        for sign, way, first in ((-1, "+", ca), (1, "-", ca + hb)):
            gather(("gz", g, 2 * sign), [("gz", g, 2 * sign)], held,
                   [z_move(("gz", g, 3 * sign), "z" + way, 2 * sign, 3 * sign, row, rows, ca, cb),
                    z_move(("gz", g, 4 * sign), "z" + way + way, 2 * sign, 4, row, rows, first, hb)])
            for d in (1, 3, 4):
                gather(("gz", g, d * sign), [("gz", g, d * sign)], held, [])
    near = [("gz", g, d) for g in (0, 1) for d in (1, 2, -1)]
    far = [("gz", g, d) for g in (0, 1) for d in (4, -4, -3, -2, 3)]
    for b, held in enumerate((["own", ("gz", 1)], near, far)):
        region = ((0, 1, 0, 4), (1, 3, 0, 4), (4, 4, 0, 4))[b]
        gather(("fb", b, 0), [], held, [(("fb", b), "core", region, region, ca, cb)], rank=1)

    block_of = lax.shift_right_logical(lax.broadcasted_iota(I32, (1, 576), 1), 6)

    def contracted(half, lo, hi, spans):
        blocks = [4 * half + lax.rem(y + n + 1 + NZ - z, 4) for n in (0, 1, 2, 3)]
        total = None
        for k0, k1 in spans:
            rows = jnp.concatenate([applied[b, :, k0:k1] for b in blocks], axis=0)
            one = lax.dot_general(
                rows, back_v[lo:hi, k0:k1], (((1,), (1,)), ((), ())), preferred_element_type=F32
            )
            total = one if total is None else total + one
        return total

    def product_early(part):
        lo, hi = ((0, 256), (256, 512), (512, 576))[part]
        early[:, lo:hi] = contracted(1, lo, hi, ((ca, 2048), (2048 + ca, 4096)))

    def product(half, part):
        lo, hi = ((0, 256), (256, 512), (512, 576))[part]
        present = jnp.zeros((1, 576), F32)
        for b in range(9):
            present = jnp.where(block_of == b, pattern_s[b].astype(F32), present)
        if half == 0 and part == 0:
            back_load.wait()
        if half == 0:
            out = contracted(0, lo, hi, ((0, 4096),))
        else:
            out = contracted(1, lo, hi, ((0, ca), (2048, 2048 + ca))) + early[:, lo:hi]
        out = out * present[:, lo:hi]
        for n in range(3):
            y_send[half, n, :, lo:hi] = out[64 * n:64 * n + 64].astype(BF16)
        mine[half, :, lo:hi] = out[192:256]

    def y_start(half, part):
        lo, hi = ((0, 512), (512, 576), (0, 256), (256, 576))[part]
        for n in (1, 0, 2):
            number = 3 * part + n
            copy = pltpu.make_async_remote_copy(
                src_ref=y_send.at[half, n, :, pl.ds(lo, hi - lo)], dst_ref=y_recv.at[half, n, :, pl.ds(lo, hi - lo)],
                send_sem=y_ssem.at[number], recv_sem=y_rsem.at[number],
                device_id=y_peers[n], device_id_type=MESH,
            )
            flights[("y", part, n)] = copy
            copy.start()
            copies.append(copy)

    before = []
    for half in (0, 1):
        if half == 1:
            gather(("fb", 2, 1), [("fb", 2)], before + [("fb", 2, 0)], [], rank=3)
            before = [("fb", 2, 1)]
            for part in (0, 1, 2):
                task(("early", part), [], before, 0.3, 3, [], lambda part=part: product_early(part))
                before = [("early", part)]
        for b in range(len(BLOCKS)):
            if BLOCKS[b][0] // 4 == half:
                gather(("fa", b, 1), [("fa", b)], before + [("gy", b)], [], rank=3)
                before = [("fa", b, 1)]
        for b in ((0, 1), ())[half]:
            gather(("fb", b, 1), [("fb", b)], before + [("fb", b, 0)], [], rank=3)
            before = [("fb", b, 1)]
        for part in (0, 1, 2):
            task(("product", half, part), [], before, (0.65, 0.45)[half], 3, [], lambda half=half, part=part: product(half, part))
            before = [("product", half, part)]
            if (half, part) in ((0, 1), (0, 2), (1, 0), (1, 2)):
                number = ((0, 1), (0, 2), (1, 0), (1, 2)).index((half, part))
                task(("y", number), [], before, 0.3, 2, [], lambda half=half, number=number: y_start(half, number))
    assert counter == [POOL, N_MSG] and gathers == [N_GATHER]
    for one in in_order(tasks):
        one[-1]()

    last = [flights[("y", part, n)] for part in (2, 3) for n in range(3)]
    for copy in copies:
        if not any(copy is other for other in last):
            copy.wait_send()
    k = lax.rem(y + NZ - z, 4)
    parity = lax.div(lax.rem(z + k + NZ - 4 * lax.div(k, 3), NZ), 4)
    for half in (0, 1):
        for n in range(3):
            flights[("y", 2 * half, n)].wait_recv()
            flights[("y", 2 * half + 1, n)].wait_recv()
        total = mine[half]
        for n in range(3):
            total = total + y_recv[half, n].astype(F32)
        base = (parity if half == 0 else 1 - parity) * 64
        for j in range(4):
            row = pl.multiple_of(base + lax.rem(x + j, NX) * 16, 16)
            whole[pl.ds(row, 16), :] = total[16 * j:16 * j + 16]
    out_ref[...] = whole[...].T
    for copy in last:
        copy.wait_send()


def per_device(left_tiles, left_row, left_lam, left_count, density, metric, back_tiles, back_pattern):
    vmem = pl.BlockSpec(memory_space=pltpu.VMEM)
    smem = pl.BlockSpec(memory_space=pltpu.SMEM)
    hbm = pl.BlockSpec(memory_space=pl.ANY)
    return pl.pallas_call(
        kernel,
        out_shape=jax.ShapeDtypeStruct((576, 128), F32),
        in_specs=[smem, smem, smem, smem, vmem, vmem, hbm, hbm],
        out_specs=vmem,
        scratch_shapes=[
            pltpu.VMEM((4, 768, 1024), BF16),
            pltpu.VMEM((576, 4096), BF16),
            pltpu.VMEM((576, 768), BF16),
            pltpu.VMEM((512, 768), BF16),
            pltpu.VMEM((8, 16, 16, 128), F32),
            pltpu.VMEM((4, 8, 16, 16, 128), F32),
            pltpu.VMEM((POOL, 16, 128), I16),
            pltpu.VMEM((POOL, 16, 128), I16),
            pltpu.VMEM((8, 64, 4096), BF16),
            pltpu.VMEM((2, 3, 64, 576), BF16),
            pltpu.VMEM((2, 3, 64, 576), BF16),
            pltpu.VMEM((2, 64, 576), F32),
            pltpu.VMEM((128, 576), F32),
            pltpu.VMEM((256, 576), F32),
            pltpu.VMEM((128, 128), F32),
            pltpu.VMEM((16, 16, 128), F32),
            pltpu.SemaphoreType.DMA((N_MSG,)),
            pltpu.SemaphoreType.DMA((N_MSG,)),
            pltpu.SemaphoreType.DMA((N_GATHER,)),
            pltpu.SemaphoreType.DMA((N_GATHER,)),
            pltpu.SemaphoreType.DMA((12,)),
            pltpu.SemaphoreType.DMA((12,)),
            pltpu.SemaphoreType.DMA((5,)),
        ],
        compiler_params=pltpu.CompilerParams(
            collective_id=0, has_side_effects=True, vmem_limit_bytes=56 * 1024 * 1024
        ),
        cost_estimate=pl.CostEstimate(flops=6_000_000_000, bytes_accessed=12_000_000, transcendentals=0),
    )(
        left_row, left_lam, left_count, back_pattern.reshape(9), density.T, metric,
        left_tiles.reshape(768, 4096), back_tiles,
    ).T


def solution(mesh):
    placed = (
        P("pair", None, None),
        P("pair"),
        P("pair"),
        P("pair"),
        P("pair", "col"),
        P(),
        P("pair", "col"),
        P("pair", "col"),
    )
    return jax.shard_map(
        per_device, mesh=mesh, in_specs=placed, out_specs=P("col", "pair"), check_vma=False
    )
```

```python
import jax
import jax.numpy as jnp
from jax import lax
from jax.experimental import pallas as pl
from jax.experimental.pallas import tpu as pltpu
from jax.sharding import PartitionSpec as P

MESH = pl.DeviceIdType.MESH
F32, BF16, I16, I32 = jnp.float32, jnp.bfloat16, jnp.int16, jnp.int32

NZ, NX, NY = 8, 4, 4
SLOTS = 12
Z_ORDER = (4, 3, 5, 2, 6, 1, 7, 0)
X_ORDER = (2, 1, 3, 0)
TOP = 32000.0
ROUND = 12582912.0
PART_A = 14
COLS_A = 1280
ROWS_A = ((0, 3), (3, 7), (7, 8))
POSITION = {0: 0, 1: 1, 2: 2, -1: 3, 4: 4, -4: 4, -3: 5, -2: 6, 3: 7}
BLOCKS = ((0, 1), (1, 3), (6, 1), (4, 2), (7, 1))
DISTANCE = (0, 1, 2, -1, 4, -3, -2, 3)
POOL = 1043
N_MSG = 35
N_GATHER = 55


def in_order(tasks):
    now, free, arrival, done, order, left = 0.0, {}, {}, set(), [], list(tasks)
    while left:
        best = None
        for task in left:
            name, needs, after, cost, rank, sends, run = task
            if all(n in arrival for n in needs) and all(t in done for t in after):
                ready = max([arrival[n] for n in needs] + [now])
                if best is None or (ready, rank) < best[:2]:
                    best = (ready, rank, task)
        ready, rank, task = best
        now = ready + task[3] + 0.08 * len(task[1])
        for key, link, hops, kib in task[5]:
            now += 0.08
            if link == "core":
                arrival[key] = now + 1.0 + kib * 0.001
                continue
            each = kib * 2 * 1.024 / 115.0
            start = max(free.get(link, 0.0), now)
            free[link] = start + each * hops
            arrival[key] = start + each + 2.3 + 0.4 * (hops - 1)
        order.append(task)
        done.add(task[0])
        left.remove(task)
    return order


def kernel(
    row_s, lam_s, count_s, pattern_s, density, metric, left_hbm, back_hbm, out_ref,
    left_v, back_v, pick, amat, stage, acc, pool_s, pool_r, applied, y_send, y_recv, mine, whole,
    metric2, turn, msg_send, msg_recv, ag_send, ag_recv, y_ssem, y_rsem, local_sem,
):
    pair = lax.axis_index("pair")
    y = lax.axis_index("col")
    core = lax.rem(pair, 2)
    x = lax.rem(lax.div(pair, 2), NX)
    z = lax.div(pair, 2 * NX)

    def at(zz, xx, cc):
        return {"pair": (lax.rem(zz, NZ) * NX + lax.rem(xx, NX)) * 2 + cc}

    peer = at(z, x, 1 - core)
    x_right, x_left = at(z, x + 1, core), at(z, x + NX - 1, core)
    z_right, z_left = at(z + 1, x, core), at(z + NZ - 1, x, core)
    y_peers = [{"col": lax.rem(y + dy, NY)} for dy in (1, 2, 3)]

    barrier = pltpu.get_barrier_semaphore()
    far_peers = [at(z, x + 2, core), at(z + 2, x, core), at(z + NZ - 2, x, core)]
    for other in [peer, x_right, x_left, z_right, z_left] + far_peers + y_peers:
        pl.semaphore_signal(barrier, inc=1, device_id=other, device_id_type=MESH)

    loads = []
    for i, off in enumerate(X_ORDER):
        first = pl.multiple_of(lax.rem(x + off, NX) * 1024, 1024)
        load = pltpu.make_async_copy(left_hbm.at[:, pl.ds(first, 1024)], left_v.at[i], local_sem.at[i])
        load.start()
        loads.append(load)
    back_load = pltpu.make_async_copy(back_hbm, back_v, local_sem.at[4])

    j = lax.broadcasted_iota(I32, (64, 64), 0)
    half_core = jnp.where(j < 32, 1 - core, core)
    sigma = half_core * 32 + 2 * (j & 15) + ((j >> 4) & 1)
    perm = jnp.where(lax.broadcasted_iota(I32, (64, 64), 1) == sigma, 1.0, 0.0).astype(BF16)
    sorted_density = jnp.dot(perm, density[...], preferred_element_type=F32).astype(BF16)
    lane = lax.broadcasted_iota(I32, (16, SLOTS * 64), 1)
    slot_of = lane >> 6
    lam_of = jnp.zeros((16, SLOTS * 64), I32)
    row_of = jnp.zeros((16, SLOTS * 64), I32)
    for s in range(SLOTS):
        lam_of = jnp.where(slot_of == s, lam_s[s], lam_of)
        row_of = jnp.where(slot_of == s, row_s[s], row_of)
    live = slot_of < count_s[0]
    source = row_of * 64 + (lane & 63)
    deep = lax.broadcasted_iota(I32, (16, SLOTS * 64), 0)
    for b in range(36):
        pick[b * 16:(b + 1) * 16, :] = jnp.where(source == deep + b * 16, 1.0, 0.0).astype(BF16)
    turned = jnp.dot(sorted_density, pick[...], preferred_element_type=F32)
    for r, off in enumerate(Z_ORDER):
        owner = lax.rem(z + off, NZ)
        here = live & (lam_of == 2 * lax.rem(owner, 4) + lax.div(owner, 4))
        for q in range(4):
            first = (q * 8 + r) * 16
            amat[first:first + 16, :] = jnp.where(here, turned[q * 16:(q + 1) * 16, :], 0.0).astype(BF16)

    metric2[...] = jnp.zeros((128, 128), F32)
    metric2[0:64, 0:64] = metric[...]
    metric2[64:128, 64:128] = metric[...]

    links = {
        "core": peer, "x+": x_right, "x-": x_left, "x2": at(z, x + 2, core),
        "z+": z_right, "z-": z_left, "z++": at(z + 2, x, core), "z--": at(z + NZ - 2, x, core),
    }
    lanes = {"x2": ("x+", 2), "z++": ("z+", 2), "z--": ("z-", 2)}
    copies, flights, tasks = [], {}, []
    counter, gathers = [0, 0], [0]

    def task(name, needs, after, cost, rank, sends, run):
        tasks.append((name, needs, after, cost, rank, [(k,) + lanes.get(l, (l, 1)) + (n,) for k, l, n in sends], run))

    def message(key, tiles, link):
        off, number = counter
        counter[0] += tiles + 1
        counter[1] += 1
        copy = pltpu.make_async_remote_copy(
            src_ref=pool_s.at[pl.ds(off, tiles + 1)], dst_ref=pool_r.at[pl.ds(off, tiles + 1)],
            send_sem=msg_send.at[number], recv_sem=msg_recv.at[number],
            device_id=links[link], device_id_type=MESH,
        )
        flights[key] = (copy, off, tiles)
        return (key, link, 4 * (tiles + 1))

    def send(get, groups, size, key, top=None):
        copy, off, tiles = flights[key]
        assert tiles == groups * size

        def largest(g, m):
            return jnp.maximum(m, jnp.max(jnp.abs(get(g)[...]), axis=0))

        def code(g, carry):
            value = (get(g)[...] * scale + ROUND) - ROUND
            pool_s[pl.ds(off + g * size, size)] = value.astype(I16)
            return carry

        if top is None:
            top = jnp.zeros((16, 128), F32)
            top = largest(0, top) if groups == 1 else lax.fori_loop(0, groups, largest, top)
        power = jnp.ceil(jnp.log2(jnp.maximum(top, 1e-30)))
        scale = jnp.exp2(-power) * TOP
        pool_s[off + tiles] = power.astype(I16)
        if groups == 1:
            code(0, 0)
        else:
            lax.fori_loop(0, groups, code, 0)
        copy.start()
        copies.append(copy)

    def receive(get, groups, size, key):
        copy, off, tiles = flights[key]
        assert tiles == groups * size
        copy.wait_recv()
        scale = jnp.exp2(pool_r[off + tiles].astype(F32)) * (1.0 / TOP)

        def add(g, carry):
            ref = get(g)
            ref[...] = ref[...] + pool_r[pl.ds(off + g * size, size)].astype(F32) * scale
            return carry

        if groups == 1:
            add(0, 0)
        else:
            lax.fori_loop(0, groups, add, 0)

    def rows_at(slot, row, first, size):
        return lambda g: acc.at[slot, row + g, pl.ds(first, size)]

    def left_step(i):
        loads[i].wait()

        def columns(jc, top):
            tile = left_v[i, :, pl.ds(pl.multiple_of(jc * 512, 512), 512)]
            part = jnp.dot(amat[...], tile, preferred_element_type=F32)
            for u in range(4):
                value = part[:, u * 128:(u + 1) * 128].reshape(32, 16, 128)
                stage[:, 4 * jc + u] = value[0:8]
                stage[:, 8 + 4 * jc + u] = value[8:16]
                acc[i, :, 4 * jc + u] = value[16:24]
                acc[i, :, 8 + 4 * jc + u] = value[24:32]
                top = jnp.maximum(top, jnp.max(jnp.abs(value[0:16]), axis=0))
            return top

        top = lax.fori_loop(0, 2, columns, jnp.zeros((16, 128), F32))
        if i == 0:
            pl.semaphore_wait(barrier, 11)
        if i == 1:
            back_load.start()
        send(lambda g: stage.at[g], 8, 16, ("core", i), top)

    for i in range(4):
        task(("left", i), [], [("left", i - 1)] if i else [], 1.4, 2,
             [message(("core", i), 128, "core")], lambda i=i: left_step(i))
        task(("sum", i), [("core", i)], [("left", i)], 0.25, 1, [],
             lambda i=i: receive(rows_at(i, 0, 0, 16), 8, 16, ("core", i)))

    na, half_a = PART_A, PART_A // 2
    for m, (first, last) in enumerate(ROWS_A):
        count = last - first

        def x_start(first=first, count=count, m=m):
            send(rows_at(0, first, 0, half_a), count, half_a, ("A", m, 0, "+"))
            send(rows_at(0, first, half_a, half_a), count, half_a, ("A", m, 0, "-"))

        def x_next(sign, first=first, count=count, m=m):
            slot, tile = (1, 0) if sign == "+" else (2, half_a)
            receive(rows_at(slot, first, tile, half_a), count, half_a, ("A", m, 0, sign))
            send(rows_at(slot, first, 0, na), count, na, ("A", m, 1, sign))

        def x_end(first=first, last=last, count=count, m=m):
            receive(rows_at(3, first, 0, na), count, na, ("A", m, 1, "+"))
            receive(rows_at(3, first, 0, na), count, na, ("A", m, 1, "-"))
            if first <= 2 < last:
                send(rows_at(3, 0, 0, half_a), 1, half_a, ("Z", 4))
                send(rows_at(3, 0, half_a, half_a), 1, half_a, ("Z", -4))
                send(rows_at(3, 1, 0, na), 1, na, ("Z", 3))
                send(rows_at(3, 2, 0, na), 1, na, ("Z", -3))
            if first <= 6 < last:
                send(rows_at(3, 5, 0, na), 1, na, ("Z", 1))
                send(rows_at(3, 6, 0, na), 1, na, ("Z", -1))

        task(("A", m, 0), [], [("sum", 0)], 0.2, 0,
             [message(("A", m, 0, "+"), half_a * count, "x+"), message(("A", m, 0, "-"), half_a * count, "x-")], x_start)
        for sign, before in (("+", 1), ("-", 2)):
            task(("A", m, 1, sign), [("A", m, 0, sign)], [("sum", before)], 0.3, 0,
                 [message(("A", m, 1, sign), na * count, "x" + sign)], lambda f=x_next, sign=sign: f(sign))
        sends = []
        if first <= 2 < last:
            sends = [message(("Z", 4), half_a, "z++"), message(("Z", -4), half_a, "z--"),
                     message(("Z", 3), na, "z+"), message(("Z", -3), na, "z-")]
        if first <= 6 < last:
            sends = sends + [message(("Z", 1), na, "z+"), message(("Z", -1), na, "z-")]
        task(("A", m, 2), [("A", m, 1, "+"), ("A", m, 1, "-")], [("sum", 3)], 0.3, 0, sends, x_end)

    relay_run = [m for m, (first, last) in enumerate(ROWS_A) if first <= 4 < last][0]
    end = len(ROWS_A) - 1

    def z_relay(sign):
        row = 3 if sign > 0 else 4
        receive(rows_at(3, row, 0, na), 1, na, ("Z", 3 * sign))
        receive(rows_at(3, row, 0 if sign > 0 else half_a, half_a), 1, half_a, ("Z", 4 * sign))
        send(rows_at(3, row, 0, na), 1, na, ("Z", 2 * sign))

    for sign in (1, -1):
        task(("Z", 2 * sign, 0), [("Z", 3 * sign), ("Z", 4 * sign)], [("A", relay_run, 2)], 0.2, 0,
             [message(("Z", 2 * sign), na, "z++" if sign > 0 else "z--")], lambda sign=sign: z_relay(sign))
    for d in (1, -1, 2, -2):
        task(("Z", d, 1), [("Z", d)], [("A", end, 2)], 0.1, 1, [],
             lambda d=d: receive(rows_at(3, 7, 0, na), 1, na, ("Z", d)))

    nb, half_b = 16 - na, (16 - na) // 2

    def parts(row, first, size):
        return lambda g: acc.at[g, row, pl.ds(na + first, size)]

    def b_start():
        for row, d in ((1, 3), (2, -3)):
            send(parts(row, 0, nb), 4, nb, ("B", d))
        send(parts(0, 0, half_b), 4, half_b, ("B", 4))
        send(parts(0, half_b, half_b), 4, half_b, ("B", -4))
        for row, d in ((5, 1), (6, -1)):
            send(parts(row, 0, nb), 4, nb, ("B", d))

    def b_relay(sign):
        row = 3 if sign > 0 else 4
        receive(parts(row, 0, nb), 4, nb, ("B", 3 * sign))
        receive(parts(row, 0 if sign > 0 else half_b, half_b), 4, half_b, ("B", 4 * sign))
        send(parts(row, 0, nb), 4, nb, ("B", 2 * sign))

    def b_cross():
        for i in range(3):
            send(rows_at(i, 7, na, nb), 1, nb, ("X", i))

    sends = [message(("B", d), 4 * n, link) for d, n, link in (
        (3, nb, "z+"), (-3, nb, "z-"), (4, half_b, "z++"), (-4, half_b, "z--"), (1, nb, "z+"), (-1, nb, "z-"))]
    task(("B", 0), [], [("sum", i) for i in range(4)], 0.6, 0, sends, b_start)
    for sign in (1, -1):
        task(("B", 2 * sign, 0), [("B", 3 * sign), ("B", 4 * sign)], [("B", 0)], 0.2, 0,
             [message(("B", 2 * sign), 4 * nb, "z++" if sign > 0 else "z--")], lambda sign=sign: b_relay(sign))
    for d in (1, -1, 2, -2):
        task(("B", d, 1), [("B", d)], [("B", 0)], 0.1, 1, [],
             lambda d=d: receive(parts(7, 0, nb), 4, nb, ("B", d)))
    ends = [("B", d, 1) for d in (1, -1, 2, -2)]
    task(("X", 0), [], ends, 0.2, 0,
         [message(("X", i), nb, link) for i, link in enumerate(("x2", "x+", "x-"))], b_cross)
    for i in range(3):
        task(("X", i, 1), [("X", i)], ends, 0.1, 1, [],
             lambda i=i: receive(rows_at(3, 7, na, nb), 1, nb, ("X", i)))
    sums = [t[0] for t in tasks]

    core_first = core * 2048

    def finish():
        rows = acc[3, 7].reshape(256, 128)
        both = jnp.dot(rows, metric2[...], precision=lax.Precision.HIGHEST, preferred_element_type=F32)
        low = lax.broadcasted_iota(I32, (16, 128), 1) < 64
        for t in range(8):
            e, o = both[t * 16:(t + 1) * 16], both[128 + t * 16:144 + t * 16]
            turn[2 * t] = jnp.where(low, e, pltpu.roll(o, 64, 1))
            turn[2 * t + 1] = jnp.where(low, pltpu.roll(e, 64, 1), o)
        for sp in range(16):
            cols = pl.ds(pl.multiple_of(core_first + sp * 128, 128), 128)
            applied[0, 0:16, cols] = turn[:, sp, :].astype(BF16)

    def share(key, link, source, target, first, size):
        number = gathers[0]
        gathers[0] += 1
        cols = pl.ds(pl.multiple_of(core_first + first, 128), size)

        def view(block, blocks, row, rows):
            return applied.at[pl.ds(block, blocks), pl.ds(16 * row, 16 * rows), cols]

        flights[key] = pltpu.make_async_remote_copy(
            src_ref=view(*source), dst_ref=view(*target), send_sem=ag_send.at[number], recv_sem=ag_recv.at[number],
            device_id=links[link], device_id_type=MESH,
        )
        return (key, link, source[1] * source[3] * size / 32)

    def gather(name, needs, after, shares, cost=0.02, rank=0, before=None):
        sends = [share(*a) for a in shares]

        def run():
            for key in needs:
                flights[key].wait_recv()
            if before is not None:
                before()
            for key, link, kib in sends:
                flights[key].start()
                copies.append(flights[key])

        task(name, needs, after, cost, rank, sends, run)

    ca, cb = COLS_A, 2048 - COLS_A
    ha, hb = ca // 2, cb // 2

    def z_move(key, link, dz, to, row, rows, first, size):
        return (key, link, (POSITION[dz], 1, row, rows), (POSITION[to], 1, row, rows), first, size)

    def x_move(key, link, b, row, to, first, size):
        return (key, link, BLOCKS[b] + (row, 1), BLOCKS[b] + (to, 1), first, size)

    def along_x(b):
        return [x_move(("gx", b, "+"), "x+", b, 0, 3, 0, ca), x_move(("gx", b, "-"), "x-", b, 0, 1, 0, ca)]

    groups = ((0, 1), (1, 3))

    def along_z(g):
        row, rows = groups[g]
        return [z_move(("gz", g, -1), "z+", 0, -1, row, rows, ca, cb),
                z_move(("gz", g, 1), "z-", 0, 1, row, rows, ca, cb),
                z_move(("gz", g, -2), "z++", 0, -2, row, rows, ca, cb),
                z_move(("gz", g, 2), "z--", 0, 2, row, rows, ca, cb)]

    own = [z_move(("ga", -1), "z+", 0, -1, 0, 1, 0, ca), z_move(("ga", 1), "z-", 0, 1, 0, 1, 0, ca),
           x_move(("gb", 3), "x+", 0, 0, 3, ca, cb), x_move(("gb", 1), "x-", 0, 0, 1, ca, cb),
           z_move(("ga", -2), "z++", 0, -2, 0, 1, 0, ca), z_move(("ga", 2), "z--", 0, 2, 0, 1, 0, ca),
           x_move(("gb", 2), "x2", 0, 0, 2, ca, cb)]
    gather("own", [], sums, own + along_x(0) + along_z(0), cost=0.6, before=finish)
    for sign, way, first in ((-1, "+", 0), (1, "-", ha)):
        gather(("ga", 2 * sign), [("ga", 2 * sign)], ["own"],
               [z_move(("ga", 3 * sign), "z" + way, 2 * sign, 3 * sign, 0, 1, 0, ca),
                z_move(("ga", 4 * sign), "z" + way + way, 2 * sign, 4, 0, 1, first, ha)])
        for d in (1, 3, 4):
            gather(("ga", d * sign), [("ga", d * sign)], ["own"], [])
    for b, (block, blocks) in enumerate(BLOCKS[1:], 1):
        held = [("ga", d) for d in DISTANCE[block:block + blocks]]
        gather(("gx", b), [], held + ([("ga", -4)] if ("ga", 4) in held else []), along_x(b), cost=0.0)
    for b in range(len(BLOCKS)):
        held = [("gx", b) if b else "own"]
        gather(("gx", b, "+"), [("gx", b, "+")], held, [x_move(("gy", b, "+"), "x+", b, 3, 2, 0, ha)])
        gather(("gx", b, "-"), [("gx", b, "-")], held, [x_move(("gy", b, "-"), "x-", b, 1, 2, ha, ha)])
        gather(("gy", b), [("gy", b, "+"), ("gy", b, "-")], [("gx", b, "+"), ("gx", b, "-")],
               [(("fa", b), "core", BLOCKS[b] + (0, 4), BLOCKS[b] + (0, 4), 0, ca)], rank=1)
    for g in (1, 2, 3):
        gather(("gb", g), [("gb", g)], ["own"], [])
    gather(("gz", 1), [], [("gb", 1), ("gb", 2), ("gb", 3), ("ga", -2), ("ga", 2)], along_z(1), cost=0.0)
    for g, (row, rows) in enumerate(groups):
        held = [("gz", 1) if g else "own"]
        for sign, way, first in ((-1, "+", ca), (1, "-", ca + hb)):
            gather(("gz", g, 2 * sign), [("gz", g, 2 * sign)], held,
                   [z_move(("gz", g, 3 * sign), "z" + way, 2 * sign, 3 * sign, row, rows, ca, cb),
                    z_move(("gz", g, 4 * sign), "z" + way + way, 2 * sign, 4, row, rows, first, hb)])
            for d in (1, 3, 4):
                gather(("gz", g, d * sign), [("gz", g, d * sign)], held, [])
    near = [("gz", g, d) for g in (0, 1) for d in (1, 2, -1)]
    far = [("gz", g, d) for g in (0, 1) for d in (4, -4, -3, -2, 3)]
    for b, held in enumerate((["own", ("gz", 1)], near, far)):
        region = ((0, 1, 0, 4), (1, 3, 0, 4), (4, 4, 0, 4))[b]
        gather(("fb", b, 0), [], held, [(("fb", b), "core", region, region, ca, cb)], rank=1)

    block_of = lax.shift_right_logical(lax.broadcasted_iota(I32, (1, 576), 1), 6)

    def product(half, part):
        lo, hi = ((0, 256), (256, 512), (512, 576))[part]
        present = jnp.zeros((1, 576), F32)
        for b in range(9):
            present = jnp.where(block_of == b, pattern_s[b].astype(F32), present)
        if half == 0 and part == 0:
            back_load.wait()
        blocks = [4 * half + lax.rem(y + n + 1 + NZ - z, 4) for n in (0, 1, 2, 3)]
        rows = jnp.concatenate([applied[b] for b in blocks], axis=0)
        out = lax.dot_general(rows, back_v[lo:hi, :], (((1,), (1,)), ((), ())), preferred_element_type=F32)
        out = out * present[:, lo:hi]
        for n in range(3):
            y_send[half, n, :, lo:hi] = out[64 * n:64 * n + 64].astype(BF16)
        mine[half, :, lo:hi] = out[192:256]

    def y_start(half, part):
        lo, hi = ((0, 512), (512, 576), (0, 256), (256, 576))[part]
        for n in (1, 0, 2):
            number = 3 * part + n
            copy = pltpu.make_async_remote_copy(
                src_ref=y_send.at[half, n, :, pl.ds(lo, hi - lo)], dst_ref=y_recv.at[half, n, :, pl.ds(lo, hi - lo)],
                send_sem=y_ssem.at[number], recv_sem=y_rsem.at[number],
                device_id=y_peers[n], device_id_type=MESH,
            )
            flights[("y", part, n)] = copy
            copy.start()
            copies.append(copy)

    before = []
    for half in (0, 1):
        for b in range(len(BLOCKS)):
            if BLOCKS[b][0] // 4 == half:
                gather(("fa", b, 1), [("fa", b)], before + [("gy", b)], [], rank=3)
                before = [("fa", b, 1)]
        for b in ((0, 1), (2,))[half]:
            gather(("fb", b, 1), [("fb", b)], before + [("fb", b, 0)], [], rank=3)
            before = [("fb", b, 1)]
        for part in (0, 1, 2):
            task(("product", half, part), [], before, 0.65, 3, [], lambda half=half, part=part: product(half, part))
            before = [("product", half, part)]
            if (half, part) in ((0, 1), (0, 2), (1, 0), (1, 2)):
                number = ((0, 1), (0, 2), (1, 0), (1, 2)).index((half, part))
                task(("y", number), [], before, 0.3, 2, [], lambda half=half, number=number: y_start(half, number))
    assert counter == [POOL, N_MSG] and gathers == [N_GATHER]
    for one in in_order(tasks):
        one[-1]()

    last = [flights[("y", part, n)] for part in (2, 3) for n in range(3)]
    for copy in copies:
        if not any(copy is other for other in last):
            copy.wait_send()
    k = lax.rem(y + NZ - z, 4)
    parity = lax.div(lax.rem(z + k + NZ - 4 * lax.div(k, 3), NZ), 4)
    for half in (0, 1):
        for n in range(3):
            flights[("y", 2 * half, n)].wait_recv()
            flights[("y", 2 * half + 1, n)].wait_recv()
        total = mine[half]
        for n in range(3):
            total = total + y_recv[half, n].astype(F32)
        base = (parity if half == 0 else 1 - parity) * 64
        for j in range(4):
            row = pl.multiple_of(base + lax.rem(x + j, NX) * 16, 16)
            whole[pl.ds(row, 16), :] = total[16 * j:16 * j + 16]
    out_ref[...] = whole[...].T
    for copy in last:
        copy.wait_send()


def per_device(left_tiles, left_row, left_lam, left_count, density, metric, back_tiles, back_pattern):
    vmem = pl.BlockSpec(memory_space=pltpu.VMEM)
    smem = pl.BlockSpec(memory_space=pltpu.SMEM)
    hbm = pl.BlockSpec(memory_space=pl.ANY)
    return pl.pallas_call(
        kernel,
        out_shape=jax.ShapeDtypeStruct((576, 128), F32),
        in_specs=[smem, smem, smem, smem, vmem, vmem, hbm, hbm],
        out_specs=vmem,
        scratch_shapes=[
            pltpu.VMEM((4, 768, 1024), BF16),
            pltpu.VMEM((576, 4096), BF16),
            pltpu.VMEM((576, 768), BF16),
            pltpu.VMEM((512, 768), BF16),
            pltpu.VMEM((8, 16, 16, 128), F32),
            pltpu.VMEM((4, 8, 16, 16, 128), F32),
            pltpu.VMEM((POOL, 16, 128), I16),
            pltpu.VMEM((POOL, 16, 128), I16),
            pltpu.VMEM((8, 64, 4096), BF16),
            pltpu.VMEM((2, 3, 64, 576), BF16),
            pltpu.VMEM((2, 3, 64, 576), BF16),
            pltpu.VMEM((2, 64, 576), F32),
            pltpu.VMEM((128, 576), F32),
            pltpu.VMEM((128, 128), F32),
            pltpu.VMEM((16, 16, 128), F32),
            pltpu.SemaphoreType.DMA((N_MSG,)),
            pltpu.SemaphoreType.DMA((N_MSG,)),
            pltpu.SemaphoreType.DMA((N_GATHER,)),
            pltpu.SemaphoreType.DMA((N_GATHER,)),
            pltpu.SemaphoreType.DMA((12,)),
            pltpu.SemaphoreType.DMA((12,)),
            pltpu.SemaphoreType.DMA((5,)),
        ],
        compiler_params=pltpu.CompilerParams(
            collective_id=0, has_side_effects=True, vmem_limit_bytes=56 * 1024 * 1024
        ),
        cost_estimate=pl.CostEstimate(flops=6_000_000_000, bytes_accessed=12_000_000, transcendentals=0),
    )(
        left_row, left_lam, left_count, back_pattern.reshape(9), density.T, metric,
        left_tiles.reshape(768, 4096), back_tiles,
    ).T


def solution(mesh):
    placed = (
        P("pair", None, None),
        P("pair"),
        P("pair"),
        P("pair"),
        P("pair", "col"),
        P(),
        P("pair", "col"),
        P("pair", "col"),
    )
    return jax.shard_map(
        per_device, mesh=mesh, in_specs=placed, out_specs=P("col", "pair"), check_vma=False
    )
```
